32 devices in a mesh: dp: 2 (over y), mp: 16 (over z, x, core).
Axes of the slice: x: 2, y: 2, z: 4, core: 2. Of those that a mesh axis runs over, the one named last changes fastest.
Arguments:
- tokens: bfloat16 [4096, 2, 768], P('mp', 'dp'), may hold values from -6 to 6
- cotangent: bfloat16 [4096, 2, 768], P('mp', 'dp'), may hold values from -6 to 6
- weight_in: float32 [2, 768, 3072], P(None, None, 'mp'), may hold values from -0.21650635 to 0.21650635
- bias_in: float32 [2, 3072], P(None, 'mp'), may hold values from -1.2 to 1.2
- weight_out: float32 [2, 3072, 768], P(None, 'mp'), may hold values from -0.108253175 to 0.108253175
- vectors: float32 [2, 5, 768], replicated, may hold values from -1 to 2
- moment_in: float32 [2, 768, 3072], P(None, None, 'mp'), may hold values from -0.0029296875 to 0.0029296875
- square_in: float32 [2, 768, 3072], P(None, None, 'mp'), may hold values from 2.5431316e-08 to 1.695421e-07
- moment_bias: float32 [2, 3072], P(None, 'mp'), may hold values from -0.0029296875 to 0.0029296875
- square_bias: float32 [2, 3072], P(None, 'mp'), may hold values from 2.5431316e-08 to 1.695421e-07
- moment_out: float32 [2, 3072, 768], P(None, 'mp'), may hold values from -0.005859375 to 0.005859375
- square_out: float32 [2, 3072, 768], P(None, 'mp'), may hold values from 1.05963814e-07 to 6.781684e-07
- moment_vec: float32 [2, 5, 768], replicated, may hold values from -0.009765625 to 0.009765625
- square_vec: float32 [2, 5, 768], replicated, may hold values from 2.966987e-07 to 1.695421e-06
Outputs:
- activations: bfloat16 [4096, 2, 768], P('mp', 'dp')
- input_grad: float32 [4096, 2, 768], P('mp', 'dp')
- grad_norm: float32 [], replicated
- new_moment_in: float32 [2, 768, 3072], P(None, None, 'mp')
- new_square_in: float32 [2, 768, 3072], P(None, None, 'mp')
- new_weight_in: float32 [2, 768, 3072], P(None, None, 'mp')
- copy_in: bfloat16 [2, 768, 3072], P(None, None, 'mp')
- new_moment_out: float32 [2, 3072, 768], P(None, 'mp')
- new_square_out: float32 [2, 3072, 768], P(None, 'mp')
- new_weight_out: float32 [2, 3072, 768], P(None, 'mp')
- copy_out: bfloat16 [2, 3072, 768], P(None, 'mp')
- new_moment_bias: float32 [2, 3072], P(None, 'mp')
- new_square_bias: float32 [2, 3072], P(None, 'mp')
- new_bias_in: float32 [2, 3072], P(None, 'mp')
- new_moment_vec: float32 [2, 5, 768], replicated
- new_square_vec: float32 [2, 5, 768], replicated
- new_vectors: float32 [2, 5, 768], replicated
The draws below stay inside these ranges and needn't reach their ends.
All inputs are finite; a program needn't handle non-finite values.
Results may differ from the reference program's by a relative error of at most 0.018.
Values may be sent and summed in bfloat16 or wider, within the bound.
A program may use at most 192 MiB of HBM per device.

```python
import math
import jax
import jax.numpy as jnp
from jax import lax

D = 768
FF = 3072
L = 4096
LAYERS = 2
STEP = 5
SEQS = 2


def ramp_values(count, start_value):
    fraction = jnp.arange(count, dtype=jnp.float32) / (count - 1)
    return start_value + fraction


def draw_weight_in(key, part):
    key = jax.random.fold_in(key, 11)
    base = jax.random.truncated_normal(key, -4.0, 4.0, (LAYERS, D, FF), jnp.float32)
    ramp = ramp_values(FF, 0.5)
    return base * ramp[None, None, :] * D ** (-0.5)


def draw_weight_out(key, part):
    key = jax.random.fold_in(key, 12)
    base = jax.random.truncated_normal(key, -4.0, 4.0, (LAYERS, FF, D), jnp.float32)
    ramp = ramp_values(FF, 0.5)
    return base * ramp[None, :, None] * FF ** (-0.5)


def draw_vectors(key, part):
    key = jax.random.fold_in(key, 13)
    key_gain, key_shift = jax.random.split(key)
    shape = (LAYERS, 5, D)
    ramp = ramp_values(D, 0.5)
    shifts = 0.3 * jax.random.truncated_normal(key_shift, -3.0, 3.0, shape, jnp.float32)
    gains = ramp[None, None, :] * (1.0 + 0.15 * jax.random.uniform(key_gain, shape, jnp.float32, -1.0, 1.0))
    kinds = jnp.arange(5, dtype=jnp.int32)[None, :, None]
    is_gain = (kinds == 0) | (kinds == 3)
    return jnp.where(is_gain, gains, shifts)


def steps_of(rng, shape, shards, low, top_value):
    level = 1.0
    for axis_at, shards_of in shards:
        draws = jax.random.uniform(jax.random.fold_in(jax.random.fold_in(rng, 6), axis_at), (shards_of,), jnp.float32, low / len(shards), top_value / len(shards))
        level = level * jnp.repeat(jnp.exp(draws), shape[axis_at] // shards_of).reshape((-1,) + (1,) * (len(shape) - 1 - axis_at))
    return level


def gaussian(key, shape, width, reach, pieces=(), kind=jnp.bfloat16):
    array = width * jax.random.normal(key, shape, jnp.float32)
    if pieces:
        array = array * steps_of(key, shape, pieces, -0.22, 0.18)
    return jnp.clip(array, -reach, reach).astype(kind)


def setup_inputs(seed: int = 0) -> dict:
    splits = jax.random.split(jax.random.key(seed), 15)
    tokens = gaussian(splits[0], (L, SEQS, D), 1.0, 6.0, ((0, 16), (1, 2)))
    cotangent = gaussian(splits[1], (L, SEQS, D), 1.0, 6.0, ((0, 16), (1, 2)))
    weight_in = draw_weight_in(jax.random.fold_in(splits[14], 71), 0)
    bias_in = gaussian(splits[3], (LAYERS, FF), 0.3, 1.2, ((1, 16),), jnp.float32)
    weight_out = draw_weight_out(jax.random.fold_in(splits[14], 71), 0)
    vectors = draw_vectors(jax.random.fold_in(splits[14], 71), 0)
    moment_in = gaussian(splits[6], (LAYERS, D, FF), (0.3 / (D * FF) ** 0.5), 0.0029296875, ((2, 16),), jnp.float32)
    square_in = jnp.clip(jnp.exp(math.log(1.6954210479980247e-07) - 1.89712 * jax.random.uniform(splits[7], (LAYERS, D, FF), jnp.float32) ** steps_of(splits[7], (LAYERS, D, FF), ((2, 16),), -0.2, 0.2)), 2.543131571997037e-08, 1.6954210479980247e-07)
    moment_bias = gaussian(splits[8], (LAYERS, FF), (0.3 / (D * FF) ** 0.5), 0.0029296875, ((1, 16),), jnp.float32)
    square_bias = jnp.clip(jnp.exp(math.log(1.6954210479980247e-07) - 1.89712 * jax.random.uniform(splits[9], (LAYERS, FF), jnp.float32) ** steps_of(splits[9], (LAYERS, FF), ((1, 16),), -0.2, 0.2)), 2.543131571997037e-08, 1.6954210479980247e-07)
    moment_out = gaussian(splits[10], (LAYERS, FF, D), (0.6 / (D * FF) ** 0.5), 0.005859375, ((1, 16),), jnp.float32)
    square_out = jnp.clip(jnp.exp(math.log(6.781684191992099e-07) - 1.856298 * jax.random.uniform(splits[11], (LAYERS, FF, D), jnp.float32) ** steps_of(splits[11], (LAYERS, FF, D), ((1, 16),), -0.2, 0.2)), 1.059638137235197e-07, 6.781684191992099e-07)
    moment_vec = gaussian(splits[12], (LAYERS, 5, D), (1.0 / (D * FF) ** 0.5), 0.009765625, (), jnp.float32)
    square_vec = jnp.clip(jnp.exp(jax.random.uniform(splits[13], (LAYERS, 5, D), jnp.float32, math.log(2.96698686952368e-07), math.log(1.6954210195763153e-06))), 2.96698686952368e-07, 1.6954210195763153e-06)
    return dict(tokens=tokens, cotangent=cotangent, weight_in=weight_in, bias_in=bias_in, weight_out=weight_out, vectors=vectors, moment_in=moment_in, square_in=square_in, moment_bias=moment_bias, square_bias=square_bias, moment_out=moment_out, square_out=square_out, moment_vec=moment_vec, square_vec=square_vec)


CLIP = 1.0
BETA_ONE = 0.5
BETA_TWO = 0.5
EPS_ADAM = 1e-08
EPS_NORM = 1e-05
DECAY = 0.01

@jax.custom_vjp
def low(v):
    return lax.optimization_barrier(v.astype(jnp.bfloat16)).astype(jnp.float32)

@jax.custom_vjp
def low_back(v):
    return v

def low_keep(v):
    return (low(v), None)

def low_pass(kept, grad):
    return (grad,)

def back_keep(v):
    return (v, None)

def back_low(kept, grad):
    return (low(grad),)
low.defvjp(low_keep, low_pass)
low_back.defvjp(back_keep, back_low)

def tables(count):
    ids = jnp.arange(count, dtype=jnp.int32)
    product = ids[:, None] * ids[None, :] % count
    angle_grid = product.astype(jnp.float32) * (2.0 * math.pi / count)
    return (low(jnp.cos(angle_grid)), low(jnp.sin(angle_grid)))

def matmul(left_op, right_op):
    return jnp.dot(left_op, right_op, precision=lax.Precision.HIGHEST, preferred_element_type=jnp.float32)

def layer_norm(value, gain, shift):
    centre = value - lax.optimization_barrier(jnp.mean(value, axis=-1, keepdims=True))
    spread = lax.optimization_barrier(jnp.mean(centre * centre, axis=-1, keepdims=True))
    return centre * lax.rsqrt(spread + EPS_NORM) * gain + shift

def encoder(value, weight_one, bias_one, weight_two, vector_set, cos_pos, sin_pos, cos_feat, sin_feat):
    factor_mix = 1.0 / math.sqrt(L * D)
    rounded = low(value)
    spec_cos = low(low_back(matmul(cos_pos, rounded)))
    spec_sin = low(low_back(matmul(sin_pos, rounded)))
    mixed = low_back(factor_mix * (matmul(spec_cos, cos_feat) - matmul(spec_sin, sin_feat)))
    normed = layer_norm(value + mixed, vector_set[0], vector_set[1])
    pre_act = low_back(matmul(low(normed), low(weight_one)) + low(bias_one))
    acts = low(jax.nn.gelu(pre_act))
    branch = low_back(matmul(acts, low(weight_two)) + vector_set[2])
    return layer_norm(normed + branch, vector_set[3], vector_set[4])

def adamw(weight, grad, moment, square, rate, decay):
    new_moment = BETA_ONE * moment + (1.0 - BETA_ONE) * grad
    new_square = BETA_TWO * square + (1.0 - BETA_TWO) * grad * grad
    moment_hat = new_moment / (1.0 - BETA_ONE ** STEP)
    square_hat = new_square / (1.0 - BETA_TWO ** STEP)
    new_weight = weight - rate * (moment_hat / (jnp.sqrt(square_hat) + EPS_ADAM) + decay * weight)
    return (new_moment, new_square, new_weight)

def reference(tokens, cotangent, weight_in, bias_in, weight_out, vectors, moment_in, square_in, moment_bias, square_bias, moment_out, square_out, moment_vec, square_vec):
    cos_pos, sin_pos = tables(L)
    cos_feat, sin_feat = tables(D)
    params = (weight_in, bias_in, weight_out, vectors)

    def network(value, param_set):
        for layer_at in range(LAYERS):
            value = encoder(value, param_set[0][layer_at], param_set[1][layer_at], param_set[2][layer_at], param_set[3][layer_at], cos_pos, sin_pos, cos_feat, sin_feat)
        return value

    def per_sequence(carry, pair):
        inputs, cot_seq = pair
        result, pull = jax.vjp(network, inputs.astype(jnp.float32), params)
        grad_value, grad_params = pull(cot_seq.astype(jnp.float32))
        carry = jax.tree.map(lambda acc, new: acc + new, carry, grad_params)
        return (carry, (result.astype(jnp.bfloat16), grad_value))
    zeros = jax.tree.map(jnp.zeros_like, params)
    sums, (results, grad_inputs) = lax.scan(per_sequence, zeros, (jnp.swapaxes(tokens, 0, 1), jnp.swapaxes(cotangent, 0, 1)))
    activations = jnp.swapaxes(results, 0, 1)
    input_grad = jnp.swapaxes(grad_inputs, 0, 1)
    grad_in, grad_bias, grad_out, grad_vec = sums
    total = jnp.sum(grad_in * grad_in) + jnp.sum(grad_bias * grad_bias) + jnp.sum(grad_out * grad_out) + jnp.sum(grad_vec * grad_vec)
    grad_norm = jnp.sqrt(total)
    factor = jnp.minimum(1.0, CLIP / grad_norm)
    m_in, v_in, w_in = adamw(weight_in, grad_in * factor, moment_in, square_in, 1.0 / math.sqrt(D), DECAY)
    m_out, v_out, w_out = adamw(weight_out, grad_out * factor, moment_out, square_out, 1.0 / math.sqrt(FF), DECAY)
    m_bias, v_bias, b_new = adamw(bias_in, grad_bias * factor, moment_bias, square_bias, 0.5, 0.0)
    m_vec, v_vec, vec_new = adamw(vectors, grad_vec * factor, moment_vec, square_vec, 0.5, 0.0)
    return (activations, input_grad, grad_norm, m_in, v_in, w_in, w_in.astype(jnp.bfloat16), m_out, v_out, w_out, w_out.astype(jnp.bfloat16), m_bias, v_bias, b_new, m_vec, v_vec, vec_new)
```

```python
import functools
import math

import jax
import jax.numpy as jnp
import ml_dtypes
import numpy as np
from jax import lax
from jax.experimental import pallas as pl
from jax.experimental.pallas import tpu as pltpu
from jax.sharding import PartitionSpec as P

D = 768
FF = 3072
L = 4096
LAYERS = 2
STEP = 5


CLIP = 1.0
BETA_ONE = 0.5
BETA_TWO = 0.5
EPS_ADAM = 1e-08
EPS_NORM = 1e-05
DECAY = 0.01
MESH = pl.DeviceIdType.MESH
F32 = jnp.float32
BF16 = jnp.bfloat16


class Plan:
    def __init__(self, parts):
        self.parts = parts
        self.rows = L // parts
        self.inner = self.rows // parts
        self.pairs = D // 2 // parts
        self.feats = -(-2 * self.pairs // 16) * 16
        rows, inner = self.rows, self.inner
        lane = np.arange(rows)
        self.place = parts * (lane % inner) + lane // inner
        packed = np.zeros((parts, self.feats, D))
        rebuild = np.zeros((parts, self.feats, D))
        n = np.arange(D)
        for at in range(parts):
            for i in range(self.pairs):
                m = self.pairs * at + i
                a, b = i, self.pairs + i
                packed[at, a] = np.cos(2 * np.pi * (m * n % D) / D)
                rebuild[at, a, m] = 1.0
                if m == 0:
                    packed[at, b] = np.cos(2 * np.pi * (D // 2 * n % D) / D)
                    rebuild[at, b, D // 2] = 1.0
                else:
                    packed[at, b] = np.sin(2 * np.pi * (m * n % D) / D)
                    rebuild[at, a, D - m] = 1.0
                    rebuild[at, b, m] = -1.0
                    rebuild[at, b, D - m] = 1.0
        bf = ml_dtypes.bfloat16
        self.packed = packed.reshape(-1, D).astype(bf)
        self.rebuild = rebuild.reshape(-1, D).astype(bf)
        turn = 2 * np.pi * (np.arange(parts)[:, None] * self.place[None, :] % L) / L
        self.turn = np.stack([np.cos(turn), np.sin(turn)]).astype(np.float32)
        angle = 2 * np.pi * (self.place[:, None] * np.arange(rows)[None, :] % rows) / rows
        self.wave = np.concatenate([np.cos(angle), np.sin(angle)]).astype(bf)


def half_dft(values):
    n = len(values)
    if n == 1:
        return [(values[0], None)]
    if n == 2:
        return [(values[0] + values[1], None), (values[0] - values[1], None)]
    even, odd = half_dft(values[0::2]), half_dft(values[1::2])
    half = n // 2
    result = [None] * (half + 1)
    for k in range(half // 2 + 1):
        er, ei = even[k]
        orr, oi = odd[k]
        if k == 0:
            result[0] = (er + orr, None)
            result[half] = (er - orr, None)
        elif 2 * k == half:
            result[k] = (er, -orr)
        else:
            c, s = math.cos(2 * math.pi * k / n), math.sin(2 * math.pi * k / n)
            tr, ti = orr * c + oi * s, oi * c - orr * s
            result[k] = (er + tr, ei + ti)
            result[half - k] = (er - tr, ti - ei)
    return result


def position_dft(plan, me, recv, work, send, turn_ref, wave_ref):
    parts, feats, rows, inner, pairs = plan.parts, plan.feats, plan.rows, plan.inner, plan.pairs
    chunk = 16
    lanes = min(rows, 128)
    for lane_at in range(0, rows, lanes):

        def body(i, carry):
            at = pl.multiple_of(i * chunk, chunk)
            values = [recv[p, pl.ds(at, chunk), lane_at : lane_at + lanes].astype(F32) for p in range(parts)]
            outs = half_dft(values)
            row = at + lax.broadcasted_iota(jnp.int32, (chunk, lanes), 0)
            is_sine = (row >= pairs) & jnp.logical_not((row == pairs) & (me == 0))
            for d in range(parts):
                re, im = outs[min(d, parts - d)]
                im = jnp.zeros_like(re) if im is None else im
                if d > parts - d:
                    im = -im
                re, im = jnp.where(is_sine, -im, re), jnp.where(is_sine, re, im)
                c = turn_ref[0, d : d + 1, lane_at : lane_at + lanes]
                s = turn_ref[1, d : d + 1, lane_at : lane_at + lanes]
                work[d, pl.ds(at, chunk), lane_at : lane_at + lanes] = (re * c + im * s).astype(BF16)
                work[d, pl.ds(at, chunk), rows + lane_at : rows + lane_at + lanes] = (im * c - re * s).astype(BF16)
            return carry

        lax.fori_loop(0, feats // chunk, body, 0)

    def swap(i, carry):
        at = pl.multiple_of(i * chunk, chunk)
        outs = [
            jnp.dot(work[d, pl.ds(at, chunk), :], wave_ref[...], preferred_element_type=F32)
            for d in range(parts)
        ]
        group = lax.broadcasted_iota(jnp.int32, (chunk, rows), 1) // inner
        bit = 1
        while bit < parts:
            upper = (group // bit) % 2 == 1
            for d in range(parts):
                if d & bit:
                    continue
                low, high = outs[d], outs[d | bit]
                shift = inner * bit
                outs[d] = jnp.where(upper, pltpu.roll(high, shift, 1), low)
                outs[d | bit] = jnp.where(upper, high, pltpu.roll(low, rows - shift, 1))
            bit *= 2
        for q in range(parts):
            send[q, pl.ds(at, chunk), :] = outs[q].astype(BF16)
        return carry

    lax.fori_loop(0, feats // chunk, swap, 0)


def exchange(plan, me, send, recv, send_sem, recv_sem):
    parts = plan.parts

    def copy_to(k):
        q = lax.rem(me + k, parts)
        return pltpu.make_async_remote_copy(
            src_ref=send.at[q],
            dst_ref=recv.at[me],
            send_sem=send_sem.at[q],
            recv_sem=recv_sem.at[me],
            device_id={"mp": q},
            device_id_type=MESH,
        )

    def copy_from(k):
        p = lax.rem(me + k, parts)
        return pltpu.make_async_remote_copy(
            src_ref=send.at[p],
            dst_ref=recv.at[p],
            send_sem=send_sem.at[p],
            recv_sem=recv_sem.at[p],
            device_id={"mp": p},
            device_id_type=MESH,
        )

    def start(k, carry):
        copy_to(k).start()
        return carry

    def finish(k, carry):
        copy_from(k).wait_recv()
        return carry

    def drain(k, carry):
        copy_to(k).wait_send()
        return carry

    lax.fori_loop(1, parts, start, 0)
    recv[me] = send[me]
    lax.fori_loop(1, parts, finish, 0)
    lax.fori_loop(1, parts, drain, 0)


def mix_kernel(plan, x_ref, packed_ref, rebuild_ref, turn_ref, wave_ref, out_ref, send, recv, work, send_back, recv_back, sems):
    me = lax.axis_index("mp")
    parts, feats, rows = plan.parts, plan.feats, plan.rows
    barrier = pltpu.get_barrier_semaphore()

    def greet(k, carry):
        pl.semaphore_signal(barrier, inc=1, device_id={"mp": lax.rem(me + k, parts)}, device_id_type=MESH)
        return carry

    lax.fori_loop(1, parts, greet, 0)
    pl.semaphore_wait(barrier, parts - 1)

    columns = lax.dot_general(packed_ref[...], x_ref[...], (((1,), (1,)), ((), ())), preferred_element_type=F32)
    send[...] = columns.astype(BF16).reshape(parts, feats, rows)
    exchange(plan, me, send, recv, sems.at[0], sems.at[1])
    position_dft(plan, me, recv, work, send_back, turn_ref, wave_ref)
    exchange(plan, me, send_back, recv_back, sems.at[2], sems.at[3])
    mixed = lax.dot_general(
        recv_back[...].reshape(parts * feats, rows), rebuild_ref[...], (((0,), (0,)), ((), ())), preferred_element_type=F32
    )
    out_ref[...] = mixed * (1.0 / math.sqrt(L * D))


def mix(plan, value):
    block = (plan.parts, plan.feats, plan.rows)
    return pl.pallas_call(
        functools.partial(mix_kernel, plan),
        out_shape=jax.ShapeDtypeStruct((plan.rows, D), F32),
        in_specs=[pl.BlockSpec(memory_space=pltpu.VMEM)] * 5,
        out_specs=pl.BlockSpec(memory_space=pltpu.VMEM),
        scratch_shapes=[
            pltpu.VMEM(block, BF16),
            pltpu.VMEM(block, BF16),
            pltpu.VMEM((plan.parts, plan.feats, 2 * plan.rows), BF16),
            pltpu.VMEM(block, BF16),
            pltpu.VMEM(block, BF16),
            pltpu.SemaphoreType.DMA((4, plan.parts)),
        ],
        compiler_params=pltpu.CompilerParams(
            collective_id=0, has_side_effects=True, vmem_limit_bytes=40 * 2**20
        ),
    )(value, plan.packed, plan.rebuild, plan.turn, plan.wave)


def matmul(left_op, right_op):
    return jnp.dot(left_op, right_op, preferred_element_type=jnp.float32)


def inner_rows(left_op, right_op):
    return lax.dot_general(
        left_op, right_op, (((0,), (0,)), ((), ())), preferred_element_type=jnp.float32
    )


def inner_cols(left_op, right_op):
    return lax.dot_general(
        left_op, right_op, (((1,), (1,)), ((), ())), preferred_element_type=jnp.float32
    )


def layer_norm(value, gain, shift):
    centre = value - jnp.mean(value, axis=-1, keepdims=True)
    spread = jnp.mean(centre * centre, axis=-1, keepdims=True)
    return centre * lax.rsqrt(spread + EPS_NORM) * gain + shift


def adamw(weight, grad, moment, square, rate, decay):
    new_moment = BETA_ONE * moment + (1.0 - BETA_ONE) * grad
    new_square = BETA_TWO * square + (1.0 - BETA_TWO) * grad * grad
    moment_hat = new_moment / (1.0 - BETA_ONE**STEP)
    square_hat = new_square / (1.0 - BETA_TWO**STEP)
    new_weight = weight - rate * (moment_hat / (jnp.sqrt(square_hat) + EPS_ADAM) + decay * weight)
    return (new_moment, new_square, new_weight)


def on_device(
    tokens,
    cotangent,
    weight_in,
    bias_in,
    weight_out,
    vectors,
    moment_in,
    square_in,
    moment_bias,
    square_bias,
    moment_out,
    square_out,
    moment_vec,
    square_vec,
):
    row_count, seq_count, feat_count = tokens.shape
    plan = Plan(L // row_count)

    def localize(value):
        return jnp.swapaxes(value.reshape(plan.inner, plan.parts, -1), 0, 1).reshape(value.shape)

    def restore(value):
        return jnp.swapaxes(value.reshape(plan.parts, plan.inner, -1), 0, 1).reshape(value.shape)

    current = localize(tokens).astype(jnp.float32)
    saved = []
    for layer_at in range(LAYERS):
        vector_set = vectors[layer_at]
        rounded = current.astype(jnp.bfloat16)
        mixed = mix(plan, rounded.reshape(row_count, feat_count)).reshape(row_count, seq_count, feat_count)
        summed = current + mixed
        normed = layer_norm(summed, vector_set[0], vector_set[1])
        hidden_in = normed.astype(jnp.bfloat16)
        weight_one = weight_in[layer_at].astype(jnp.bfloat16)
        weight_two = weight_out[layer_at].astype(jnp.bfloat16)
        bias_one = bias_in[layer_at].astype(jnp.bfloat16)
        whole_one, whole_two, whole_bias = (
            lax.all_gather(weight_one, "mp", axis=1, tiled=True),
            lax.all_gather(weight_two, "mp", axis=0, tiled=True),
            lax.all_gather(bias_one, "mp", axis=0, tiled=True),
        )
        inputs = hidden_in.reshape(-1, feat_count)
        pre_act = matmul(inputs, whole_one) + whole_bias.astype(jnp.float32)
        acts = jax.nn.gelu(pre_act).astype(jnp.bfloat16)
        branch = matmul(acts, whole_two).reshape(row_count, seq_count, feat_count)
        held = (inputs, whole_one, whole_two)
        total = normed + branch + vector_set[2]
        current = layer_norm(total, vector_set[3], vector_set[4])
        saved.append((summed, total, pre_act, acts, held))
    activations = restore(current.astype(jnp.bfloat16))
    grad = localize(cotangent).astype(jnp.float32)
    layer_grads = [None] * LAYERS
    for layer_at in reversed(range(LAYERS)):
        vector_set = vectors[layer_at]
        summed, total, pre_act, acts, held = saved[layer_at]
        inputs, mat_one, mat_two = held
        _, pull_out = jax.vjp(layer_norm, total, vector_set[3], vector_set[4])
        grad_total, gain_two, shift_two = pull_out(grad)
        grad_branch = grad_total.astype(jnp.bfloat16)
        grad_bias_two = jnp.sum(grad_branch.astype(jnp.float32), axis=(0, 1))
        flat_grad = grad_branch.reshape(-1, feat_count)
        grad_act = inner_cols(flat_grad, mat_two)
        _, pull_gelu = jax.vjp(jax.nn.gelu, pre_act)
        grad_pre = pull_gelu(grad_act)[0].astype(jnp.bfloat16)
        full_one = inner_rows(inputs, grad_pre)
        full_two = inner_rows(acts, flat_grad)
        full_bias = jnp.sum(grad_pre.astype(jnp.float32), axis=0)
        grad_one, grad_two, grad_bias_one = (
            lax.psum_scatter(
                full_one.astype(jnp.bfloat16), "mp", scatter_dimension=1, tiled=True
            ).astype(jnp.float32),
            lax.psum_scatter(
                full_two.astype(jnp.bfloat16), "mp", scatter_dimension=0, tiled=True
            ).astype(jnp.float32),
            lax.psum_scatter(
                full_bias.astype(jnp.bfloat16), "mp", scatter_dimension=0, tiled=True
            ).astype(jnp.float32),
        )
        grad_normed = inner_cols(grad_pre, mat_one).reshape(row_count, seq_count, feat_count)
        grad_normed = grad_normed + grad_total
        _, pull_in = jax.vjp(layer_norm, summed, vector_set[0], vector_set[1])
        grad_summed, gain_one, shift_one = pull_in(grad_normed)
        mix_grad = grad_summed.astype(jnp.bfloat16).reshape(-1, feat_count)
        grad_mix = mix(plan, mix_grad).reshape(row_count, seq_count, feat_count)
        grad = grad_summed + grad_mix
        layer_grads[layer_at] = (
            grad_one,
            grad_two,
            grad_bias_one,
            jnp.stack([gain_one, shift_one, grad_bias_two, gain_two, shift_two]),
        )
    stack_in = jnp.stack([entry[0] for entry in layer_grads])
    stack_out = jnp.stack([entry[1] for entry in layer_grads])
    stack_bias = jnp.stack([entry[2] for entry in layer_grads])
    stack_vec = jnp.stack([entry[3] for entry in layer_grads])
    sum_in, sum_out, sum_bias, sum_vec = (
        lax.psum(stack_in.astype(jnp.bfloat16), "dp").astype(jnp.float32),
        lax.psum(stack_out.astype(jnp.bfloat16), "dp").astype(jnp.float32),
        lax.psum(stack_bias.astype(jnp.bfloat16), "dp").astype(jnp.float32),
        lax.psum(stack_vec.astype(jnp.bfloat16), "dp").astype(jnp.float32),
    )
    local_squares = (
        jnp.sum(sum_in * sum_in) + jnp.sum(sum_out * sum_out) + jnp.sum(sum_bias * sum_bias)
    )
    sum_vec, total_squares = lax.psum((sum_vec, local_squares), "mp")
    grad_norm = jnp.sqrt(total_squares + jnp.sum(sum_vec * sum_vec))
    factor = jnp.minimum(1.0, CLIP / grad_norm)
    m_in, v_in, w_in = adamw(
        weight_in, sum_in * factor, moment_in, square_in, 1.0 / math.sqrt(D), DECAY
    )
    m_out, v_out, w_out = adamw(
        weight_out, sum_out * factor, moment_out, square_out, 1.0 / math.sqrt(FF), DECAY
    )
    m_bias, v_bias, b_new = adamw(bias_in, sum_bias * factor, moment_bias, square_bias, 0.5, 0.0)
    m_vec, v_vec, vec_new = adamw(vectors, sum_vec * factor, moment_vec, square_vec, 0.5, 0.0)
    return (
        activations,
        restore(grad),
        grad_norm,
        m_in,
        v_in,
        w_in,
        w_in.astype(jnp.bfloat16),
        m_out,
        v_out,
        w_out,
        w_out.astype(jnp.bfloat16),
        m_bias,
        v_bias,
        b_new,
        m_vec,
        v_vec,
        vec_new,
    )


def solution(mesh):
    return jax.shard_map(
        on_device,
        mesh=mesh,
        in_specs=(
            P("mp", "dp", None),
            P("mp", "dp", None),
            P(None, None, "mp"),
            P(None, "mp"),
            P(None, "mp", None),
            P(),
            P(None, None, "mp"),
            P(None, None, "mp"),
            P(None, "mp"),
            P(None, "mp"),
            P(None, "mp", None),
            P(None, "mp", None),
            P(),
            P(),
        ),
        out_specs=(
            P("mp", "dp", None),
            P("mp", "dp", None),
            P(),
            P(None, None, "mp"),
            P(None, None, "mp"),
            P(None, None, "mp"),
            P(None, None, "mp"),
            P(None, "mp", None),
            P(None, "mp", None),
            P(None, "mp", None),
            P(None, "mp", None),
            P(None, "mp"),
            P(None, "mp"),
            P(None, "mp"),
            P(),
            P(),
            P(),
        ),
        check_vma=False,
    )
```

```python
import functools
import math

import jax
import jax.numpy as jnp
import ml_dtypes
import numpy as np
from jax import lax
from jax.experimental import pallas as pl
from jax.experimental.pallas import tpu as pltpu
from jax.sharding import PartitionSpec as P

D = 768
FF = 3072
L = 4096
LAYERS = 2
STEP = 5


CLIP = 1.0
BETA_ONE = 0.5
BETA_TWO = 0.5
EPS_ADAM = 1e-08
EPS_NORM = 1e-05
DECAY = 0.01
MESH = pl.DeviceIdType.MESH
F32 = jnp.float32
BF16 = jnp.bfloat16


class Plan:
    def __init__(self, parts):
        self.parts = parts
        self.rows = L // parts
        self.inner = self.rows // parts
        self.pairs = D // 2 // parts
        self.feats = -(-2 * self.pairs // 16) * 16
        rows, inner = self.rows, self.inner
        lane = np.arange(rows)
        self.place = parts * (lane % inner) + lane // inner
        packed = np.zeros((parts, self.feats, D))
        rebuild = np.zeros((parts, self.feats, D))
        n = np.arange(D)
        for at in range(parts):
            for i in range(self.pairs):
                m = self.pairs * at + i
                a, b = i, self.pairs + i
                packed[at, a] = np.cos(2 * np.pi * (m * n % D) / D)
                rebuild[at, a, m] = 1.0
                if m == 0:
                    packed[at, b] = np.cos(2 * np.pi * (D // 2 * n % D) / D)
                    rebuild[at, b, D // 2] = 1.0
                else:
                    packed[at, b] = np.sin(2 * np.pi * (m * n % D) / D)
                    rebuild[at, a, D - m] = 1.0
                    rebuild[at, b, m] = -1.0
                    rebuild[at, b, D - m] = 1.0
        bf = ml_dtypes.bfloat16
        self.packed = packed.reshape(-1, D).astype(bf)
        self.rebuild = rebuild.reshape(-1, D).astype(bf)
        turn = 2 * np.pi * (np.arange(parts)[:, None] * self.place[None, :] % L) / L
        self.turn = np.stack([np.cos(turn), np.sin(turn)]).astype(np.float32)
        angle = 2 * np.pi * (self.place[:, None] * np.arange(rows)[None, :] % rows) / rows
        self.wave = np.concatenate([np.cos(angle), np.sin(angle)]).astype(bf)


def half_dft(values):
    n = len(values)
    if n == 1:
        return [(values[0], None)]
    if n == 2:
        return [(values[0] + values[1], None), (values[0] - values[1], None)]
    even, odd = half_dft(values[0::2]), half_dft(values[1::2])
    half = n // 2
    result = [None] * (half + 1)
    for k in range(half // 2 + 1):
        er, ei = even[k]
        orr, oi = odd[k]
        if k == 0:
            result[0] = (er + orr, None)
            result[half] = (er - orr, None)
        elif 2 * k == half:
            result[k] = (er, -orr)
        else:
            c, s = math.cos(2 * math.pi * k / n), math.sin(2 * math.pi * k / n)
            tr, ti = orr * c + oi * s, oi * c - orr * s
            result[k] = (er + tr, ei + ti)
            result[half - k] = (er - tr, ti - ei)
    return result


def position_dft(plan, me, recv, work, send, turn_ref, wave_ref):
    parts, feats, rows, inner, pairs = plan.parts, plan.feats, plan.rows, plan.inner, plan.pairs
    chunk = 16
    lanes = min(rows, 128)
    for lane_at in range(0, rows, lanes):

        def body(i, carry):
            at = pl.multiple_of(i * chunk, chunk)
            values = [recv[p, pl.ds(at, chunk), lane_at : lane_at + lanes].astype(F32) for p in range(parts)]
            outs = half_dft(values)
            row = at + lax.broadcasted_iota(jnp.int32, (chunk, lanes), 0)
            is_sine = (row >= pairs) & jnp.logical_not((row == pairs) & (me == 0))
            for d in range(parts):
                re, im = outs[min(d, parts - d)]
                im = jnp.zeros_like(re) if im is None else im
                if d > parts - d:
                    im = -im
                re, im = jnp.where(is_sine, -im, re), jnp.where(is_sine, re, im)
                c = turn_ref[0, d : d + 1, lane_at : lane_at + lanes]
                s = turn_ref[1, d : d + 1, lane_at : lane_at + lanes]
                work[d, pl.ds(at, chunk), lane_at : lane_at + lanes] = (re * c + im * s).astype(BF16)
                work[d, pl.ds(at, chunk), rows + lane_at : rows + lane_at + lanes] = (im * c - re * s).astype(BF16)
            return carry

        lax.fori_loop(0, feats // chunk, body, 0)

    def swap(i, carry):
        at = pl.multiple_of(i * chunk, chunk)
        outs = [
            jnp.dot(work[d, pl.ds(at, chunk), :], wave_ref[...], preferred_element_type=F32)
            for d in range(parts)
        ]
        group = lax.broadcasted_iota(jnp.int32, (chunk, rows), 1) // inner
        bit = 1
        while bit < parts:
            upper = (group // bit) % 2 == 1
            for d in range(parts):
                if d & bit:
                    continue
                low, high = outs[d], outs[d | bit]
                shift = inner * bit
                outs[d] = jnp.where(upper, pltpu.roll(high, shift, 1), low)
                outs[d | bit] = jnp.where(upper, high, pltpu.roll(low, rows - shift, 1))
            bit *= 2
        for q in range(parts):
            send[q, pl.ds(at, chunk), :] = outs[q].astype(BF16)
        return carry

    lax.fori_loop(0, feats // chunk, swap, 0)


def exchange(plan, me, send, recv, send_sem, recv_sem):
    parts = plan.parts

    def copy_to(k):
        q = lax.rem(me + k, parts)
        return pltpu.make_async_remote_copy(
            src_ref=send.at[q],
            dst_ref=recv.at[me],
            send_sem=send_sem.at[q],
            recv_sem=recv_sem.at[me],
            device_id={"mp": q},
            device_id_type=MESH,
        )

    def copy_from(k):
        p = lax.rem(me + k, parts)
        return pltpu.make_async_remote_copy(
            src_ref=send.at[p],
            dst_ref=recv.at[p],
            send_sem=send_sem.at[p],
            recv_sem=recv_sem.at[p],
            device_id={"mp": p},
            device_id_type=MESH,
        )

    def start(k, carry):
        copy_to(k).start()
        return carry

    def finish(k, carry):
        copy_from(k).wait_recv()
        return carry

    def drain(k, carry):
        copy_to(k).wait_send()
        return carry

    lax.fori_loop(1, parts, start, 0)
    recv[me] = send[me]
    lax.fori_loop(1, parts, finish, 0)
    lax.fori_loop(1, parts, drain, 0)


def mix_kernel(plan, x_ref, packed_ref, rebuild_ref, turn_ref, wave_ref, out_ref, send, recv, work, send_back, recv_back, sems):
    me = lax.axis_index("mp")
    parts, feats, rows = plan.parts, plan.feats, plan.rows
    barrier = pltpu.get_barrier_semaphore()

    def greet(k, carry):
        pl.semaphore_signal(barrier, inc=1, device_id={"mp": lax.rem(me + k, parts)}, device_id_type=MESH)
        return carry

    lax.fori_loop(1, parts, greet, 0)
    pl.semaphore_wait(barrier, parts - 1)

    columns = lax.dot_general(packed_ref[...], x_ref[...], (((1,), (1,)), ((), ())), preferred_element_type=F32)
    send[...] = columns.astype(BF16).reshape(parts, feats, rows)
    exchange(plan, me, send, recv, sems.at[0], sems.at[1])
    position_dft(plan, me, recv, work, send_back, turn_ref, wave_ref)
    exchange(plan, me, send_back, recv_back, sems.at[2], sems.at[3])
    mixed = lax.dot_general(
        recv_back[...].reshape(parts * feats, rows), rebuild_ref[...], (((0,), (0,)), ((), ())), preferred_element_type=F32
    )
    out_ref[...] = mixed * (1.0 / math.sqrt(L * D))


def mix(plan, value):
    block = (plan.parts, plan.feats, plan.rows)
    return pl.pallas_call(
        functools.partial(mix_kernel, plan),
        out_shape=jax.ShapeDtypeStruct((plan.rows, D), F32),
        in_specs=[pl.BlockSpec(memory_space=pltpu.VMEM)] * 5,
        out_specs=pl.BlockSpec(memory_space=pltpu.VMEM),
        scratch_shapes=[
            pltpu.VMEM(block, BF16),
            pltpu.VMEM(block, BF16),
            pltpu.VMEM((plan.parts, plan.feats, 2 * plan.rows), BF16),
            pltpu.VMEM(block, BF16),
            pltpu.VMEM(block, BF16),
            pltpu.SemaphoreType.DMA((4, plan.parts)),
        ],
        compiler_params=pltpu.CompilerParams(
            collective_id=0, has_side_effects=True, vmem_limit_bytes=40 * 2**20
        ),
    )(value, plan.packed, plan.rebuild, plan.turn, plan.wave)


class Spot:
    def __init__(self):
        self.y = lax.axis_index("dp")
        self.me = lax.axis_index("mp")
        self.z, self.x, self.core = self.me // 4, (self.me // 2) % 2, self.me % 2
        self.own = self.me // 2

    def at(self, y=None, z=None, x=None, core=None):
        y = self.y if y is None else y
        z = self.z if z is None else z
        x = self.x if x is None else x
        core = self.core if core is None else core
        return {"dp": y, "mp": z * 4 + x * 2 + core}

    def y_mate(self):
        return self.at(y=1 - self.y)

    def x_mate(self):
        return self.at(x=1 - self.x)

    def core_mate(self):
        return self.at(core=1 - self.core)

    def z_mate(self, k):
        return self.at(z=self.z ^ k)


class Lines:
    def __init__(self, send_sems, recv_sems):
        self.send_sems, self.recv_sems = send_sems, recv_sems
        self.sent = []

    def copy(self, number, src, dst, device):
        return pltpu.make_async_remote_copy(
            src_ref=src,
            dst_ref=dst,
            send_sem=self.send_sems.at[number],
            recv_sem=self.recv_sems.at[number],
            device_id=device,
            device_id_type=MESH,
        )

    def send(self, number, src, dst, device):
        self.copy(number, src, dst, device).start()
        self.sent.append((number, src, device))

    def wait(self, number, land, device):
        self.copy(number, land, land, device).wait_recv()

    def drain(self):
        for number, src, device in self.sent:
            self.copy(number, src, src, device).wait_send()
        self.sent = []


class Gather:
    def __init__(self, spot, lines, base, win_own, wout_own, win, wout):
        self.spot, self.lines, self.base = spot, lines, base
        self.win_own, self.wout_own, self.win, self.wout = win_own, wout_own, win, wout

    def start(self):
        s, n, b = self.spot, self.lines, self.base
        n.send(b + 13, self.win_own, self.win.at[s.z, s.x], s.x_mate())
        n.send(b + 9, self.wout_own.at[s.y], self.wout.at[s.z, s.x, s.y], s.x_mate())
        for k in (1, 2, 3):
            n.send(b + 2 * k - 2, self.win_own.at[s.y], self.win.at[s.z, s.x, s.y], s.z_mate(k))
            n.send(b + 2 * k - 1, self.wout_own.at[s.y], self.wout.at[s.z, s.x, s.y], s.z_mate(k))
        self.win[s.z, s.x] = self.win_own[...]
        self.wout[s.z, s.x] = self.wout_own[...]

    def second(self, k):
        s, n, b = self.spot, self.lines, self.base
        zk = s.z ^ k
        a, c = self.win.at[zk, s.x, s.y], self.wout.at[zk, s.x, s.y]
        n.wait(b + 2 * k - 2, a, s.z_mate(k))
        n.wait(b + 2 * k - 1, c, s.z_mate(k))
        n.send(b + 5 + k, a, a, s.y_mate())
        n.send(b + 9 + k, c, c, s.x_mate())
        n.send(b + 17 + 2 * k, c, c, s.y_mate())

    def third(self, k):
        s, n, b = self.spot, self.lines, self.base
        zk = s.z ^ k
        if k:
            n.wait(b + 5 + k, self.win.at[zk, s.x, 1 - s.y], s.y_mate())
            n.send(b + 13 + k, self.win.at[zk, s.x], self.win.at[zk, s.x], s.x_mate())
        far = self.wout.at[zk, 1 - s.x, s.y]
        n.wait(b + 9 + k, far, s.x_mate())
        n.send(b + 18 + 2 * k, far, far, s.y_mate())

    def finish(self, k):
        s, n, b = self.spot, self.lines, self.base
        zk = s.z ^ k
        n.wait(b + 13 + k, self.win.at[zk, 1 - s.x], s.x_mate())
        if k:
            n.wait(b + 17 + 2 * k, self.wout.at[zk, s.x, 1 - s.y], s.y_mate())
        n.wait(b + 18 + 2 * k, self.wout.at[zk, 1 - s.x, 1 - s.y], s.y_mate())


GATHER_LINES = 25


class Reduce:
    def __init__(self, spot, lines, base, din, dout, xin, yout, yin, xout, zin, result):
        self.spot, self.lines, self.base = spot, lines, base
        self.din, self.dout, self.xin, self.yout = din, dout, xin, yout
        self.yin, self.xout, self.zin, self.result = yin, xout, zin, result

    @staticmethod
    def add(ref, more):
        ref[...] = (ref[...].astype(F32) + more[...].astype(F32)).astype(BF16)

    def first_in(self, k):
        s, n, b = self.spot, self.lines, self.base
        n.send(b + k, self.din.at[s.z ^ k, 1 - s.x], self.xin.at[k], s.x_mate())

    def first_out(self, k):
        s, n, b = self.spot, self.lines, self.base
        for x in (0, 1):
            n.send(b + 4 + 2 * k + x, self.dout.at[s.z ^ k, x, 1 - s.y], self.yout.at[k, x], s.y_mate())

    def second(self, k):
        s, n, b = self.spot, self.lines, self.base
        zk = s.z ^ k
        n.wait(b + k, self.xin.at[k], s.x_mate())
        self.add(self.din.at[zk, s.x], self.xin.at[k])
        n.send(b + 12 + k, self.din.at[zk, s.x, 1 - s.y], self.yin.at[k], s.y_mate())
        for x in (0, 1):
            n.wait(b + 4 + 2 * k + x, self.yout.at[k, x], s.y_mate())
            self.add(self.dout.at[zk, x, s.y], self.yout.at[k, x])
        n.send(b + 16 + k, self.dout.at[zk, 1 - s.x, s.y], self.xout.at[k], s.x_mate())

    def third(self, k):
        s, n, b = self.spot, self.lines, self.base
        zk = s.z ^ k
        a, c = self.din.at[zk, s.x, s.y], self.dout.at[zk, s.x, s.y]
        n.wait(b + 12 + k, self.yin.at[k], s.y_mate())
        self.add(a, self.yin.at[k])
        if k:
            n.send(b + 20 + 2 * k, a, self.zin.at[k - 1, 0], s.z_mate(k))
        n.wait(b + 16 + k, self.xout.at[k], s.x_mate())
        self.add(c, self.xout.at[k])
        if k:
            n.send(b + 21 + 2 * k, c, self.zin.at[k - 1, 1], s.z_mate(k))

    def fourth(self):
        s, n, b = self.spot, self.lines, self.base
        for i, part in ((0, self.din), (1, self.dout)):
            total = part[s.z, s.x, s.y].astype(F32)
            for k in (1, 2, 3):
                n.wait(b + 20 + 2 * k + i, self.zin.at[k - 1, i], s.z_mate(k))
                total = total + self.zin[k - 1, i].astype(F32)
            self.result[i, s.y] = total.astype(BF16)
            n.send(b + 20 + i, self.result.at[i, s.y], self.result.at[i, s.y], s.y_mate())

    def finish(self):
        s, n, b = self.spot, self.lines, self.base
        for i in (0, 1):
            n.wait(b + 20 + i, self.result.at[i, 1 - s.y], s.y_mate())


REDUCE_LINES = 28


def normalize(value):
    centre = value - jnp.mean(value, axis=-1, keepdims=True)
    scale = lax.rsqrt(jnp.mean(centre * centre, axis=-1, keepdims=True) + EPS_NORM)
    return centre * scale, scale


def normalize_back(grad, gain, unit, scale):
    gain_grad = jnp.sum(grad * unit, axis=0, keepdims=True)
    shift_grad = jnp.sum(grad, axis=0, keepdims=True)
    inner = grad * gain
    mean = jnp.mean(inner, axis=-1, keepdims=True)
    along = jnp.mean(inner * unit, axis=-1, keepdims=True)
    return scale * (inner - mean - unit * along), gain_grad, shift_grad


def dot_t(left, right):
    return lax.dot_general(left, right, (((1,), (1,)), ((), ())), preferred_element_type=F32)


def t_dot(left, right):
    return lax.dot_general(left, right, (((0,), (0,)), ((), ())), preferred_element_type=F32)


def gelu_pair(v):
    root = math.sqrt(2.0 / math.pi)
    square = v * v
    tanh = jnp.tanh(root * v * (1.0 + 0.044715 * square))
    half = 0.5 + 0.5 * tanh
    slope = half + 0.5 * v * (1.0 - tanh * tanh) * (root * (1.0 + 3 * 0.044715 * square))
    return v * half, slope


def fused_kernel(
    plan,
    tokens, cotangent, win_own, wout_own, bias_own, vec, packed, rebuild, turn, wave,
    act_out, grad_out, weights_out, vec_out, square_out,
    win, wout, bias_all, hidden, acts, slopes, unit_mix, unit_out, scale_mix, scale_out, normed_keep,
    branch_send, branch_recv, grad_branch, grad_pre,
    din, dout, xin, yout, yin, xout, zin,
    send, recv, work, send_back, recv_back,
    vec_send, vec_recv, square_send, square_recv,
    mix_sems, send_sems, recv_sems,
):
    spot = Spot()
    lines = Lines(send_sems, recv_sems)
    parts, feats, rows = plan.parts, plan.feats, plan.rows
    me = spot.me
    barrier = pltpu.get_barrier_semaphore()

    def greet(k, carry):
        pl.semaphore_signal(barrier, inc=1, device_id={"mp": lax.rem(me + k, parts)}, device_id_type=MESH)
        return carry

    lax.fori_loop(1, parts, greet, 0)
    pl.semaphore_signal(barrier, inc=1, device_id=spot.y_mate(), device_id_type=MESH)

    base = 0
    gathers = []
    for l in range(LAYERS):
        gathers.append(Gather(spot, lines, base, win_own.at[l], wout_own.at[l], win.at[l], wout.at[l]))
        base += GATHER_LINES
    reduces = []
    for l in range(LAYERS):
        reduces.append(
            Reduce(
                spot, lines, base, din.at[l], dout.at[l], xin.at[l], yout.at[l], yin.at[l], xout.at[l], zin.at[l],
                weights_out.at[l],
            )
        )
        base += REDUCE_LINES
    bias_base = base
    base += 8
    mate_base = base
    base += 8
    vec_base = base
    base += 5

    def copy_to(k, src, dst, lane):
        q = lax.rem(me + k, parts)
        return pltpu.make_async_remote_copy(
            src_ref=src.at[q],
            dst_ref=dst.at[me],
            send_sem=mix_sems.at[lane, q],
            recv_sem=mix_sems.at[lane + 1, me],
            device_id={"mp": q},
            device_id_type=MESH,
        )

    def copy_from(k, src, dst, lane):
        p = lax.rem(me + k, parts)
        return pltpu.make_async_remote_copy(
            src_ref=src.at[p],
            dst_ref=dst.at[p],
            send_sem=mix_sems.at[lane, p],
            recv_sem=mix_sems.at[lane + 1, p],
            device_id={"mp": p},
            device_id_type=MESH,
        )

    def each(action):
        def body(k, carry):
            action(k)
            return carry

        lax.fori_loop(1, parts, body, 0)

    def mix_enter(value):
        send[...] = dot_t(packed[...], value).astype(BF16).reshape(parts, feats, rows)

    def mix_go():
        each(lambda k: copy_to(k, send, recv, 0).start())
        recv[me] = send[me]

    def mix_middle():
        each(lambda k: copy_from(k, send, recv, 0).wait_recv())
        position_dft(plan, me, recv, work, send_back, turn, wave)
        each(lambda k: copy_to(k, send_back, recv_back, 2).start())
        recv_back[me] = send_back[me]

    def mix_leave():
        each(lambda k: copy_from(k, send_back, recv_back, 2).wait_recv())
        mixed = t_dot(recv_back[...].reshape(parts * feats, rows), rebuild[...])
        each(lambda k: copy_to(k, send, recv, 0).wait_send())
        each(lambda k: copy_to(k, send_back, recv_back, 2).wait_send())
        return mixed * (1.0 / math.sqrt(L * D))

    group = 2 * FF // parts
    eye = (
        lax.broadcasted_iota(jnp.int32, (FF // parts, 256), 0) == lax.broadcasted_iota(jnp.int32, (FF // parts, 256), 1)
    ).astype(BF16)

    def bias_column(l, zk):
        return jnp.concatenate([dot_t(eye, bias_all[zk, x])[:, l : l + 1] for x in (0, 1)], axis=0)

    def forward(l, current, mixed, per_group):
        summed = current + mixed
        unit, scale = normalize(summed)
        unit_mix[l] = unit
        scale_mix[l] = scale
        normed = unit * vec[l, 0:1] + vec[l, 1:2]
        normed_keep[...] = normed
        hidden[l, 0] = normed.astype(BF16)
        lines.send(mate_base + 4 * l, hidden.at[l, 0], hidden.at[l, 1], spot.core_mate())
        for k in range(4):
            per_group(k)
            zk = spot.z ^ k
            weights = win[l, zk].reshape(group, D)
            column = bias_column(l, zk)
            for slot in (0, 1):
                if k == 0 and slot == 1:
                    lines.wait(mate_base + 4 * l, hidden.at[l, 1], spot.core_mate())
                value, slope = gelu_pair(dot_t(weights, hidden[l, slot]) + column)
                acts[l, zk, :, slot * rows : (slot + 1) * rows] = value.astype(BF16)
                slopes[l, zk, :, slot * rows : (slot + 1) * rows] = slope.astype(BF16)
        outs = wout[l].reshape(FF // 2, D)
        branch_send[0] = t_dot(acts[l, :, :, rows : 2 * rows].reshape(FF // 2, rows), outs).astype(BF16)
        lines.send(mate_base + 4 * l + 1, branch_send.at[0], branch_recv.at[0], spot.core_mate())
        branch = t_dot(acts[l, :, :, 0:rows].reshape(FF // 2, rows), outs)
        lines.wait(mate_base + 4 * l + 1, branch_recv.at[0], spot.core_mate())
        total = normed_keep[...] + branch + branch_recv[0].astype(F32) + vec[l, 2:3]
        unit, scale = normalize(total)
        unit_out[l] = unit
        scale_out[l] = scale
        lines.copy(mate_base + 4 * l + 1, branch_send.at[0], branch_recv.at[0], spot.core_mate()).wait_send()
        lines.sent.pop()
        return unit * vec[l, 3:4] + vec[l, 4:5]

    def vec_put(l, i, value):
        vec_send[0, 2 + i : 3 + i, l * D : (l + 1) * D] = value

    def weight_grads(l):
        both = grad_branch[l].reshape(2 * rows, D)
        source = hidden[l].reshape(2 * rows, D)
        for k in range(4):
            zk = spot.z ^ k
            din[l, zk] = jnp.dot(grad_pre[zk], source, preferred_element_type=F32).astype(BF16).reshape(2, 2, -1, D)
            reduces[l].first_in(k)
            dout[l, zk] = jnp.dot(acts[l, zk], both, preferred_element_type=F32).astype(BF16).reshape(2, 2, -1, D)
            reduces[l].first_out(k)
        ones = jnp.ones((16, 2 * rows), BF16)
        vec_send[0, l : l + 1, :] = dot_t(ones, grad_pre[...].reshape(FF // 2, 2 * rows))[0:1]

    def backward(l, grad, meanwhile):
        grad_total, gain_grad, shift_grad = normalize_back(grad, vec[l, 3:4], unit_out[l], scale_out[l])
        low = grad_total.astype(BF16)
        grad_branch[l, 0] = low
        lines.send(mate_base + 4 * l + 2, grad_branch.at[l, 0], grad_branch.at[l, 1], spot.core_mate())
        normed_keep[...] = grad_total
        vec_put(l, 2, jnp.sum(low.astype(F32), axis=0, keepdims=True))
        vec_put(l, 3, gain_grad)
        vec_put(l, 4, shift_grad)
        for slot in (0, 1):
            if slot == 1:
                lines.wait(mate_base + 4 * l + 2, grad_branch.at[l, 1], spot.core_mate())
            for zk in range(4):
                grad_act = dot_t(wout[l, zk].reshape(group, D), grad_branch[l, slot])
                span = slice(slot * rows, (slot + 1) * rows)
                grad_pre[zk, :, span] = (grad_act * slopes[l, zk, :, span].astype(F32)).astype(BF16)
        meanwhile()
        ins = win[l].reshape(FF // 2, D)
        branch_send[1] = t_dot(grad_pre[:, :, rows : 2 * rows].reshape(FF // 2, rows), ins).astype(BF16)
        lines.send(mate_base + 4 * l + 3, branch_send.at[1], branch_recv.at[1], spot.core_mate())
        grad_normed = t_dot(grad_pre[:, :, 0:rows].reshape(FF // 2, rows), ins)
        lines.wait(mate_base + 4 * l + 3, branch_recv.at[1], spot.core_mate())
        grad_normed = normed_keep[...] + grad_normed + branch_recv[1].astype(F32)
        lines.copy(mate_base + 4 * l + 3, branch_send.at[1], branch_recv.at[1], spot.core_mate()).wait_send()
        lines.sent.pop()
        grad_summed, gain_grad, shift_grad = normalize_back(grad_normed, vec[l, 0:1], unit_mix[l], scale_mix[l])
        vec_put(l, 0, gain_grad)
        vec_put(l, 1, shift_grad)
        return grad_summed

    mix_enter(tokens[...])
    vec_send[0] = jnp.zeros_like(vec_send[0])
    pl.semaphore_wait(barrier, parts)
    mix_go()
    gathers[0].start()
    for j in range(1, 8):
        other = spot.own ^ j
        lines.send(
            bias_base + j, bias_own, bias_all.at[spot.z, spot.x],
            {"dp": spot.y, "mp": other * 2 + spot.core},
        )
    bias_all[spot.z, spot.x] = bias_own[...]
    mix_middle()
    for k in (1, 2, 3):
        gathers[0].second(k)
    gathers[1].start()
    for k in range(4):
        gathers[0].third(k)
    for j in range(1, 8):
        other = spot.own ^ j
        lines.wait(bias_base + j, bias_all.at[other // 2, other % 2], {"dp": spot.y, "mp": other * 2 + spot.core})
    mixed = mix_leave()
    current = forward(0, tokens[...].astype(F32), mixed, lambda k: gathers[0].finish(k))
    mix_enter(current.astype(BF16))
    mix_go()
    for k in (1, 2, 3):
        gathers[1].second(k)
    for k in range(4):
        gathers[1].third(k)
    grad_out[...] = current
    mix_middle()
    mixed = mix_leave()
    current = forward(1, grad_out[...], mixed, lambda k: gathers[1].finish(k))
    act_out[...] = current.astype(BF16)

    grad = backward(1, cotangent[...].astype(F32), lambda: None)
    grad_out[...] = grad
    mix_enter(grad.astype(BF16))
    mix_go()
    weight_grads(1)
    mix_middle()
    for k in (1, 2, 3, 0):
        reduces[1].second(k)
    mixed = mix_leave()
    grad = backward(0, grad_out[...] + mixed, lambda: weight_grads(0))
    grad_out[...] = grad
    mix_enter(grad.astype(BF16))
    mix_go()
    for k in (1, 2, 3, 0):
        reduces[1].third(k)
    for k in (1, 2, 3, 0):
        reduces[0].second(k)
    mix_middle()
    reduces[1].fourth()

    mates = [spot.at(core=1 - spot.core), spot.x_mate(), spot.z_mate(1), spot.z_mate(2), spot.y_mate()]
    for i, mate in enumerate(mates):
        lines.send(vec_base + i, vec_send.at[i], vec_recv.at[i], mate)
        lines.wait(vec_base + i, vec_recv.at[i], mate)
        more = vec_recv[i]
        if i == 0:
            more = jnp.where(lax.broadcasted_iota(jnp.int32, more.shape, 0) < LAYERS, 0.0, more)
        vec_send[i + 1] = vec_send[i] + more
    for k in (1, 2, 3, 0):
        reduces[0].third(k)
    mixed = mix_leave()
    grad_out[...] = grad_out[...] + mixed
    reduces[0].fourth()
    reduces[1].finish()
    reduces[0].finish()
    totals = vec_send[5]
    vec_out[...] = totals

    row = lax.broadcasted_iota(jnp.int32, totals.shape, 0)
    lane = lax.broadcasted_iota(jnp.int32, totals.shape, 1)
    own_bias = (row < LAYERS) & (lane // (FF // parts) == spot.own)
    squares = totals * totals
    local = jnp.sum(jnp.where(own_bias, squares, 0.0), axis=(0, 1), keepdims=True)
    for l in range(LAYERS):
        for i in (0, 1):
            value = weights_out[l, i].reshape(FF // parts, D).astype(F32)
            local = local + jnp.sum(value * value, axis=(0, 1), keepdims=True)
    square_send[...] = jnp.broadcast_to(local, square_send.shape)

    def square_to(k):
        q = lax.rem(me + k, parts)
        return pltpu.make_async_remote_copy(
            src_ref=square_send, dst_ref=square_recv.at[me], send_sem=mix_sems.at[4, q], recv_sem=mix_sems.at[5, me],
            device_id={"mp": q}, device_id_type=MESH,
        )

    def square_from(k):
        p = lax.rem(me + k, parts)
        return pltpu.make_async_remote_copy(
            src_ref=square_send, dst_ref=square_recv.at[p], send_sem=mix_sems.at[4, p], recv_sem=mix_sems.at[5, p],
            device_id={"mp": p}, device_id_type=MESH,
        )

    each(lambda k: square_to(k).start())
    square_recv[me] = square_send[...]
    each(lambda k: square_from(k).wait_recv())
    vec_squares = jnp.sum(jnp.where(row >= LAYERS, squares, 0.0), axis=(0, 1), keepdims=True)
    square_out[...] = jnp.sum(square_recv[...], axis=0) + vec_squares
    each(lambda k: square_to(k).wait_send())
    lines.drain()


def fused(plan, tokens, cotangent, win_own, wout_own, bias_own, vec):
    parts, feats, rows = plan.parts, plan.feats, plan.rows
    block = (parts, feats, rows)
    hid = FF // parts
    half = hid // 2
    group = 2 * hid
    vm = pltpu.VMEM
    line_count = LAYERS * (GATHER_LINES + REDUCE_LINES) + 8 + 8 + 5
    return pl.pallas_call(
        functools.partial(fused_kernel, plan),
        out_shape=(
            jax.ShapeDtypeStruct((rows, D), BF16),
            jax.ShapeDtypeStruct((rows, D), F32),
            jax.ShapeDtypeStruct((LAYERS, 2, 2, half, D), BF16),
            jax.ShapeDtypeStruct((8, FF // 2), F32),
            jax.ShapeDtypeStruct((8, 128), F32),
        ),
        in_specs=[pl.BlockSpec(memory_space=vm)] * 10,
        out_specs=[pl.BlockSpec(memory_space=vm)] * 5,
        scratch_shapes=[
            vm((LAYERS, 4, 2, 2, half, D), BF16),
            vm((LAYERS, 4, 2, 2, half, D), BF16),
            vm((4, 2, 16, 256), BF16),
            vm((LAYERS, 2, rows, D), BF16),
            vm((LAYERS, 4, group, 2 * rows), BF16),
            vm((LAYERS, 4, group, 2 * rows), BF16),
            vm((LAYERS, rows, D), F32),
            vm((LAYERS, rows, D), F32),
            vm((LAYERS, rows, 1), F32),
            vm((LAYERS, rows, 1), F32),
            vm((rows, D), F32),
            vm((2, rows, D), BF16),
            vm((2, rows, D), BF16),
            vm((LAYERS, 2, rows, D), BF16),
            vm((4, group, 2 * rows), BF16),
            vm((LAYERS, 4, 2, 2, half, D), BF16),
            vm((LAYERS, 4, 2, 2, half, D), BF16),
            vm((LAYERS, 4, 2, half, D), BF16),
            vm((LAYERS, 4, 2, half, D), BF16),
            vm((LAYERS, 4, half, D), BF16),
            vm((LAYERS, 4, half, D), BF16),
            vm((LAYERS, 3, 2, half, D), BF16),
            vm(block, BF16),
            vm(block, BF16),
            vm((parts, feats, 2 * rows), BF16),
            vm(block, BF16),
            vm(block, BF16),
            vm((6, 8, FF // 2), F32),
            vm((5, 8, FF // 2), F32),
            vm((8, 128), F32),
            vm((parts, 8, 128), F32),
            pltpu.SemaphoreType.DMA((6, parts)),
            pltpu.SemaphoreType.DMA((line_count,)),
            pltpu.SemaphoreType.DMA((line_count,)),
        ],
        compiler_params=pltpu.CompilerParams(collective_id=1, has_side_effects=True, vmem_limit_bytes=62 * 2**20),
    )(tokens, cotangent, win_own, wout_own, bias_own, vec, plan.packed, plan.rebuild, plan.turn, plan.wave)


def on_block(
    tokens, cotangent, weight_in, bias_in, weight_out, vectors, moment_in, square_in,
    moment_bias, square_bias, moment_out, square_out, moment_vec, square_vec,
):
    rows = tokens.shape[0]
    plan = Plan(L // rows)
    hid = FF // plan.parts

    def localize(value):
        return jnp.swapaxes(value.reshape(plan.inner, plan.parts, D), 0, 1).reshape(rows, D)

    def restore(value):
        return jnp.swapaxes(value.reshape(plan.parts, plan.inner, D), 0, 1).reshape(rows, 1, D)

    win_own = jnp.swapaxes(weight_in.astype(BF16), 1, 2).reshape(LAYERS, 2, hid // 2, D)
    wout_own = weight_out.astype(BF16).reshape(LAYERS, 2, hid // 2, D)
    bias_own = jnp.pad(bias_in.astype(BF16), ((0, 16 - LAYERS), (0, 256 - hid)))
    acts, grad, weights, sums, squares = fused(
        plan, localize(tokens), localize(cotangent), win_own, wout_own, bias_own, vectors
    )
    grad_norm = jnp.sqrt(squares[0, 0])
    factor = jnp.minimum(1.0, CLIP / grad_norm)
    weights = weights.reshape(LAYERS, 2, hid, D).astype(F32)
    sum_in = jnp.swapaxes(weights[:, 0], 1, 2)
    sum_out = weights[:, 1]
    sum_bias = lax.dynamic_slice(sums, (0, lax.axis_index("mp") // 2 * hid), (LAYERS, hid))
    sum_vec = jnp.swapaxes(sums[2:7].reshape(5, LAYERS, D), 0, 1)
    m_in, v_in, w_in = adamw(weight_in, sum_in * factor, moment_in, square_in, 1.0 / math.sqrt(D), DECAY)
    m_out, v_out, w_out = adamw(weight_out, sum_out * factor, moment_out, square_out, 1.0 / math.sqrt(FF), DECAY)
    m_bias, v_bias, b_new = adamw(bias_in, sum_bias * factor, moment_bias, square_bias, 0.5, 0.0)
    m_vec, v_vec, vec_new = adamw(vectors, sum_vec * factor, moment_vec, square_vec, 0.5, 0.0)
    return (
        restore(acts),
        restore(grad),
        grad_norm,
        m_in,
        v_in,
        w_in,
        w_in.astype(BF16),
        m_out,
        v_out,
        w_out,
        w_out.astype(BF16),
        m_bias,
        v_bias,
        b_new,
        m_vec,
        v_vec,
        vec_new,
    )


def matmul(left_op, right_op):
    return jnp.dot(left_op, right_op, preferred_element_type=jnp.float32)


def inner_rows(left_op, right_op):
    return lax.dot_general(
        left_op, right_op, (((0,), (0,)), ((), ())), preferred_element_type=jnp.float32
    )


def inner_cols(left_op, right_op):
    return lax.dot_general(
        left_op, right_op, (((1,), (1,)), ((), ())), preferred_element_type=jnp.float32
    )


def layer_norm(value, gain, shift):
    centre = value - jnp.mean(value, axis=-1, keepdims=True)
    spread = jnp.mean(centre * centre, axis=-1, keepdims=True)
    return centre * lax.rsqrt(spread + EPS_NORM) * gain + shift


def adamw(weight, grad, moment, square, rate, decay):
    new_moment = BETA_ONE * moment + (1.0 - BETA_ONE) * grad
    new_square = BETA_TWO * square + (1.0 - BETA_TWO) * grad * grad
    moment_hat = new_moment / (1.0 - BETA_ONE**STEP)
    square_hat = new_square / (1.0 - BETA_TWO**STEP)
    new_weight = weight - rate * (moment_hat / (jnp.sqrt(square_hat) + EPS_ADAM) + decay * weight)
    return (new_moment, new_square, new_weight)


def on_device(
    tokens,
    cotangent,
    weight_in,
    bias_in,
    weight_out,
    vectors,
    moment_in,
    square_in,
    moment_bias,
    square_bias,
    moment_out,
    square_out,
    moment_vec,
    square_vec,
):
    row_count, seq_count, feat_count = tokens.shape
    plan = Plan(L // row_count)

    def localize(value):
        return jnp.swapaxes(value.reshape(plan.inner, plan.parts, -1), 0, 1).reshape(value.shape)

    def restore(value):
        return jnp.swapaxes(value.reshape(plan.parts, plan.inner, -1), 0, 1).reshape(value.shape)

    current = localize(tokens).astype(jnp.float32)
    saved = []
    for layer_at in range(LAYERS):
        vector_set = vectors[layer_at]
        rounded = current.astype(jnp.bfloat16)
        mixed = mix(plan, rounded.reshape(row_count, feat_count)).reshape(row_count, seq_count, feat_count)
        summed = current + mixed
        normed = layer_norm(summed, vector_set[0], vector_set[1])
        hidden_in = normed.astype(jnp.bfloat16)
        weight_one = weight_in[layer_at].astype(jnp.bfloat16)
        weight_two = weight_out[layer_at].astype(jnp.bfloat16)
        bias_one = bias_in[layer_at].astype(jnp.bfloat16)
        whole_one, whole_two, whole_bias = (
            lax.all_gather(weight_one, "mp", axis=1, tiled=True),
            lax.all_gather(weight_two, "mp", axis=0, tiled=True),
            lax.all_gather(bias_one, "mp", axis=0, tiled=True),
        )
        inputs = hidden_in.reshape(-1, feat_count)
        pre_act = matmul(inputs, whole_one) + whole_bias.astype(jnp.float32)
        acts = jax.nn.gelu(pre_act).astype(jnp.bfloat16)
        branch = matmul(acts, whole_two).reshape(row_count, seq_count, feat_count)
        held = (inputs, whole_one, whole_two)
        total = normed + branch + vector_set[2]
        current = layer_norm(total, vector_set[3], vector_set[4])
        saved.append((summed, total, pre_act, acts, held))
    activations = restore(current.astype(jnp.bfloat16))
    grad = localize(cotangent).astype(jnp.float32)
    layer_grads = [None] * LAYERS
    for layer_at in reversed(range(LAYERS)):
        vector_set = vectors[layer_at]
        summed, total, pre_act, acts, held = saved[layer_at]
        inputs, mat_one, mat_two = held
        _, pull_out = jax.vjp(layer_norm, total, vector_set[3], vector_set[4])
        grad_total, gain_two, shift_two = pull_out(grad)
        grad_branch = grad_total.astype(jnp.bfloat16)
        grad_bias_two = jnp.sum(grad_branch.astype(jnp.float32), axis=(0, 1))
        flat_grad = grad_branch.reshape(-1, feat_count)
        grad_act = inner_cols(flat_grad, mat_two)
        _, pull_gelu = jax.vjp(jax.nn.gelu, pre_act)
        grad_pre = pull_gelu(grad_act)[0].astype(jnp.bfloat16)
        full_one = inner_rows(inputs, grad_pre)
        full_two = inner_rows(acts, flat_grad)
        full_bias = jnp.sum(grad_pre.astype(jnp.float32), axis=0)
        grad_one, grad_two, grad_bias_one = (
            lax.psum_scatter(
                full_one.astype(jnp.bfloat16), "mp", scatter_dimension=1, tiled=True
            ).astype(jnp.float32),
            lax.psum_scatter(
                full_two.astype(jnp.bfloat16), "mp", scatter_dimension=0, tiled=True
            ).astype(jnp.float32),
            lax.psum_scatter(
                full_bias.astype(jnp.bfloat16), "mp", scatter_dimension=0, tiled=True
            ).astype(jnp.float32),
        )
        grad_normed = inner_cols(grad_pre, mat_one).reshape(row_count, seq_count, feat_count)
        grad_normed = grad_normed + grad_total
        _, pull_in = jax.vjp(layer_norm, summed, vector_set[0], vector_set[1])
        grad_summed, gain_one, shift_one = pull_in(grad_normed)
        mix_grad = grad_summed.astype(jnp.bfloat16).reshape(-1, feat_count)
        grad_mix = mix(plan, mix_grad).reshape(row_count, seq_count, feat_count)
        grad = grad_summed + grad_mix
        layer_grads[layer_at] = (
            grad_one,
            grad_two,
            grad_bias_one,
            jnp.stack([gain_one, shift_one, grad_bias_two, gain_two, shift_two]),
        )
    stack_in = jnp.stack([entry[0] for entry in layer_grads])
    stack_out = jnp.stack([entry[1] for entry in layer_grads])
    stack_bias = jnp.stack([entry[2] for entry in layer_grads])
    stack_vec = jnp.stack([entry[3] for entry in layer_grads])
    sum_in, sum_out, sum_bias, sum_vec = (
        lax.psum(stack_in.astype(jnp.bfloat16), "dp").astype(jnp.float32),
        lax.psum(stack_out.astype(jnp.bfloat16), "dp").astype(jnp.float32),
        lax.psum(stack_bias.astype(jnp.bfloat16), "dp").astype(jnp.float32),
        lax.psum(stack_vec.astype(jnp.bfloat16), "dp").astype(jnp.float32),
    )
    local_squares = (
        jnp.sum(sum_in * sum_in) + jnp.sum(sum_out * sum_out) + jnp.sum(sum_bias * sum_bias)
    )
    sum_vec, total_squares = lax.psum((sum_vec, local_squares), "mp")
    grad_norm = jnp.sqrt(total_squares + jnp.sum(sum_vec * sum_vec))
    factor = jnp.minimum(1.0, CLIP / grad_norm)
    m_in, v_in, w_in = adamw(
        weight_in, sum_in * factor, moment_in, square_in, 1.0 / math.sqrt(D), DECAY
    )
    m_out, v_out, w_out = adamw(
        weight_out, sum_out * factor, moment_out, square_out, 1.0 / math.sqrt(FF), DECAY
    )
    m_bias, v_bias, b_new = adamw(bias_in, sum_bias * factor, moment_bias, square_bias, 0.5, 0.0)
    m_vec, v_vec, vec_new = adamw(vectors, sum_vec * factor, moment_vec, square_vec, 0.5, 0.0)
    return (
        activations,
        restore(grad),
        grad_norm,
        m_in,
        v_in,
        w_in,
        w_in.astype(jnp.bfloat16),
        m_out,
        v_out,
        w_out,
        w_out.astype(jnp.bfloat16),
        m_bias,
        v_bias,
        b_new,
        m_vec,
        v_vec,
        vec_new,
    )


def solution(mesh):
    body = on_block if (mesh.shape["dp"], mesh.shape["mp"]) == (2, 16) else on_device
    return jax.shard_map(
        body,
        mesh=mesh,
        in_specs=(
            P("mp", "dp", None),
            P("mp", "dp", None),
            P(None, None, "mp"),
            P(None, "mp"),
            P(None, "mp", None),
            P(),
            P(None, None, "mp"),
            P(None, None, "mp"),
            P(None, "mp"),
            P(None, "mp"),
            P(None, "mp", None),
            P(None, "mp", None),
            P(),
            P(),
        ),
        out_specs=(
            P("mp", "dp", None),
            P("mp", "dp", None),
            P(),
            P(None, None, "mp"),
            P(None, None, "mp"),
            P(None, None, "mp"),
            P(None, None, "mp"),
            P(None, "mp", None),
            P(None, "mp", None),
            P(None, "mp", None),
            P(None, "mp", None),
            P(None, "mp"),
            P(None, "mp"),
            P(None, "mp"),
            P(),
            P(),
            P(),
        ),
        check_vma=False,
    )
```

```python
import functools
import math

import jax
import jax.numpy as jnp
import ml_dtypes
import numpy as np
from jax import lax
from jax.experimental import pallas as pl
from jax.experimental.pallas import tpu as pltpu
from jax.sharding import PartitionSpec as P

D = 768
FF = 3072
L = 4096
LAYERS = 2
STEP = 5


CLIP = 1.0
BETA_ONE = 0.5
BETA_TWO = 0.5
EPS_ADAM = 1e-08
EPS_NORM = 1e-05
DECAY = 0.01
MESH = pl.DeviceIdType.MESH
F32 = jnp.float32
BF16 = jnp.bfloat16


class Plan:
    def __init__(self, parts):
        self.parts = parts
        self.rows = L // parts
        self.inner = self.rows // parts
        self.pairs = D // 2 // parts
        self.feats = -(-2 * self.pairs // 16) * 16
        rows, inner = self.rows, self.inner
        lane = np.arange(rows)
        self.place = parts * (lane % inner) + lane // inner
        packed = np.zeros((parts, self.feats, D))
        rebuild = np.zeros((parts, self.feats, D))
        n = np.arange(D)
        for at in range(parts):
            for i in range(self.pairs):
                m = self.pairs * at + i
                a, b = i, self.pairs + i
                packed[at, a] = np.cos(2 * np.pi * (m * n % D) / D)
                rebuild[at, a, m] = 1.0
                if m == 0:
                    packed[at, b] = np.cos(2 * np.pi * (D // 2 * n % D) / D)
                    rebuild[at, b, D // 2] = 1.0
                else:
                    packed[at, b] = np.sin(2 * np.pi * (m * n % D) / D)
                    rebuild[at, a, D - m] = 1.0
                    rebuild[at, b, m] = -1.0
                    rebuild[at, b, D - m] = 1.0
        bf = ml_dtypes.bfloat16
        self.packed = packed.reshape(-1, D).astype(bf)
        self.rebuild = rebuild.reshape(-1, D).astype(bf)
        turn = 2 * np.pi * (np.arange(parts)[:, None] * self.place[None, :] % L) / L
        self.turn = np.stack([np.cos(turn), np.sin(turn)]).astype(np.float32)
        angle = 2 * np.pi * (self.place[:, None] * np.arange(rows)[None, :] % rows) / rows
        self.wave = np.concatenate([np.cos(angle), np.sin(angle)]).astype(bf)


def half_dft(values):
    n = len(values)
    if n == 1:
        return [(values[0], None)]
    if n == 2:
        return [(values[0] + values[1], None), (values[0] - values[1], None)]
    even, odd = half_dft(values[0::2]), half_dft(values[1::2])
    half = n // 2
    result = [None] * (half + 1)
    for k in range(half // 2 + 1):
        er, ei = even[k]
        orr, oi = odd[k]
        if k == 0:
            result[0] = (er + orr, None)
            result[half] = (er - orr, None)
        elif 2 * k == half:
            result[k] = (er, -orr)
        else:
            c, s = math.cos(2 * math.pi * k / n), math.sin(2 * math.pi * k / n)
            tr, ti = orr * c + oi * s, oi * c - orr * s
            result[k] = (er + tr, ei + ti)
            result[half - k] = (er - tr, ti - ei)
    return result


def position_dft(plan, me, recv, work, send, turn_ref, wave_ref):
    parts, feats, rows, inner, pairs = plan.parts, plan.feats, plan.rows, plan.inner, plan.pairs
    chunk = 16
    lanes = min(rows, 128)
    for lane_at in range(0, rows, lanes):

        def body(i, carry):
            at = pl.multiple_of(i * chunk, chunk)
            values = [recv[p, pl.ds(at, chunk), lane_at : lane_at + lanes].astype(F32) for p in range(parts)]
            outs = half_dft(values)
            row = at + lax.broadcasted_iota(jnp.int32, (chunk, lanes), 0)
            is_sine = (row >= pairs) & jnp.logical_not((row == pairs) & (me == 0))
            for d in range(parts):
                re, im = outs[min(d, parts - d)]
                im = jnp.zeros_like(re) if im is None else im
                if d > parts - d:
                    im = -im
                re, im = jnp.where(is_sine, -im, re), jnp.where(is_sine, re, im)
                c = turn_ref[0, d : d + 1, lane_at : lane_at + lanes]
                s = turn_ref[1, d : d + 1, lane_at : lane_at + lanes]
                work[d, pl.ds(at, chunk), lane_at : lane_at + lanes] = (re * c + im * s).astype(BF16)
                work[d, pl.ds(at, chunk), rows + lane_at : rows + lane_at + lanes] = (im * c - re * s).astype(BF16)
            return carry

        lax.fori_loop(0, feats // chunk, body, 0)

    def swap(i, carry):
        at = pl.multiple_of(i * chunk, chunk)
        outs = [
            jnp.dot(work[d, pl.ds(at, chunk), :], wave_ref[...], preferred_element_type=F32)
            for d in range(parts)
        ]
        group = lax.broadcasted_iota(jnp.int32, (chunk, rows), 1) // inner
        bit = 1
        while bit < parts:
            upper = (group // bit) % 2 == 1
            for d in range(parts):
                if d & bit:
                    continue
                low, high = outs[d], outs[d | bit]
                shift = inner * bit
                outs[d] = jnp.where(upper, pltpu.roll(high, shift, 1), low)
                outs[d | bit] = jnp.where(upper, high, pltpu.roll(low, rows - shift, 1))
            bit *= 2
        for q in range(parts):
            send[q, pl.ds(at, chunk), :] = outs[q].astype(BF16)
        return carry

    lax.fori_loop(0, feats // chunk, swap, 0)


def exchange(plan, me, send, recv, send_sem, recv_sem):
    parts = plan.parts

    def copy_to(k):
        q = lax.rem(me + k, parts)
        return pltpu.make_async_remote_copy(
            src_ref=send.at[q],
            dst_ref=recv.at[me],
            send_sem=send_sem.at[q],
            recv_sem=recv_sem.at[me],
            device_id={"mp": q},
            device_id_type=MESH,
        )

    def copy_from(k):
        p = lax.rem(me + k, parts)
        return pltpu.make_async_remote_copy(
            src_ref=send.at[p],
            dst_ref=recv.at[p],
            send_sem=send_sem.at[p],
            recv_sem=recv_sem.at[p],
            device_id={"mp": p},
            device_id_type=MESH,
        )

    def start(k, carry):
        copy_to(k).start()
        return carry

    def finish(k, carry):
        copy_from(k).wait_recv()
        return carry

    def drain(k, carry):
        copy_to(k).wait_send()
        return carry

    lax.fori_loop(1, parts, start, 0)
    recv[me] = send[me]
    lax.fori_loop(1, parts, finish, 0)
    lax.fori_loop(1, parts, drain, 0)


def mix_kernel(plan, x_ref, packed_ref, rebuild_ref, turn_ref, wave_ref, out_ref, send, recv, work, send_back, recv_back, sems):
    me = lax.axis_index("mp")
    parts, feats, rows = plan.parts, plan.feats, plan.rows
    barrier = pltpu.get_barrier_semaphore()

    def greet(k, carry):
        pl.semaphore_signal(barrier, inc=1, device_id={"mp": lax.rem(me + k, parts)}, device_id_type=MESH)
        return carry

    lax.fori_loop(1, parts, greet, 0)
    pl.semaphore_wait(barrier, parts - 1)

    columns = lax.dot_general(packed_ref[...], x_ref[...], (((1,), (1,)), ((), ())), preferred_element_type=F32)
    send[...] = columns.astype(BF16).reshape(parts, feats, rows)
    exchange(plan, me, send, recv, sems.at[0], sems.at[1])
    position_dft(plan, me, recv, work, send_back, turn_ref, wave_ref)
    exchange(plan, me, send_back, recv_back, sems.at[2], sems.at[3])
    mixed = lax.dot_general(
        recv_back[...].reshape(parts * feats, rows), rebuild_ref[...], (((0,), (0,)), ((), ())), preferred_element_type=F32
    )
    out_ref[...] = mixed * (1.0 / math.sqrt(L * D))


def mix(plan, value):
    block = (plan.parts, plan.feats, plan.rows)
    return pl.pallas_call(
        functools.partial(mix_kernel, plan),
        out_shape=jax.ShapeDtypeStruct((plan.rows, D), F32),
        in_specs=[pl.BlockSpec(memory_space=pltpu.VMEM)] * 5,
        out_specs=pl.BlockSpec(memory_space=pltpu.VMEM),
        scratch_shapes=[
            pltpu.VMEM(block, BF16),
            pltpu.VMEM(block, BF16),
            pltpu.VMEM((plan.parts, plan.feats, 2 * plan.rows), BF16),
            pltpu.VMEM(block, BF16),
            pltpu.VMEM(block, BF16),
            pltpu.SemaphoreType.DMA((4, plan.parts)),
        ],
        compiler_params=pltpu.CompilerParams(
            collective_id=0, has_side_effects=True, vmem_limit_bytes=40 * 2**20
        ),
    )(value, plan.packed, plan.rebuild, plan.turn, plan.wave)


class Spot:
    def __init__(self):
        self.y = lax.axis_index("dp")
        self.me = lax.axis_index("mp")
        self.z, self.x, self.core = self.me // 4, (self.me // 2) % 2, self.me % 2
        self.own = self.me // 2
        self.inner = (self.z == 1) | (self.z == 2)

    def at(self, y=None, z=None, x=None, core=None):
        y = self.y if y is None else y
        z = self.z if z is None else z
        x = self.x if x is None else x
        core = self.core if core is None else core
        return {"dp": y, "mp": z * 4 + x * 2 + core}

    def y_mate(self):
        return self.at(y=1 - self.y)

    def x_mate(self):
        return self.at(x=1 - self.x)

    def core_mate(self):
        return self.at(core=1 - self.core)

    def z_mate(self, k):
        return self.at(z=self.z ^ k)


class Lines:
    def __init__(self, send_sems, recv_sems):
        self.send_sems, self.recv_sems = send_sems, recv_sems
        self.next = 0
        self.sent = []

    def copy(self, sender, number, src, dst, device):
        return pltpu.make_async_remote_copy(
            src_ref=src,
            dst_ref=dst,
            send_sem=self.send_sems.at[sender],
            recv_sem=self.recv_sems.at[number],
            device_id=device,
            device_id_type=MESH,
        )

    def send(self, number, src, dst, device, sender=None, like=None, when=None, keep=True):
        if sender is None:
            sender = self.next
            self.next += 1
        self.copy(sender, number, src, dst, device).start()
        if keep:
            self.sent.append((sender, src if like is None else like, when))
        return sender

    def wait(self, number, land, device):
        self.copy(0, number, land, land, device).wait_recv()

    def wait_sent(self, sender, src, device):
        self.copy(sender, 0, src, src, device).wait_send()

    def drain(self, device):
        for sender, src, when in self.sent:
            if when is None:
                self.wait_sent(sender, src, device)
            else:
                pl.when(when)(functools.partial(self.wait_sent, sender, src, device))
        self.sent = []


class Gather:
    split = (3,)

    def __init__(self, spot, lines, base, win, wout):
        self.spot, self.lines, self.base = spot, lines, base
        self.win, self.wout = win, wout
        self.like = win.at[0, 0, 0]
        self.senders = {}

    def along_z(self, block, hop, number):
        s, n, b = self.spot, self.lines, self.base
        zk = s.z ^ block
        for i, part in ((0, self.win), (1, self.wout)):
            ref = part.at[zk, s.x, s.y]
            when = None if block == 0 and hop == 1 else s.inner
            n.send(b + 2 * number - 2 + i, ref, ref, s.z_mate(hop), like=self.like, when=when)

    def start_z(self):
        self.along_z(0, 1, 1)
        pl.when(self.spot.inner)(lambda: self.along_z(0, 3, 3))

    def start_x(self):
        s, n, b = self.spot, self.lines, self.base
        own = self.wout.at[s.z, s.x, s.y]
        n.send(b + 9, own, own, s.x_mate())
        own = self.win.at[s.z, s.x]
        n.send(b + 13, own, own, s.x_mate())

    def arrive(self, k):
        s, n, b = self.spot, self.lines, self.base
        zk = s.z ^ k
        a, c = self.win.at[zk, s.x, s.y], self.wout.at[zk, s.x, s.y]
        n.wait(b + 2 * k - 2, a, s.z_mate(k))
        n.wait(b + 2 * k - 1, c, s.z_mate(k))
        hop, number = {1: (3, 2), 3: (1, 2), 2: (1, 3)}[k]
        return lambda: self.along_z(k, hop, number)

    def second(self, k):
        s, n, b = self.spot, self.lines, self.base
        zk = s.z ^ k
        a, c = self.win.at[zk, s.x, s.y], self.wout.at[zk, s.x, s.y]
        steps = [(b + 5 + k, a, s.y_mate()), (b + 9 + k, c, s.x_mate()), (b + 17 + 2 * k, c, s.y_mate())]
        if k in self.split:
            steps.append((b + 13 + k, a, s.x_mate()))
        for i, (number, ref, device) in enumerate(steps):
            known = self.senders.get((k, i))
            used = n.send(number, ref, ref, device, sender=known, like=self.like, keep=known is None)
            self.senders[(k, i)] = used

    def early(self):
        onward = self.arrive(1)
        pl.when(self.spot.inner)(onward)
        self.second(1)

        def near():
            self.arrive(3)()
            self.second(3)

        pl.when(self.spot.inner)(near)

    def late(self):
        onward = self.arrive(2)
        pl.when(self.spot.inner)(onward)
        self.second(2)

    def last(self):
        def far():
            self.arrive(3)
            self.second(3)

        pl.when(jnp.logical_not(self.spot.inner))(far)

    def third(self, k):
        s, n, b = self.spot, self.lines, self.base
        zk = s.z ^ k
        far = self.wout.at[zk, 1 - s.x, s.y]
        n.wait(b + 9 + k, far, s.x_mate())
        n.send(b + 18 + 2 * k, far, far, s.y_mate())
        if k:
            n.wait(b + 5 + k, self.win.at[zk, s.x, 1 - s.y], s.y_mate())
        if k in self.split:
            far = self.win.at[zk, 1 - s.x, s.y]
            n.wait(b + 13 + k, far, s.x_mate())
            n.send(b + 25 + k, far, far, s.y_mate())
        elif k:
            n.send(b + 13 + k, self.win.at[zk, s.x], self.win.at[zk, s.x], s.x_mate())

    def finish(self, k):
        s, n, b = self.spot, self.lines, self.base
        zk = s.z ^ k
        if k in self.split:
            n.wait(b + 25 + k, self.win.at[zk, 1 - s.x, 1 - s.y], s.y_mate())
        else:
            n.wait(b + 13 + k, self.win.at[zk, 1 - s.x], s.x_mate())
        if k:
            n.wait(b + 17 + 2 * k, self.wout.at[zk, s.x, 1 - s.y], s.y_mate())
        n.wait(b + 18 + 2 * k, self.wout.at[zk, 1 - s.x, 1 - s.y], s.y_mate())


GATHER_LINES = 29


class Reduce:
    def __init__(self, spot, lines, base, parts, yins, zin, result):
        self.spot, self.lines, self.base = spot, lines, base
        self.parts, self.yins, self.zin, self.result = parts, yins, zin, result

    order = ((0, 2), (0, 3), (1, 2), (1, 3), (0, 1), (1, 1), (0, 0), (1, 0))

    def first(self, ready):
        s, n, b = self.spot, self.lines, self.base
        for i, k in self.order[2 * ready : 2 + 6 * ready]:
            n.send(b + 2 * k + i, self.parts[i].at[s.z ^ k, 1 - s.y], self.yins[i].at[k], s.y_mate())

    def second(self, first, last):
        s, n, b = self.spot, self.lines, self.base
        for i, k in self.order[first:last]:
            ref, more = self.parts[i].at[s.z ^ k, s.y], self.yins[i].at[k]
            n.wait(b + 2 * k + i, more, s.y_mate())
            ref[...] = (ref[...].astype(F32) + more[...].astype(F32)).astype(BF16)
            if k:
                n.send(b + 6 + 2 * k + i, ref, self.zin.at[k - 1, i], s.z_mate(k))

    def third(self):
        s, n, b = self.spot, self.lines, self.base
        for i in (0, 1):
            total = self.parts[i][s.z, s.y].astype(F32)
            for k in (1, 2, 3):
                n.wait(b + 6 + 2 * k + i, self.zin.at[k - 1, i], s.z_mate(k))
                total = total + self.zin[k - 1, i].astype(F32)
            self.result[i, s.y] = total.astype(BF16)
            n.send(b + 14 + i, self.result.at[i, s.y], self.result.at[i, s.y], s.y_mate())

    def finish(self):
        s, n, b = self.spot, self.lines, self.base
        for i in (0, 1):
            n.wait(b + 14 + i, self.result.at[i, 1 - s.y], s.y_mate())


REDUCE_LINES = 16
MATE_LINES = 8
SEND_LINES = 200


def normalize(value):
    centre = value - jnp.mean(value, axis=-1, keepdims=True)
    scale = lax.rsqrt(jnp.mean(centre * centre, axis=-1, keepdims=True) + EPS_NORM)
    return centre * scale, scale


def normalize_back(grad, gain, unit, scale):
    gain_grad = jnp.sum(grad * unit, axis=0, keepdims=True)
    shift_grad = jnp.sum(grad, axis=0, keepdims=True)
    inner = grad * gain
    mean = jnp.mean(inner, axis=-1, keepdims=True)
    along = jnp.mean(inner * unit, axis=-1, keepdims=True)
    return scale * (inner - mean - unit * along), gain_grad, shift_grad


def dot(left, right):
    return jnp.dot(left, right, preferred_element_type=F32)


def dot_t(left, right):
    return lax.dot_general(left, right, (((1,), (1,)), ((), ())), preferred_element_type=F32)


def t_dot(left, right):
    return lax.dot_general(left, right, (((0,), (0,)), ((), ())), preferred_element_type=F32)


def pick(rows, columns, where):
    at = [lax.broadcasted_iota(jnp.int32, (rows, columns), axis) for axis in (0, 1)]
    return where(*at).astype(F32).astype(BF16)


def gelu_pair(v):
    root = math.sqrt(2.0 / math.pi)
    square = v * v
    tanh = jnp.tanh(root * v * (1.0 + 0.044715 * square))
    half = 0.5 + 0.5 * tanh
    slope = half + 0.5 * v * (1.0 - tanh * tanh) * (root * (1.0 + 3 * 0.044715 * square))
    return v * half, slope


def fused_kernel(
    plan,
    tokens, cotangent_far, win_far, wout_far, bias, vec, packed, rebuild_far, turn, wave_far,
    act_out, grad_out, weights_out, piece_out, pieces_out,
    cotangent, win_own, wout_own, rebuild, wave, local_sems,
    win, wout, bias_own, bias_all, hidden, acts, slopes, unit_mix, unit_out, scale_mix, scale_out, start, keep,
    branch_send, branch_recv, grad_branch, grad_pre, far_acts, far_pre,
    din, dout, yin, yout, zin, result,
    send, recv, work, send_back, recv_back,
    tiles, tiles_in, piece, pieces,
    mix_sems, all_sems, send_sems, recv_sems,
):
    spot = Spot()
    lines = Lines(send_sems, recv_sems)
    parts, feats, rows = plan.parts, plan.feats, plan.rows
    me = spot.me
    hid = FF // parts
    group = 2 * hid
    barrier = pltpu.get_barrier_semaphore()

    devices = 2 * parts
    here = spot.y * parts + me

    def other(k):
        q = lax.rem(here + k, devices)
        return q, {"dp": q // parts, "mp": lax.rem(q, parts)}

    def everyone(action):
        def body(k, carry):
            action(k)
            return carry

        lax.fori_loop(1, devices, body, 0)

    everyone(lambda k: pl.semaphore_signal(barrier, inc=1, device_id=other(k)[1], device_id_type=MESH))

    loads = [
        pltpu.make_async_copy(src, dst, local_sems.at[i])
        for i, (src, dst) in enumerate(
            (
                (win_far.at[0], win_own.at[0]),
                (wout_far.at[0], wout_own.at[0]),
                (wave_far, wave),
                (rebuild_far, rebuild),
                (win_far.at[1], win_own.at[1]),
                (wout_far.at[1], wout_own.at[1]),
                (cotangent_far, cotangent),
            )
        )
    ]
    for load in loads:
        load.start()

    base = 0
    gathers, reduces = [], []
    for l in range(LAYERS):
        gathers.append(Gather(spot, lines, base, win.at[l], wout.at[l]))
        base += GATHER_LINES
    for l in range(LAYERS):
        reduces.append(
            Reduce(
                spot, lines, base, (din.at[l], dout.at[l]), (yin.at[l], yout.at[l]), zin.at[l], result.at[l]
            )
        )
        base += REDUCE_LINES
    mates = []
    for l in range(LAYERS):
        mates.append(base)
        base += MATE_LINES
    bias_base = base

    def copy_to(k, src, dst, lane):
        q = lax.rem(me + k, parts)
        return pltpu.make_async_remote_copy(
            src_ref=src.at[q],
            dst_ref=dst.at[me],
            send_sem=mix_sems.at[lane, q],
            recv_sem=mix_sems.at[lane + 1, me],
            device_id={"mp": q},
            device_id_type=MESH,
        )

    def copy_from(k, src, dst, lane):
        p = lax.rem(me + k, parts)
        return pltpu.make_async_remote_copy(
            src_ref=src.at[p],
            dst_ref=dst.at[p],
            send_sem=mix_sems.at[lane, p],
            recv_sem=mix_sems.at[lane + 1, p],
            device_id={"mp": p},
            device_id_type=MESH,
        )

    def each(action):
        def body(k, carry):
            action(k)
            return carry

        lax.fori_loop(1, parts, body, 0)

    def mix_enter(value):
        send[...] = dot_t(packed[...], value).astype(BF16).reshape(parts, feats, rows)

    def mix_go():
        each(lambda k: copy_to(k, send, recv, 0).start())
        recv[me] = send[me]

    def mix_middle():
        each(lambda k: copy_from(k, send, recv, 0).wait_recv())
        position_dft(plan, me, recv, work, send_back, turn, wave)
        each(lambda k: copy_to(k, send_back, recv_back, 2).start())
        recv_back[me] = send_back[me]

    def mix_leave():
        each(lambda k: copy_from(k, send_back, recv_back, 2).wait_recv())
        mixed = t_dot(recv_back[...].reshape(parts * feats, rows), rebuild[...])
        each(lambda k: copy_to(k, send, recv, 0).wait_send())
        each(lambda k: copy_to(k, send_back, recv_back, 2).wait_send())
        return mixed * (1.0 / math.sqrt(L * D))

    eye = pick(hid, 256, lambda i, j: i == j)

    def bias_column(l, zk, x):
        return dot_t(eye, bias_all[zk, x])[:, l : l + 1]

    def own_weights(l):
        square = pick(hid, hid, lambda i, j: i == j)
        win[l, spot.z, spot.x] = dot_t(square, win_own[l].astype(BF16)).astype(BF16).reshape(2, hid // 2, D)
        wout[l, spot.z, spot.x] = wout_own[l].astype(BF16).reshape(2, hid // 2, D)

    def swap_branch(number, slot):
        ref, land = branch_send.at[slot], branch_recv.at[slot]
        return lines.send(number, ref, land, spot.core_mate(), keep=False)

    def forward(l, current, mixed, per_group):
        unit, scale = normalize(current + mixed)
        unit_mix[l] = unit
        scale_mix[l] = scale
        normed = unit * vec[l, 0:1] + vec[l, 1:2]
        keep[...] = normed
        hidden[l, 0] = normed.astype(BF16)
        lines.send(mates[l], hidden.at[l, 0], hidden.at[l, 1], spot.core_mate())
        for k in range(4):
            per_group(k)
            zk = spot.z ^ k
            weights = win[l, zk].reshape(group, D)
            column = jnp.concatenate([bias_column(l, zk, x) for x in (0, 1)], axis=0)
            for slot in (0, 1):
                if k == 0 and slot == 1:
                    lines.wait(mates[l], hidden.at[l, 1], spot.core_mate())
                value, slope = gelu_pair(dot_t(weights, hidden[l, slot]) + column)
                span = slice(slot * rows, (slot + 1) * rows)
                acts[l, zk, :, :, span] = value.astype(BF16).reshape(2, hid, rows)
                slopes[l, zk, :, :, span] = slope.astype(BF16).reshape(2, hid, rows)
        outs = wout[l].reshape(FF // 2, D)
        branch_send[0] = t_dot(acts[l, :, :, :, rows : 2 * rows].reshape(FF // 2, rows), outs).astype(BF16)
        sender = swap_branch(mates[l] + 1, 0)
        branch = t_dot(acts[l, :, :, :, 0:rows].reshape(FF // 2, rows), outs)
        lines.wait(mates[l] + 1, branch_recv.at[0], spot.core_mate())
        total = keep[...] + branch + branch_recv[0].astype(F32) + vec[l, 2:3]
        unit, scale = normalize(total)
        unit_out[l] = unit
        scale_out[l] = scale
        lines.wait_sent(sender, branch_send.at[0], spot.core_mate())
        return unit * vec[l, 3:4] + vec[l, 4:5]

    def vec_put(l, i, value):
        for t in range(3):
            for j in (0, 1):
                at = 256 * t + 128 * j
                tiles[3 * (5 * l + i) + t, j : j + 1, :] = value[:, at : at + 128]

    def bias_put(l):
        ones = jnp.ones((16, 2 * rows), BF16)
        for zk in range(4):
            for x in (0, 1):
                row = dot_t(ones, grad_pre[zk, x])[0:1]
                for y in (0, 1):
                    to = y * parts + zk * 4 + x * 2 + spot.core
                    tiles[to, 2 + 2 * l : 3 + 2 * l, :] = row[:, 0:128]
                    tiles[to, 3 + 2 * l : 4 + 2 * l, 0 : hid - 128] = row[:, 128:hid]

    def hidden_away(l):
        lines.send(mates[l] + 4, hidden.at[l, 0], hidden.at[l, 2], spot.x_mate())

    def from_x_mate(l):
        for i, part in ((4, hidden), (6, grad_branch)):
            lines.wait(mates[l] + i, part.at[l, 2], spot.x_mate())
            lines.send(mates[l] + i + 1, part.at[l, 2], part.at[l, 3], spot.core_mate())

    def weight_grads(l):
        half = FF // 4
        ins = win[l, :, spot.x].reshape(half, D)
        outs = wout[l, :, spot.x].reshape(half, D)
        column = jnp.concatenate([bias_column(l, zk, spot.x) for zk in range(4)], axis=0)
        for slot in (2, 3):
            if slot == 3:
                for i, part in ((5, hidden), (7, grad_branch)):
                    lines.wait(mates[l] + i, part.at[l, 3], spot.core_mate())
            span = slice((slot - 2) * rows, (slot - 1) * rows)
            value, slope = gelu_pair(dot_t(ins, hidden[l, slot]) + column)
            far_acts[:, span] = value.astype(BF16)
            far_pre[:, span] = (dot_t(outs, grad_branch[l, slot]) * slope).astype(BF16)
        for i, (near, far, part, out) in enumerate(
            (
                (grad_pre[:, spot.x], far_pre, hidden, din),
                (acts[l, :, spot.x], far_acts, grad_branch, dout),
            )
        ):
            total = dot(near.reshape(half, 2 * rows), part[l, 0:2].reshape(2 * rows, D))
            total = total + dot(far[...], part[l, 2:4].reshape(2 * rows, D))
            out[l] = total.astype(BF16).reshape(4, 2, hid // 2, D)
            reduces[l].first(i)

    def backward(l, grad, meanwhile, later):
        grad_total, gain_grad, shift_grad = normalize_back(grad, vec[l, 3:4], unit_out[l], scale_out[l])
        low = grad_total.astype(BF16)
        grad_branch[l, 0] = low
        lines.send(mates[l] + 2, grad_branch.at[l, 0], grad_branch.at[l, 1], spot.core_mate())
        lines.send(mates[l] + 6, grad_branch.at[l, 0], grad_branch.at[l, 2], spot.x_mate())
        keep[...] = grad_total
        meanwhile()
        vec_put(l, 2, jnp.sum(low.astype(F32), axis=0, keepdims=True))
        vec_put(l, 3, gain_grad)
        vec_put(l, 4, shift_grad)
        for slot in (0, 1):
            if slot == 1:
                lines.wait(mates[l] + 2, grad_branch.at[l, 1], spot.core_mate())
            span = slice(slot * rows, (slot + 1) * rows)
            for zk in range(4):
                grad_act = dot_t(wout[l, zk].reshape(group, D), grad_branch[l, slot]).reshape(2, hid, rows)
                grad_pre[zk, :, :, span] = (grad_act * slopes[l, zk, :, :, span].astype(F32)).astype(BF16)
        ins = win[l].reshape(FF // 2, D)
        branch_send[1] = t_dot(grad_pre[:, :, :, rows : 2 * rows].reshape(FF // 2, rows), ins).astype(BF16)
        sender = swap_branch(mates[l] + 3, 1)
        grad_normed = t_dot(grad_pre[:, :, :, 0:rows].reshape(FF // 2, rows), ins)
        bias_put(l)
        later()
        lines.wait(mates[l] + 3, branch_recv.at[1], spot.core_mate())
        grad_normed = keep[...] + grad_normed + branch_recv[1].astype(F32)
        lines.wait_sent(sender, branch_send.at[1], spot.core_mate())
        grad_summed, gain_grad, shift_grad = normalize_back(grad_normed, vec[l, 0:1], unit_mix[l], scale_mix[l])
        vec_put(l, 0, gain_grad)
        vec_put(l, 1, shift_grad)
        return grad_summed

    inner = plan.inner

    def to_local(i, j):
        return j == parts * (i % inner) + i // inner

    local = dot(pick(rows, rows, to_local), tokens[...])
    start[...] = local
    mix_enter(local.astype(BF16))
    for load in loads[:2]:
        load.wait()
    own_weights(0)
    bias_own[...] = jnp.zeros_like(bias_own)
    bias_own[0:LAYERS, 0:hid] = bias[...]
    bias_all[spot.z, spot.x] = bias_own[...].astype(BF16)
    tiles[...] = jnp.zeros_like(tiles)
    pl.semaphore_wait(barrier, devices - 1)
    gathers[0].start_z()
    gathers[0].start_x()
    mix_go()
    for j in range(1, 8):
        far = spot.own ^ j
        own = bias_all.at[spot.z, spot.x]
        lines.send(bias_base + j, own, own, {"dp": spot.y, "mp": far * 2 + spot.core})
    for load in loads[2:]:
        load.wait()
    own_weights(1)
    gathers[0].early()
    gathers[0].third(0)
    gathers[0].late()
    gathers[0].third(1)
    mix_middle()
    gathers[0].last()
    gathers[1].start_z()
    gathers[0].third(2)
    gathers[0].third(3)
    gathers[1].start_x()
    for j in range(1, 8):
        far = spot.own ^ j
        lines.wait(bias_base + j, bias_all.at[far // 2, far % 2], {"dp": spot.y, "mp": far * 2 + spot.core})
    mixed = mix_leave()

    def between(k):
        if k == 2:
            gathers[1].early()
        gathers[0].finish(k)

    current = forward(0, start[...], mixed, between)
    start[...] = current
    mix_enter(current.astype(BF16))
    mix_go()
    gathers[1].third(0)
    gathers[1].late()
    gathers[1].third(1)
    gathers[1].last()
    gathers[1].third(2)
    mix_middle()
    gathers[1].third(3)
    mixed = mix_leave()
    current = forward(1, start[...], mixed, lambda k: gathers[1].finish(k))
    hidden_away(1)
    act_out[...] = t_dot(pick(rows, rows, to_local), current.astype(BF16)).astype(BF16)

    grad = backward(1, dot(pick(rows, rows, to_local), cotangent[...]), lambda: None, lambda: None)
    start[...] = grad
    mix_enter(grad.astype(BF16))
    mix_go()
    hidden_away(0)
    from_x_mate(1)
    weight_grads(1)
    mix_middle()
    mixed = mix_leave()
    grad = backward(0, start[...] + mixed, lambda: reduces[1].second(0, 4), lambda: reduces[1].second(4, 8))

    def tile_to(k):
        q, device = other(k)
        return pltpu.make_async_remote_copy(
            src_ref=tiles.at[q], dst_ref=tiles_in.at[here], send_sem=all_sems.at[0, q], recv_sem=all_sems.at[1, here],
            device_id=device, device_id_type=MESH,
        )

    def tile_from(k):
        p, device = other(k)
        return pltpu.make_async_remote_copy(
            src_ref=tiles.at[p], dst_ref=tiles_in.at[p], send_sem=all_sems.at[0, p], recv_sem=all_sems.at[1, p],
            device_id=device, device_id_type=MESH,
        )

    everyone(lambda k: tile_to(k).start())
    tiles_in[here] = tiles[here]
    start[...] = grad
    mix_enter(grad.astype(BF16))
    mix_go()
    from_x_mate(0)
    weight_grads(0)
    reduces[1].third()
    reduces[0].second(0, 4)
    mix_middle()
    reduces[0].second(4, 8)
    everyone(lambda k: tile_from(k).wait_recv())
    total = tiles_in[0]
    for d in range(1, devices):
        total = total + tiles_in[d]
    piece_out[...] = total
    reduces[1].finish()
    weights_out[1] = result[1]
    mixed = mix_leave()
    grad = start[...] + mixed
    back = pick(rows, rows, lambda i, j: to_local(j, i))
    high = grad.astype(BF16)
    rest = grad - high.astype(F32)
    middle = rest.astype(BF16)
    low = (rest - middle.astype(F32)).astype(BF16)
    grad_out[...] = dot(back, high) + (dot(back, middle) + dot(back, low))

    def squares(ref):
        value = ref[...].reshape(hid, D).astype(F32)
        return jnp.sum(value * value, axis=(0, 1), keepdims=True)

    row = lax.broadcasted_iota(jnp.int32, total.shape, 0)
    local = jnp.sum(jnp.where((row >= 2) & (row < 6), total * total, 0.0), axis=(0, 1), keepdims=True)
    local = local + squares(result.at[1, 0]) + squares(result.at[1, 1])
    reduces[0].third()
    reduces[0].finish()
    weights_out[0] = result[0]
    local = local + squares(result.at[0, 0]) + squares(result.at[0, 1])
    piece[...] = jnp.where(row < 2, total, jnp.broadcast_to(local, total.shape))

    def piece_to(k):
        q, device = other(k)
        return pltpu.make_async_remote_copy(
            src_ref=piece, dst_ref=pieces.at[here], send_sem=all_sems.at[2, q], recv_sem=all_sems.at[3, here],
            device_id=device, device_id_type=MESH,
        )

    def piece_from(k):
        p, device = other(k)
        return pltpu.make_async_remote_copy(
            src_ref=piece, dst_ref=pieces.at[p], send_sem=all_sems.at[2, p], recv_sem=all_sems.at[3, p],
            device_id=device, device_id_type=MESH,
        )

    everyone(lambda k: piece_to(k).start())
    pieces[here] = piece[...]
    everyone(lambda k: tile_to(k).wait_send())
    lines.drain(spot.core_mate())
    everyone(lambda k: piece_from(k).wait_recv())
    pieces_out[...] = pieces[...]
    everyone(lambda k: piece_to(k).wait_send())


def fused(plan, tokens, cotangent, weight_in, weight_out, bias_in, vec):
    parts, feats, rows = plan.parts, plan.feats, plan.rows
    block = (parts, feats, rows)
    hid = FF // parts
    half = hid // 2
    vm = pltpu.VMEM
    near, far = pl.BlockSpec(memory_space=vm), pl.BlockSpec(memory_space=pl.ANY)
    line_count = LAYERS * (GATHER_LINES + REDUCE_LINES + MATE_LINES) + 8
    return pl.pallas_call(
        functools.partial(fused_kernel, plan),
        out_shape=(
            jax.ShapeDtypeStruct((rows, D), BF16),
            jax.ShapeDtypeStruct((rows, D), F32),
            jax.ShapeDtypeStruct((LAYERS, 2, 2, half, D), BF16),
            jax.ShapeDtypeStruct((8, 128), F32),
            jax.ShapeDtypeStruct((2 * parts, 8, 128), F32),
        ),
        in_specs=[near, far, far, far, near, near, near, far, near, far],
        out_specs=[near] * 5,
        scratch_shapes=[
            vm((rows, D), BF16),
            vm((LAYERS, D, hid), F32),
            vm((LAYERS, hid, D), F32),
            vm((parts * feats, D), BF16),
            vm((2 * rows, rows), BF16),
            pltpu.SemaphoreType.DMA((7,)),
            vm((LAYERS, 4, 2, 2, half, D), BF16),
            vm((LAYERS, 4, 2, 2, half, D), BF16),
            vm((16, 256), F32),
            vm((4, 2, 16, 256), BF16),
            vm((LAYERS, 4, rows, D), BF16),
            vm((LAYERS, 4, 2, hid, 2 * rows), BF16),
            vm((LAYERS, 4, 2, hid, 2 * rows), BF16),
            vm((LAYERS, rows, D), F32),
            vm((LAYERS, rows, D), F32),
            vm((LAYERS, rows, 1), F32),
            vm((LAYERS, rows, 1), F32),
            vm((rows, D), F32),
            vm((rows, D), F32),
            vm((2, rows, D), BF16),
            vm((2, rows, D), BF16),
            vm((LAYERS, 4, rows, D), BF16),
            vm((4, 2, hid, 2 * rows), BF16),
            vm((FF // 4, 2 * rows), BF16),
            vm((FF // 4, 2 * rows), BF16),
            vm((LAYERS, 4, 2, half, D), BF16),
            vm((LAYERS, 4, 2, half, D), BF16),
            vm((LAYERS, 4, half, D), BF16),
            vm((LAYERS, 4, half, D), BF16),
            vm((LAYERS, 3, 2, half, D), BF16),
            vm((LAYERS, 2, 2, half, D), BF16),
            vm(block, BF16),
            vm(block, BF16),
            vm((parts, feats, 2 * rows), BF16),
            vm(block, BF16),
            vm(block, BF16),
            vm((2 * parts, 8, 128), F32),
            vm((2 * parts, 8, 128), F32),
            vm((8, 128), F32),
            vm((2 * parts, 8, 128), F32),
            pltpu.SemaphoreType.DMA((4, parts)),
            pltpu.SemaphoreType.DMA((4, 2 * parts)),
            pltpu.SemaphoreType.DMA((SEND_LINES,)),
            pltpu.SemaphoreType.DMA((line_count,)),
        ],
        compiler_params=pltpu.CompilerParams(collective_id=1, has_side_effects=True, vmem_limit_bytes=62 * 2**20),
    )(tokens, cotangent, weight_in, weight_out, bias_in, vec, plan.packed, plan.rebuild, plan.turn, plan.wave)


def on_block(
    tokens, cotangent, weight_in, bias_in, weight_out, vectors, moment_in, square_in,
    moment_bias, square_bias, moment_out, square_out, moment_vec, square_vec,
):
    rows = tokens.shape[0]
    plan = Plan(L // rows)
    hid = FF // plan.parts
    acts, grad, weights, piece, pieces = fused(
        plan, tokens.reshape(rows, D), cotangent.reshape(rows, D), weight_in, weight_out, bias_in, vectors
    )
    sum_vec = pieces[: 10 * D // 256, 0:2].reshape(LAYERS, 5, D)
    grad_norm = jnp.sqrt(0.5 * jnp.sum(pieces[:, 2, 0]) + jnp.sum(sum_vec * sum_vec))
    factor = jnp.minimum(1.0, CLIP / grad_norm)
    weights = weights.reshape(LAYERS, 2, hid, D).astype(F32)
    sum_in = jnp.swapaxes(weights[:, 0], 1, 2)
    sum_out = weights[:, 1]
    sum_bias = piece[2:6].reshape(LAYERS, 256)[:, :hid]
    m_in, v_in, w_in = adamw(weight_in, sum_in * factor, moment_in, square_in, 1.0 / math.sqrt(D), DECAY)
    m_out, v_out, w_out = adamw(weight_out, sum_out * factor, moment_out, square_out, 1.0 / math.sqrt(FF), DECAY)
    m_bias, v_bias, b_new = adamw(bias_in, sum_bias * factor, moment_bias, square_bias, 0.5, 0.0)
    m_vec, v_vec, vec_new = adamw(vectors, sum_vec * factor, moment_vec, square_vec, 0.5, 0.0)
    return (
        acts.reshape(rows, 1, D),
        grad.reshape(rows, 1, D),
        grad_norm,
        m_in,
        v_in,
        w_in,
        w_in.astype(BF16),
        m_out,
        v_out,
        w_out,
        w_out.astype(BF16),
        m_bias,
        v_bias,
        b_new,
        m_vec,
        v_vec,
        vec_new,
    )


def matmul(left_op, right_op):
    return jnp.dot(left_op, right_op, preferred_element_type=jnp.float32)


def inner_rows(left_op, right_op):
    return lax.dot_general(
        left_op, right_op, (((0,), (0,)), ((), ())), preferred_element_type=jnp.float32
    )


def inner_cols(left_op, right_op):
    return lax.dot_general(
        left_op, right_op, (((1,), (1,)), ((), ())), preferred_element_type=jnp.float32
    )


def layer_norm(value, gain, shift):
    centre = value - jnp.mean(value, axis=-1, keepdims=True)
    spread = jnp.mean(centre * centre, axis=-1, keepdims=True)
    return centre * lax.rsqrt(spread + EPS_NORM) * gain + shift


def adamw(weight, grad, moment, square, rate, decay):
    new_moment = BETA_ONE * moment + (1.0 - BETA_ONE) * grad
    new_square = BETA_TWO * square + (1.0 - BETA_TWO) * grad * grad
    moment_hat = new_moment / (1.0 - BETA_ONE**STEP)
    square_hat = new_square / (1.0 - BETA_TWO**STEP)
    new_weight = weight - rate * (moment_hat / (jnp.sqrt(square_hat) + EPS_ADAM) + decay * weight)
    return (new_moment, new_square, new_weight)


def on_device(
    tokens,
    cotangent,
    weight_in,
    bias_in,
    weight_out,
    vectors,
    moment_in,
    square_in,
    moment_bias,
    square_bias,
    moment_out,
    square_out,
    moment_vec,
    square_vec,
):
    row_count, seq_count, feat_count = tokens.shape
    plan = Plan(L // row_count)

    def localize(value):
        return jnp.swapaxes(value.reshape(plan.inner, plan.parts, -1), 0, 1).reshape(value.shape)

    def restore(value):
        return jnp.swapaxes(value.reshape(plan.parts, plan.inner, -1), 0, 1).reshape(value.shape)

    current = localize(tokens).astype(jnp.float32)
    saved = []
    for layer_at in range(LAYERS):
        vector_set = vectors[layer_at]
        rounded = current.astype(jnp.bfloat16)
        mixed = mix(plan, rounded.reshape(row_count, feat_count)).reshape(row_count, seq_count, feat_count)
        summed = current + mixed
        normed = layer_norm(summed, vector_set[0], vector_set[1])
        hidden_in = normed.astype(jnp.bfloat16)
        weight_one = weight_in[layer_at].astype(jnp.bfloat16)
        weight_two = weight_out[layer_at].astype(jnp.bfloat16)
        bias_one = bias_in[layer_at].astype(jnp.bfloat16)
        whole_one, whole_two, whole_bias = (
            lax.all_gather(weight_one, "mp", axis=1, tiled=True),
            lax.all_gather(weight_two, "mp", axis=0, tiled=True),
            lax.all_gather(bias_one, "mp", axis=0, tiled=True),
        )
        inputs = hidden_in.reshape(-1, feat_count)
        pre_act = matmul(inputs, whole_one) + whole_bias.astype(jnp.float32)
        acts = jax.nn.gelu(pre_act).astype(jnp.bfloat16)
        branch = matmul(acts, whole_two).reshape(row_count, seq_count, feat_count)
        held = (inputs, whole_one, whole_two)
        total = normed + branch + vector_set[2]
        current = layer_norm(total, vector_set[3], vector_set[4])
        saved.append((summed, total, pre_act, acts, held))
    activations = restore(current.astype(jnp.bfloat16))
    grad = localize(cotangent).astype(jnp.float32)
    layer_grads = [None] * LAYERS
    for layer_at in reversed(range(LAYERS)):
        vector_set = vectors[layer_at]
        summed, total, pre_act, acts, held = saved[layer_at]
        inputs, mat_one, mat_two = held
        _, pull_out = jax.vjp(layer_norm, total, vector_set[3], vector_set[4])
        grad_total, gain_two, shift_two = pull_out(grad)
        grad_branch = grad_total.astype(jnp.bfloat16)
        grad_bias_two = jnp.sum(grad_branch.astype(jnp.float32), axis=(0, 1))
        flat_grad = grad_branch.reshape(-1, feat_count)
        grad_act = inner_cols(flat_grad, mat_two)
        _, pull_gelu = jax.vjp(jax.nn.gelu, pre_act)
        grad_pre = pull_gelu(grad_act)[0].astype(jnp.bfloat16)
        full_one = inner_rows(inputs, grad_pre)
        full_two = inner_rows(acts, flat_grad)
        full_bias = jnp.sum(grad_pre.astype(jnp.float32), axis=0)
        grad_one, grad_two, grad_bias_one = (
            lax.psum_scatter(
                full_one.astype(jnp.bfloat16), "mp", scatter_dimension=1, tiled=True
            ).astype(jnp.float32),
            lax.psum_scatter(
                full_two.astype(jnp.bfloat16), "mp", scatter_dimension=0, tiled=True
            ).astype(jnp.float32),
            lax.psum_scatter(
                full_bias.astype(jnp.bfloat16), "mp", scatter_dimension=0, tiled=True
            ).astype(jnp.float32),
        )
        grad_normed = inner_cols(grad_pre, mat_one).reshape(row_count, seq_count, feat_count)
        grad_normed = grad_normed + grad_total
        _, pull_in = jax.vjp(layer_norm, summed, vector_set[0], vector_set[1])
        grad_summed, gain_one, shift_one = pull_in(grad_normed)
        mix_grad = grad_summed.astype(jnp.bfloat16).reshape(-1, feat_count)
        grad_mix = mix(plan, mix_grad).reshape(row_count, seq_count, feat_count)
        grad = grad_summed + grad_mix
        layer_grads[layer_at] = (
            grad_one,
            grad_two,
            grad_bias_one,
            jnp.stack([gain_one, shift_one, grad_bias_two, gain_two, shift_two]),
        )
    stack_in = jnp.stack([entry[0] for entry in layer_grads])
    stack_out = jnp.stack([entry[1] for entry in layer_grads])
    stack_bias = jnp.stack([entry[2] for entry in layer_grads])
    stack_vec = jnp.stack([entry[3] for entry in layer_grads])
    sum_in, sum_out, sum_bias, sum_vec = (
        lax.psum(stack_in.astype(jnp.bfloat16), "dp").astype(jnp.float32),
        lax.psum(stack_out.astype(jnp.bfloat16), "dp").astype(jnp.float32),
        lax.psum(stack_bias.astype(jnp.bfloat16), "dp").astype(jnp.float32),
        lax.psum(stack_vec.astype(jnp.bfloat16), "dp").astype(jnp.float32),
    )
    local_squares = (
        jnp.sum(sum_in * sum_in) + jnp.sum(sum_out * sum_out) + jnp.sum(sum_bias * sum_bias)
    )
    sum_vec, total_squares = lax.psum((sum_vec, local_squares), "mp")
    grad_norm = jnp.sqrt(total_squares + jnp.sum(sum_vec * sum_vec))
    factor = jnp.minimum(1.0, CLIP / grad_norm)
    m_in, v_in, w_in = adamw(
        weight_in, sum_in * factor, moment_in, square_in, 1.0 / math.sqrt(D), DECAY
    )
    m_out, v_out, w_out = adamw(
        weight_out, sum_out * factor, moment_out, square_out, 1.0 / math.sqrt(FF), DECAY
    )
    m_bias, v_bias, b_new = adamw(bias_in, sum_bias * factor, moment_bias, square_bias, 0.5, 0.0)
    m_vec, v_vec, vec_new = adamw(vectors, sum_vec * factor, moment_vec, square_vec, 0.5, 0.0)
    return (
        activations,
        restore(grad),
        grad_norm,
        m_in,
        v_in,
        w_in,
        w_in.astype(jnp.bfloat16),
        m_out,
        v_out,
        w_out,
        w_out.astype(jnp.bfloat16),
        m_bias,
        v_bias,
        b_new,
        m_vec,
        v_vec,
        vec_new,
    )


def solution(mesh):
    body = on_block if (mesh.shape["dp"], mesh.shape["mp"]) == (2, 16) else on_device
    return jax.shard_map(
        body,
        mesh=mesh,
        in_specs=(
            P("mp", "dp", None),
            P("mp", "dp", None),
            P(None, None, "mp"),
            P(None, "mp"),
            P(None, "mp", None),
            P(),
            P(None, None, "mp"),
            P(None, None, "mp"),
            P(None, "mp"),
            P(None, "mp"),
            P(None, "mp", None),
            P(None, "mp", None),
            P(),
            P(),
        ),
        out_specs=(
            P("mp", "dp", None),
            P("mp", "dp", None),
            P(),
            P(None, None, "mp"),
            P(None, None, "mp"),
            P(None, None, "mp"),
            P(None, None, "mp"),
            P(None, "mp", None),
            P(None, "mp", None),
            P(None, "mp", None),
            P(None, "mp", None),
            P(None, "mp"),
            P(None, "mp"),
            P(None, "mp"),
            P(),
            P(),
            P(),
        ),
        check_vma=False,
    )
```

```python
import functools
import math

import jax
import jax.numpy as jnp
import ml_dtypes
import numpy as np
from jax import lax
from jax.experimental import pallas as pl
from jax.experimental.pallas import tpu as pltpu
from jax.sharding import PartitionSpec as P

D = 768
FF = 3072
L = 4096
LAYERS = 2
STEP = 5


CLIP = 1.0
BETA_ONE = 0.5
BETA_TWO = 0.5
EPS_ADAM = 1e-08
EPS_NORM = 1e-05
DECAY = 0.01
MESH = pl.DeviceIdType.MESH
F32 = jnp.float32
BF16 = jnp.bfloat16


class Plan:
    def __init__(self, parts):
        self.parts = parts
        self.rows = L // parts
        self.inner = self.rows // parts
        self.pairs = D // 2 // parts
        self.feats = -(-2 * self.pairs // 16) * 16
        rows, inner = self.rows, self.inner
        lane = np.arange(rows)
        self.place = parts * (lane % inner) + lane // inner
        packed = np.zeros((parts, self.feats, D))
        rebuild = np.zeros((parts, self.feats, D))
        n = np.arange(D)
        for at in range(parts):
            for i in range(self.pairs):
                m = self.pairs * at + i
                a, b = i, self.pairs + i
                packed[at, a] = np.cos(2 * np.pi * (m * n % D) / D)
                rebuild[at, a, m] = 1.0
                if m == 0:
                    packed[at, b] = np.cos(2 * np.pi * (D // 2 * n % D) / D)
                    rebuild[at, b, D // 2] = 1.0
                else:
                    packed[at, b] = np.sin(2 * np.pi * (m * n % D) / D)
                    rebuild[at, a, D - m] = 1.0
                    rebuild[at, b, m] = -1.0
                    rebuild[at, b, D - m] = 1.0
        bf = ml_dtypes.bfloat16
        self.packed = packed.reshape(-1, D).astype(bf)
        self.rebuild = rebuild.reshape(-1, D).astype(bf)
        turn = 2 * np.pi * (np.arange(parts)[:, None] * self.place[None, :] % L) / L
        self.turn = np.stack([np.cos(turn), np.sin(turn)]).astype(np.float32)
        angle = 2 * np.pi * (self.place[:, None] * np.arange(rows)[None, :] % rows) / rows
        self.wave = np.concatenate([np.cos(angle), np.sin(angle)]).astype(bf)


def half_dft(values):
    n = len(values)
    if n == 1:
        return [(values[0], None)]
    if n == 2:
        return [(values[0] + values[1], None), (values[0] - values[1], None)]
    even, odd = half_dft(values[0::2]), half_dft(values[1::2])
    half = n // 2
    result = [None] * (half + 1)
    for k in range(half // 2 + 1):
        er, ei = even[k]
        orr, oi = odd[k]
        if k == 0:
            result[0] = (er + orr, None)
            result[half] = (er - orr, None)
        elif 2 * k == half:
            result[k] = (er, -orr)
        else:
            c, s = math.cos(2 * math.pi * k / n), math.sin(2 * math.pi * k / n)
            tr, ti = orr * c + oi * s, oi * c - orr * s
            result[k] = (er + tr, ei + ti)
            result[half - k] = (er - tr, ti - ei)
    return result


def position_dft(plan, me, recv, work, send, turn_ref, wave_ref):
    parts, feats, rows, inner, pairs = plan.parts, plan.feats, plan.rows, plan.inner, plan.pairs
    chunk = 16
    lanes = min(rows, 128)
    for lane_at in range(0, rows, lanes):

        def body(i, carry):
            at = pl.multiple_of(i * chunk, chunk)
            values = [recv[p, pl.ds(at, chunk), lane_at : lane_at + lanes].astype(F32) for p in range(parts)]
            outs = half_dft(values)
            row = at + lax.broadcasted_iota(jnp.int32, (chunk, lanes), 0)
            is_sine = (row >= pairs) & jnp.logical_not((row == pairs) & (me == 0))
            for d in range(parts):
                re, im = outs[min(d, parts - d)]
                im = jnp.zeros_like(re) if im is None else im
                if d > parts - d:
                    im = -im
                re, im = jnp.where(is_sine, -im, re), jnp.where(is_sine, re, im)
                c = turn_ref[0, d : d + 1, lane_at : lane_at + lanes]
                s = turn_ref[1, d : d + 1, lane_at : lane_at + lanes]
                work[d, pl.ds(at, chunk), lane_at : lane_at + lanes] = (re * c + im * s).astype(BF16)
                work[d, pl.ds(at, chunk), rows + lane_at : rows + lane_at + lanes] = (im * c - re * s).astype(BF16)
            return carry

        lax.fori_loop(0, feats // chunk, body, 0)

    def swap(i, carry):
        at = pl.multiple_of(i * chunk, chunk)
        spectrum = jnp.dot(
            work[:, pl.ds(at, chunk), :].reshape(parts * chunk, 2 * rows), wave_ref[...], preferred_element_type=F32
        )
        outs = [spectrum[d * chunk : (d + 1) * chunk] for d in range(parts)]
        group = lax.broadcasted_iota(jnp.int32, (chunk, rows), 1) // inner
        bit = 1
        while bit < parts:
            upper = (group // bit) % 2 == 1
            for d in range(parts):
                if d & bit:
                    continue
                low, high = outs[d], outs[d | bit]
                shift = inner * bit
                outs[d] = jnp.where(upper, pltpu.roll(high, shift, 1), low)
                outs[d | bit] = jnp.where(upper, high, pltpu.roll(low, rows - shift, 1))
            bit *= 2
        for q in range(parts):
            send[q, pl.ds(at, chunk), :] = outs[q].astype(BF16)
        return carry

    lax.fori_loop(0, feats // chunk, swap, 0)


def exchange(plan, me, send, recv, send_sem, recv_sem):
    parts = plan.parts

    def copy_to(k):
        q = lax.rem(me + k, parts)
        return pltpu.make_async_remote_copy(
            src_ref=send.at[q],
            dst_ref=recv.at[me],
            send_sem=send_sem.at[q],
            recv_sem=recv_sem.at[me],
            device_id={"mp": q},
            device_id_type=MESH,
        )

    def copy_from(k):
        p = lax.rem(me + k, parts)
        return pltpu.make_async_remote_copy(
            src_ref=send.at[p],
            dst_ref=recv.at[p],
            send_sem=send_sem.at[p],
            recv_sem=recv_sem.at[p],
            device_id={"mp": p},
            device_id_type=MESH,
        )

    def start(k, carry):
        copy_to(k).start()
        return carry

    def finish(k, carry):
        copy_from(k).wait_recv()
        return carry

    def drain(k, carry):
        copy_to(k).wait_send()
        return carry

    lax.fori_loop(1, parts, start, 0)
    recv[me] = send[me]
    lax.fori_loop(1, parts, finish, 0)
    lax.fori_loop(1, parts, drain, 0)


def mix_kernel(plan, x_ref, packed_ref, rebuild_ref, turn_ref, wave_ref, out_ref, send, recv, work, send_back, recv_back, sems):
    me = lax.axis_index("mp")
    parts, feats, rows = plan.parts, plan.feats, plan.rows
    barrier = pltpu.get_barrier_semaphore()

    def greet(k, carry):
        pl.semaphore_signal(barrier, inc=1, device_id={"mp": lax.rem(me + k, parts)}, device_id_type=MESH)
        return carry

    lax.fori_loop(1, parts, greet, 0)
    pl.semaphore_wait(barrier, parts - 1)

    columns = lax.dot_general(packed_ref[...], x_ref[...], (((1,), (1,)), ((), ())), preferred_element_type=F32)
    send[...] = columns.astype(BF16).reshape(parts, feats, rows)
    exchange(plan, me, send, recv, sems.at[0], sems.at[1])
    position_dft(plan, me, recv, work, send_back, turn_ref, wave_ref)
    exchange(plan, me, send_back, recv_back, sems.at[2], sems.at[3])
    mixed = lax.dot_general(
        recv_back[...].reshape(parts * feats, rows), rebuild_ref[...], (((0,), (0,)), ((), ())), preferred_element_type=F32
    )
    out_ref[...] = mixed * (1.0 / math.sqrt(L * D))


def mix(plan, value):
    block = (plan.parts, plan.feats, plan.rows)
    return pl.pallas_call(
        functools.partial(mix_kernel, plan),
        out_shape=jax.ShapeDtypeStruct((plan.rows, D), F32),
        in_specs=[pl.BlockSpec(memory_space=pltpu.VMEM)] * 5,
        out_specs=pl.BlockSpec(memory_space=pltpu.VMEM),
        scratch_shapes=[
            pltpu.VMEM(block, BF16),
            pltpu.VMEM(block, BF16),
            pltpu.VMEM((plan.parts, plan.feats, 2 * plan.rows), BF16),
            pltpu.VMEM(block, BF16),
            pltpu.VMEM(block, BF16),
            pltpu.SemaphoreType.DMA((4, plan.parts)),
        ],
        compiler_params=pltpu.CompilerParams(
            collective_id=0, has_side_effects=True, vmem_limit_bytes=40 * 2**20
        ),
    )(value, plan.packed, plan.rebuild, plan.turn, plan.wave)


class Spot:
    def __init__(self):
        self.y = lax.axis_index("dp")
        self.me = lax.axis_index("mp")
        self.z, self.x, self.core = self.me // 4, (self.me // 2) % 2, self.me % 2
        self.own = self.me // 2
        self.inner = (self.z == 1) | (self.z == 2)

    def at(self, y=None, z=None, x=None, core=None):
        y = self.y if y is None else y
        z = self.z if z is None else z
        x = self.x if x is None else x
        core = self.core if core is None else core
        return {"dp": y, "mp": z * 4 + x * 2 + core}

    def y_mate(self):
        return self.at(y=1 - self.y)

    def x_mate(self):
        return self.at(x=1 - self.x)

    def core_mate(self):
        return self.at(core=1 - self.core)

    def z_mate(self, k):
        return self.at(z=self.z ^ k)


class Lines:
    def __init__(self, send_sems, recv_sems):
        self.send_sems, self.recv_sems = send_sems, recv_sems
        self.next = 0
        self.sent = []

    def copy(self, sender, number, src, dst, device):
        return pltpu.make_async_remote_copy(
            src_ref=src,
            dst_ref=dst,
            send_sem=self.send_sems.at[sender],
            recv_sem=self.recv_sems.at[number],
            device_id=device,
            device_id_type=MESH,
        )

    def send(self, number, src, dst, device, sender=None, like=None, when=None, keep=True):
        if sender is None:
            sender = self.next
            self.next += 1
        self.copy(sender, number, src, dst, device).start()
        if keep:
            self.sent.append((sender, src if like is None else like, when))
        return sender

    def wait(self, number, land, device):
        self.copy(0, number, land, land, device).wait_recv()

    def wait_sent(self, sender, src, device):
        self.copy(sender, 0, src, src, device).wait_send()

    def drain(self, device):
        for sender, src, when in self.sent:
            if when is None:
                self.wait_sent(sender, src, device)
            else:
                pl.when(when)(functools.partial(self.wait_sent, sender, src, device))
        self.sent = []


class Gather:
    split = (2, 3)

    def __init__(self, spot, lines, base, win, wout):
        self.spot, self.lines, self.base = spot, lines, base
        self.win, self.wout = win, wout
        self.like = win.at[0, 0, 0]
        self.senders = {}

    def along_z(self, block, hop, number):
        s, n, b = self.spot, self.lines, self.base
        zk = s.z ^ block
        for i, part in ((0, self.win), (1, self.wout)):
            ref = part.at[zk, s.x, s.y]
            when = None if block == 0 and hop == 1 else s.inner
            n.send(b + 2 * number - 2 + i, ref, ref, s.z_mate(hop), like=self.like, when=when)

    def start_z(self):
        self.along_z(0, 1, 1)
        pl.when(self.spot.inner)(lambda: self.along_z(0, 3, 3))

    def start_x(self):
        s, n, b = self.spot, self.lines, self.base
        own = self.wout.at[s.z, s.x, s.y]
        n.send(b + 9, own, own, s.x_mate())
        own = self.win.at[s.z, s.x]
        n.send(b + 13, own, own, s.x_mate())

    def arrive(self, k):
        s, n, b = self.spot, self.lines, self.base
        zk = s.z ^ k
        a, c = self.win.at[zk, s.x, s.y], self.wout.at[zk, s.x, s.y]
        n.wait(b + 2 * k - 2, a, s.z_mate(k))
        n.wait(b + 2 * k - 1, c, s.z_mate(k))
        hop, number = {1: (3, 2), 3: (1, 2), 2: (1, 3)}[k]
        return lambda: self.along_z(k, hop, number)

    def second(self, k):
        s, n, b = self.spot, self.lines, self.base
        zk = s.z ^ k
        a, c = self.win.at[zk, s.x, s.y], self.wout.at[zk, s.x, s.y]
        steps = [(b + 5 + k, a, s.y_mate()), (b + 9 + k, c, s.x_mate()), (b + 17 + 2 * k, c, s.y_mate())]
        if k in self.split:
            steps.append((b + 13 + k, a, s.x_mate()))
        for i, (number, ref, device) in enumerate(steps):
            known = self.senders.get((k, i))
            used = n.send(number, ref, ref, device, sender=known, like=self.like, keep=known is None)
            self.senders[(k, i)] = used

    def early(self):
        onward = self.arrive(1)
        pl.when(self.spot.inner)(onward)
        self.second(1)

        def near():
            self.arrive(3)()
            self.second(3)

        pl.when(self.spot.inner)(near)

    def late(self):
        onward = self.arrive(2)
        pl.when(self.spot.inner)(onward)
        self.second(2)

    def last(self):
        def far():
            self.arrive(3)
            self.second(3)

        pl.when(jnp.logical_not(self.spot.inner))(far)

    def third(self, k):
        s, n, b = self.spot, self.lines, self.base
        zk = s.z ^ k
        far = self.wout.at[zk, 1 - s.x, s.y]
        n.wait(b + 9 + k, far, s.x_mate())
        n.send(b + 18 + 2 * k, far, far, s.y_mate())
        if k:
            n.wait(b + 5 + k, self.win.at[zk, s.x, 1 - s.y], s.y_mate())
        if k in self.split:
            far = self.win.at[zk, 1 - s.x, s.y]
            n.wait(b + 13 + k, far, s.x_mate())
            n.send(b + 25 + k, far, far, s.y_mate())
        elif k:
            n.send(b + 13 + k, self.win.at[zk, s.x], self.win.at[zk, s.x], s.x_mate())

    def finish(self, k):
        s, n, b = self.spot, self.lines, self.base
        zk = s.z ^ k
        if k in self.split:
            n.wait(b + 25 + k, self.win.at[zk, 1 - s.x, 1 - s.y], s.y_mate())
        else:
            n.wait(b + 13 + k, self.win.at[zk, 1 - s.x], s.x_mate())
        if k:
            n.wait(b + 17 + 2 * k, self.wout.at[zk, s.x, 1 - s.y], s.y_mate())
        n.wait(b + 18 + 2 * k, self.wout.at[zk, 1 - s.x, 1 - s.y], s.y_mate())


GATHER_LINES = 29


class Reduce:
    def __init__(self, spot, lines, base, parts, yins, zin, result):
        self.spot, self.lines, self.base = spot, lines, base
        self.parts, self.yins, self.zin, self.result = parts, yins, zin, result
        self.blocks = (jnp.where(spot.inner, 2, 3), jnp.where(spot.inner, 3, 2), 1, 0)
        self.like = parts[0].at[0, 0]

    def first(self, ready):
        s, n, b = self.spot, self.lines, self.base
        order = ((0, 0), (0, 1)) if ready == 0 else ((1, 0), (1, 1), (0, 2), (1, 2), (0, 3), (1, 3))
        for i, step in order:
            k = self.blocks[step]
            n.send(b + 2 * k + i, self.parts[i].at[s.z ^ k, 1 - s.y], self.yins[i].at[k], s.y_mate())

    def add(self, ref, more):
        ref[...] = (ref[...].astype(F32) + more[...].astype(F32)).astype(BF16)

    def take(self, slot, i):
        self.lines.wait(self.base + 8 + 2 * slot + i, self.zin.at[slot, i], self.spot.z_mate(1))
        return self.zin.at[slot, i]

    def second(self, first, last):
        for at in range(first, last):
            step, i = at // 2, at % 2
            self.step(step, i)

    def step(self, step, i):
        s, n, b = self.spot, self.lines, self.base
        k = self.blocks[step]
        ref, more = self.parts[i].at[s.z ^ k, s.y], self.yins[i].at[k]
        n.wait(b + 2 * k + i, more, s.y_mate())
        self.add(ref, more)
        if step == 3:
            return
        sender = n.next
        n.next += 1
        n.sent.append((sender, self.like, None))

        def onward(slot, device):
            number = b + 8 + 2 * slot + i
            n.send(number, ref, self.zin.at[slot, i], device, sender=sender, like=self.like, keep=False)

        def at_end():
            onward(step, s.z_mate(1))

        def inside():
            come, slot, hop = ((0, 4, 3), (1, 3, 3), (4, 5, 1))[step]
            self.add(ref, self.take(come, i))
            onward(slot, s.z_mate(hop))

        pl.when(s.inner)(inside)
        pl.when(jnp.logical_not(s.inner))(at_end)

    def third(self):
        s, n, b = self.spot, self.lines, self.base
        for i in (0, 1):

            def total(slots):
                value = self.parts[i][s.z, s.y].astype(F32)
                for slot in slots:
                    value = value + self.take(slot, i)[...].astype(F32)
                self.result[i, s.y] = value.astype(BF16)

            pl.when(s.inner)(lambda: total((2, 3)))
            pl.when(jnp.logical_not(s.inner))(lambda: total((5,)))
            n.send(b + 20 + i, self.result.at[i, s.y], self.result.at[i, s.y], s.y_mate())

    def finish(self):
        s, n, b = self.spot, self.lines, self.base
        for i in (0, 1):
            n.wait(b + 20 + i, self.result.at[i, 1 - s.y], s.y_mate())


REDUCE_LINES = 22
MATE_LINES = 8
SEND_LINES = 200


def normalize(value):
    centre = value - jnp.mean(value, axis=-1, keepdims=True)
    scale = lax.rsqrt(jnp.mean(centre * centre, axis=-1, keepdims=True) + EPS_NORM)
    return centre * scale, scale


def normalize_back(grad, gain, unit, scale):
    gain_grad = jnp.sum(grad * unit, axis=0, keepdims=True)
    shift_grad = jnp.sum(grad, axis=0, keepdims=True)
    inner = grad * gain
    mean = jnp.mean(inner, axis=-1, keepdims=True)
    along = jnp.mean(inner * unit, axis=-1, keepdims=True)
    return scale * (inner - mean - unit * along), gain_grad, shift_grad


def dot(left, right):
    return jnp.dot(left, right, preferred_element_type=F32)


def dot_t(left, right):
    return lax.dot_general(left, right, (((1,), (1,)), ((), ())), preferred_element_type=F32)


def t_dot(left, right):
    return lax.dot_general(left, right, (((0,), (0,)), ((), ())), preferred_element_type=F32)


def pick(rows, columns, where):
    at = [lax.broadcasted_iota(jnp.int32, (rows, columns), axis) for axis in (0, 1)]
    return where(*at).astype(F32).astype(BF16)


def gelu_pair(v):
    root = math.sqrt(2.0 / math.pi)
    square = v * v
    tanh = jnp.tanh(root * v * (1.0 + 0.044715 * square))
    half = 0.5 + 0.5 * tanh
    slope = half + 0.5 * v * (1.0 - tanh * tanh) * (root * (1.0 + 3 * 0.044715 * square))
    return v * half, slope


def fused_kernel(
    plan,
    tokens, cotangent_far, win_far, wout_far, bias, vec, packed_far, rebuild_far, turn, wave_far,
    act_out, grad_out, weights_out, piece_out, vec_out, norm_out,
    cotangent, win_own, wout_own, packed, rebuild, wave, local_sems,
    win, wout, bias_own, bias_all, hidden, acts, slopes, unit_mix, unit_out, scale_mix, scale_out, start, keep,
    branch_send, branch_recv, grad_branch, grad_pre, far_acts, far_pre,
    din, dout, yin, yout, zin, result,
    send, recv, work, send_back, recv_back,
    tiles, tiles_in, piece, pieces, square_send, square_recv,
    mix_sems, all_sems, send_sems, recv_sems,
):
    spot = Spot()
    lines = Lines(send_sems, recv_sems)
    parts, feats, rows = plan.parts, plan.feats, plan.rows
    me = spot.me
    hid = FF // parts
    group = 2 * hid
    barrier = pltpu.get_barrier_semaphore()

    devices = 2 * parts
    here = spot.y * parts + me

    def other(k):
        q = lax.rem(here + k, devices)
        return q, {"dp": q // parts, "mp": lax.rem(q, parts)}

    def everyone(action):
        def body(k, carry):
            action(k)
            return carry

        lax.fori_loop(1, devices, body, 0)

    everyone(lambda k: pl.semaphore_signal(barrier, inc=1, device_id=other(k)[1], device_id_type=MESH))

    loads = [
        pltpu.make_async_copy(src, dst, local_sems.at[i])
        for i, (src, dst) in enumerate(
            (
                (win_far.at[0], win_own.at[0]),
                (wout_far.at[0], wout_own.at[0]),
                (packed_far, packed),
                (wave_far, wave),
                (rebuild_far, rebuild),
                (win_far.at[1], win_own.at[1]),
                (wout_far.at[1], wout_own.at[1]),
                (cotangent_far, cotangent),
            )
        )
    ]
    for load in loads:
        load.start()

    base = 0
    gathers, reduces = [], []
    for l in range(LAYERS):
        gathers.append(Gather(spot, lines, base, win.at[l], wout.at[l]))
        base += GATHER_LINES
    for l in range(LAYERS):
        reduces.append(
            Reduce(
                spot, lines, base, (din.at[l], dout.at[l]), (yin.at[l], yout.at[l]), zin.at[l], result.at[l]
            )
        )
        base += REDUCE_LINES
    mates = []
    for l in range(LAYERS):
        mates.append(base)
        base += MATE_LINES
    bias_base = base

    def copy_to(k, src, dst, lane):
        q = lax.rem(me + k, parts)
        return pltpu.make_async_remote_copy(
            src_ref=src.at[q],
            dst_ref=dst.at[me],
            send_sem=mix_sems.at[lane, q],
            recv_sem=mix_sems.at[lane + 1, me],
            device_id={"mp": q},
            device_id_type=MESH,
        )

    def copy_from(k, src, dst, lane):
        p = lax.rem(me + k, parts)
        return pltpu.make_async_remote_copy(
            src_ref=src.at[p],
            dst_ref=dst.at[p],
            send_sem=mix_sems.at[lane, p],
            recv_sem=mix_sems.at[lane + 1, p],
            device_id={"mp": p},
            device_id_type=MESH,
        )

    def each(action):
        def body(k, carry):
            action(k)
            return carry

        lax.fori_loop(1, parts, body, 0)

    def mix_enter(value):
        send[...] = dot_t(packed[...], value).astype(BF16).reshape(parts, feats, rows)

    def mix_go():
        each(lambda k: copy_to(k, send, recv, 0).start())
        recv[me] = send[me]

    def mix_middle():
        each(lambda k: copy_from(k, send, recv, 0).wait_recv())
        position_dft(plan, me, recv, work, send_back, turn, wave)
        each(lambda k: copy_to(k, send_back, recv_back, 2).start())
        recv_back[me] = send_back[me]

    def mix_leave():
        each(lambda k: copy_from(k, send_back, recv_back, 2).wait_recv())
        mixed = t_dot(recv_back[...].reshape(parts * feats, rows), rebuild[...])
        each(lambda k: copy_to(k, send, recv, 0).wait_send())
        each(lambda k: copy_to(k, send_back, recv_back, 2).wait_send())
        return mixed * (1.0 / math.sqrt(L * D))

    eye = pick(hid, 256, lambda i, j: i == j)

    def bias_column(l, zk, x):
        return dot_t(eye, bias_all[zk, x])[:, l : l + 1]

    def own_weights(l):
        win[l, spot.z, spot.x] = win_own[l].astype(BF16).reshape(2, hid // 2, D)
        wout[l, spot.z, spot.x] = wout_own[l].astype(BF16).reshape(2, hid // 2, D)

    def swap_branch(number, slot):
        ref, land = branch_send.at[slot], branch_recv.at[slot]
        return lines.send(number, ref, land, spot.core_mate(), keep=False)

    def hidden_away(l):
        lines.send(mates[l] + 4, hidden.at[l, 0], hidden.at[l, 2], spot.x_mate())

    def forward(l, current, mixed, per_group):
        unit, scale = normalize(current + mixed)
        unit_mix[l] = unit
        scale_mix[l] = scale
        normed = unit * vec[0, l : l + 1] + vec[1, l : l + 1]
        keep[...] = normed
        hidden[l, 0] = normed.astype(BF16)
        lines.send(mates[l], hidden.at[l, 0], hidden.at[l, 1], spot.core_mate())
        for k in range(4):
            per_group(k)
            zk = spot.z ^ k
            weights = win[l, zk].reshape(group, D)
            column = jnp.concatenate([bias_column(l, zk, x) for x in (0, 1)], axis=0)
            for slot in (0, 1):
                if k == 0 and slot == 1:
                    lines.wait(mates[l], hidden.at[l, 1], spot.core_mate())
                value, slope = gelu_pair(dot_t(weights, hidden[l, slot]) + column)
                span = slice(slot * rows, (slot + 1) * rows)
                acts[l, zk, :, :, span] = value.astype(BF16).reshape(2, hid, rows)
                slopes[l, zk, :, :, span] = slope.astype(BF16).reshape(2, hid, rows)
        if l == LAYERS - 1:
            hidden_away(l)
        outs = wout[l].reshape(FF // 2, D)
        branch_send[0] = t_dot(acts[l, :, :, :, rows : 2 * rows].reshape(FF // 2, rows), outs).astype(BF16)
        sender = swap_branch(mates[l] + 1, 0)
        branch = t_dot(acts[l, :, :, :, 0:rows].reshape(FF // 2, rows), outs)
        lines.wait(mates[l] + 1, branch_recv.at[0], spot.core_mate())
        total = keep[...] + branch + branch_recv[0].astype(F32) + vec[2, l : l + 1]
        unit, scale = normalize(total)
        unit_out[l] = unit
        scale_out[l] = scale
        lines.wait_sent(sender, branch_send.at[0], spot.core_mate())
        return unit * vec[3, l : l + 1] + vec[4, l : l + 1]

    def vec_put(l, i, value):
        for t in range(3):
            for j in (0, 1):
                at = 256 * t + 128 * j
                tiles[3 * (5 * l + i) + t, j : j + 1, :] = value[:, at : at + 128]

    def bias_put(l):
        ones = jnp.ones((16, 2 * rows), BF16)
        for zk in range(4):
            for x in (0, 1):
                row = dot_t(ones, grad_pre[zk, x])[0:1]
                for y in (0, 1):
                    to = y * parts + zk * 4 + x * 2 + spot.core
                    tiles[to, 2 + 2 * l : 3 + 2 * l, :] = row[:, 0:128]
                    tiles[to, 3 + 2 * l : 4 + 2 * l, 0 : hid - 128] = row[:, 128:hid]

    def from_x_mate(l):
        for i, part in ((4, hidden), (6, grad_branch)):
            lines.wait(mates[l] + i, part.at[l, 2], spot.x_mate())
            lines.send(mates[l] + i + 1, part.at[l, 2], part.at[l, 3], spot.core_mate())

    half = FF // 4

    def far_grads(l):
        ins = win[l, :, spot.x].reshape(half, D)
        outs = wout[l, :, spot.x].reshape(half, D)
        column = jnp.concatenate([bias_column(l, zk, spot.x) for zk in range(4)], axis=0)
        for slot in (2, 3):
            if slot == 3:
                for i, part in ((5, hidden), (7, grad_branch)):
                    lines.wait(mates[l] + i, part.at[l, 3], spot.core_mate())
            span = slice((slot - 2) * rows, (slot - 1) * rows)
            value, slope = gelu_pair(dot_t(ins, hidden[l, slot]) + column)
            far_acts[:, span] = value.astype(BF16)
            far_pre[:, span] = (dot_t(outs, grad_branch[l, slot]) * slope).astype(BF16)

    def weight_grads(l):
        for i, (near, far, part, out) in enumerate(
            (
                (grad_pre[:, spot.x], far_pre, hidden, din),
                (acts[l, :, spot.x], far_acts, grad_branch, dout),
            )
        ):
            total = dot(near.reshape(half, 2 * rows), part[l, 0:2].reshape(2 * rows, D))
            total = total + dot(far[...], part[l, 2:4].reshape(2 * rows, D))
            out[l] = total.astype(BF16).reshape(4, 2, hid // 2, D)
            reduces[l].first(i)

    def backward(l, grad, later):
        grad_total, gain_grad, shift_grad = normalize_back(grad, vec[3, l : l + 1], unit_out[l], scale_out[l])
        low = grad_total.astype(BF16)
        grad_branch[l, 0] = low
        lines.send(mates[l] + 2, grad_branch.at[l, 0], grad_branch.at[l, 1], spot.core_mate())
        lines.send(mates[l] + 6, grad_branch.at[l, 0], grad_branch.at[l, 2], spot.x_mate())
        keep[...] = grad_total
        vec_put(l, 2, jnp.sum(low.astype(F32), axis=0, keepdims=True))
        vec_put(l, 3, gain_grad)
        vec_put(l, 4, shift_grad)
        for slot in (0, 1):
            if slot == 1:
                lines.wait(mates[l] + 2, grad_branch.at[l, 1], spot.core_mate())
            span = slice(slot * rows, (slot + 1) * rows)
            for zk in range(4):
                grad_act = dot_t(wout[l, zk].reshape(group, D), grad_branch[l, slot]).reshape(2, hid, rows)
                grad_pre[zk, :, :, span] = (grad_act * slopes[l, zk, :, :, span].astype(F32)).astype(BF16)
        ins = win[l].reshape(FF // 2, D)
        branch_send[1] = t_dot(grad_pre[:, :, :, rows : 2 * rows].reshape(FF // 2, rows), ins).astype(BF16)
        sender = swap_branch(mates[l] + 3, 1)
        grad_normed = t_dot(grad_pre[:, :, :, 0:rows].reshape(FF // 2, rows), ins)
        bias_put(l)
        later()
        lines.wait(mates[l] + 3, branch_recv.at[1], spot.core_mate())
        grad_normed = keep[...] + grad_normed + branch_recv[1].astype(F32)
        lines.wait_sent(sender, branch_send.at[1], spot.core_mate())
        grad_summed, gain_grad, shift_grad = normalize_back(grad_normed, vec[0, l : l + 1], unit_mix[l], scale_mix[l])
        vec_put(l, 0, gain_grad)
        vec_put(l, 1, shift_grad)
        return grad_summed

    inner = plan.inner

    def to_local(i, j):
        return j == parts * (i % inner) + i // inner

    for load in loads[:2]:
        load.wait()
    own_weights(0)
    bias_own[...] = jnp.zeros_like(bias_own)
    bias_own[0:LAYERS, 0:hid] = bias[...]
    bias_all[spot.z, spot.x] = bias_own[...].astype(BF16)
    tiles[...] = jnp.zeros_like(tiles)
    pl.semaphore_wait(barrier, devices - 1)
    gathers[0].start_z()
    gathers[0].start_x()
    local = dot(pick(rows, rows, to_local), tokens[...])
    start[...] = local
    for load in loads[2:4]:
        load.wait()
    mix_enter(local.astype(BF16))
    mix_go()
    for j in range(1, 8):
        far = spot.own ^ j
        own = bias_all.at[spot.z, spot.x]
        lines.send(bias_base + j, own, own, {"dp": spot.y, "mp": far * 2 + spot.core})
    for load in loads[4:]:
        load.wait()
    own_weights(1)
    gathers[0].early()
    gathers[0].third(0)
    gathers[0].late()
    gathers[0].third(1)
    mix_middle()
    gathers[0].last()
    gathers[1].start_z()
    gathers[0].third(2)
    gathers[0].third(3)
    gathers[1].start_x()
    for j in range(1, 8):
        far = spot.own ^ j
        lines.wait(bias_base + j, bias_all.at[far // 2, far % 2], {"dp": spot.y, "mp": far * 2 + spot.core})
    mixed = mix_leave()

    def between(k):
        if k == 2:
            gathers[1].early()
        gathers[0].finish(k)

    current = forward(0, start[...], mixed, between)
    start[...] = current
    mix_enter(current.astype(BF16))
    mix_go()
    gathers[1].third(0)
    gathers[1].late()
    gathers[1].third(1)
    gathers[1].last()
    gathers[1].third(2)
    mix_middle()
    gathers[1].third(3)
    mixed = mix_leave()
    current = forward(1, start[...], mixed, lambda k: gathers[1].finish(k))
    act_out[...] = t_dot(pick(rows, rows, to_local), current.astype(BF16)).astype(BF16)

    grad = backward(1, dot(pick(rows, rows, to_local), cotangent[...]), lambda: None)
    start[...] = grad
    mix_enter(grad.astype(BF16))
    mix_go()
    from_x_mate(1)
    far_grads(1)
    mix_middle()
    hidden_away(0)
    weight_grads(1)
    mixed = mix_leave()
    grad = backward(0, start[...] + mixed, lambda: reduces[1].second(0, 4))

    def tile_to(k):
        q, device = other(k)
        return pltpu.make_async_remote_copy(
            src_ref=tiles.at[q], dst_ref=tiles_in.at[here], send_sem=all_sems.at[0, q], recv_sem=all_sems.at[1, here],
            device_id=device, device_id_type=MESH,
        )

    def tile_from(k):
        p, device = other(k)
        return pltpu.make_async_remote_copy(
            src_ref=tiles.at[p], dst_ref=tiles_in.at[p], send_sem=all_sems.at[0, p], recv_sem=all_sems.at[1, p],
            device_id=device, device_id_type=MESH,
        )

    everyone(lambda k: tile_to(k).start())
    tiles_in[here] = tiles[here]
    start[...] = grad
    mix_enter(grad.astype(BF16))
    mix_go()
    from_x_mate(0)
    far_grads(0)
    reduces[1].second(4, 8)
    weight_grads(0)
    reduces[1].third()
    reduces[0].second(0, 4)
    mix_middle()
    reduces[0].second(4, 8)
    everyone(lambda k: tile_from(k).wait_recv())
    total = tiles_in[0]
    for d in range(1, devices):
        total = total + tiles_in[d]
    piece_out[...] = total
    piece[...] = total

    def piece_to(k):
        q, device = other(k)
        return pltpu.make_async_remote_copy(
            src_ref=piece, dst_ref=pieces.at[here], send_sem=all_sems.at[2, q], recv_sem=all_sems.at[3, here],
            device_id=device, device_id_type=MESH,
        )

    def piece_from(k):
        p, device = other(k)
        return pltpu.make_async_remote_copy(
            src_ref=piece, dst_ref=pieces.at[p], send_sem=all_sems.at[2, p], recv_sem=all_sems.at[3, p],
            device_id=device, device_id_type=MESH,
        )

    everyone(lambda k: piece_to(k).start())
    pieces[here] = total
    reduces[1].finish()
    weights_out[1] = result[1]
    mixed = mix_leave()
    grad = start[...] + mixed
    back = pick(rows, rows, lambda i, j: to_local(j, i))
    high = grad.astype(BF16)
    rest = grad - high.astype(F32)
    middle = rest.astype(BF16)
    low = (rest - middle.astype(F32)).astype(BF16)
    grad = dot(back, high) + (dot(back, middle) + dot(back, low))
    for t in range(D // 128):
        grad_out[pl.ds(t, rows, stride=D // 128), :] = grad[:, 128 * t : 128 * (t + 1)]

    def squares(ref):
        value = ref[...].reshape(hid, D).astype(F32)
        return jnp.sum(value * value, axis=(0, 1), keepdims=True)

    row = lax.broadcasted_iota(jnp.int32, total.shape, 0)
    local = jnp.sum(jnp.where((row >= 2) & (row < 6), total * total, 0.0), axis=(0, 1), keepdims=True)
    local = local + squares(result.at[1, 0]) + squares(result.at[1, 1])
    reduces[0].third()
    reduces[0].finish()
    weights_out[0] = result[0]
    local = local + squares(result.at[0, 0]) + squares(result.at[0, 1])
    square_send[...] = jnp.broadcast_to(local, square_send.shape)

    def square_to(k):
        q = lax.rem(me + k, parts)
        return pltpu.make_async_remote_copy(
            src_ref=square_send, dst_ref=square_recv.at[me], send_sem=all_sems.at[4, q], recv_sem=all_sems.at[5, me],
            device_id={"mp": q}, device_id_type=MESH,
        )

    def square_from(k):
        p = lax.rem(me + k, parts)
        return pltpu.make_async_remote_copy(
            src_ref=square_send, dst_ref=square_recv.at[p], send_sem=all_sems.at[4, p], recv_sem=all_sems.at[5, p],
            device_id={"mp": p}, device_id_type=MESH,
        )

    each(lambda k: square_to(k).start())
    square_recv[me] = square_send[...]
    everyone(lambda k: tile_to(k).wait_send())
    lines.drain(spot.core_mate())
    everyone(lambda k: piece_from(k).wait_recv())
    for l in range(LAYERS):
        for i in range(5):
            for t in range(3):
                for j in (0, 1):
                    at = 256 * t + 128 * j
                    vec_out[i, l : l + 1, at : at + 128] = pieces[3 * (5 * l + i) + t, j : j + 1, :]
    every = jnp.sum(jnp.where(row < 2, pieces[...] * pieces[...], 0.0), axis=0)
    norms = jnp.sum(every, axis=(0, 1), keepdims=True)
    each(lambda k: square_from(k).wait_recv())
    norms = norms + jnp.sum(square_recv[...], axis=0)[0:1, 0:1]
    norm_out[...] = jnp.broadcast_to(jnp.sqrt(norms), norm_out.shape)
    everyone(lambda k: piece_to(k).wait_send())
    each(lambda k: square_to(k).wait_send())


def fused(plan, tokens, cotangent, weight_in, weight_out, bias_in, vec):
    parts, feats, rows = plan.parts, plan.feats, plan.rows
    block = (parts, feats, rows)
    hid = FF // parts
    half = hid // 2
    vm = pltpu.VMEM
    near, far = pl.BlockSpec(memory_space=vm), pl.BlockSpec(memory_space=pl.ANY)
    line_count = LAYERS * (GATHER_LINES + REDUCE_LINES + MATE_LINES) + 8
    return pl.pallas_call(
        functools.partial(fused_kernel, plan),
        out_shape=(
            jax.ShapeDtypeStruct((rows, D), BF16),
            jax.ShapeDtypeStruct((rows * D // 128, 128), F32),
            jax.ShapeDtypeStruct((LAYERS, 2, 2, half, D), BF16),
            jax.ShapeDtypeStruct((8, 128), F32),
            jax.ShapeDtypeStruct((5, LAYERS, D), F32),
            jax.ShapeDtypeStruct((8, 128), F32),
        ),
        in_specs=[near, far, far, far, near, near, far, far, near, far],
        out_specs=[near] * 6,
        scratch_shapes=[
            vm((rows, D), BF16),
            vm((LAYERS, hid, D), F32),
            vm((LAYERS, hid, D), F32),
            vm((parts * feats, D), BF16),
            vm((parts * feats, D), BF16),
            vm((2 * rows, rows), BF16),
            pltpu.SemaphoreType.DMA((8,)),
            vm((LAYERS, 4, 2, 2, half, D), BF16),
            vm((LAYERS, 4, 2, 2, half, D), BF16),
            vm((16, 256), F32),
            vm((4, 2, 16, 256), BF16),
            vm((LAYERS, 4, rows, D), BF16),
            vm((LAYERS, 4, 2, hid, 2 * rows), BF16),
            vm((LAYERS, 4, 2, hid, 2 * rows), BF16),
            vm((LAYERS, rows, D), F32),
            vm((LAYERS, rows, D), F32),
            vm((LAYERS, rows, 1), F32),
            vm((LAYERS, rows, 1), F32),
            vm((rows, D), F32),
            vm((rows, D), F32),
            vm((2, rows, D), BF16),
            vm((2, rows, D), BF16),
            vm((LAYERS, 4, rows, D), BF16),
            vm((4, 2, hid, 2 * rows), BF16),
            vm((FF // 4, 2 * rows), BF16),
            vm((FF // 4, 2 * rows), BF16),
            vm((LAYERS, 4, 2, half, D), BF16),
            vm((LAYERS, 4, 2, half, D), BF16),
            vm((LAYERS, 4, half, D), BF16),
            vm((LAYERS, 4, half, D), BF16),
            vm((LAYERS, 6, 2, half, D), BF16),
            vm((LAYERS, 2, 2, half, D), BF16),
            vm(block, BF16),
            vm(block, BF16),
            vm((parts, feats, 2 * rows), BF16),
            vm(block, BF16),
            vm(block, BF16),
            vm((2 * parts, 8, 128), F32),
            vm((2 * parts, 8, 128), F32),
            vm((8, 128), F32),
            vm((2 * parts, 8, 128), F32),
            vm((8, 128), F32),
            vm((parts, 8, 128), F32),
            pltpu.SemaphoreType.DMA((4, parts)),
            pltpu.SemaphoreType.DMA((6, 2 * parts)),
            pltpu.SemaphoreType.DMA((SEND_LINES,)),
            pltpu.SemaphoreType.DMA((line_count,)),
        ],
        compiler_params=pltpu.CompilerParams(collective_id=1, has_side_effects=True, vmem_limit_bytes=62 * 2**20),
    )(tokens, cotangent, weight_in, weight_out, bias_in, vec, plan.packed, plan.rebuild, plan.turn, plan.wave)


def update_kernel(
    norm, bias, moment_bias, square_bias, piece, vec, moment_vec, square_vec, sum_vec, change, *refs
):
    ins, (acts, grad) = refs[0:6], refs[6:8]
    outs, (acts_out, grad_out) = refs[8:16], refs[16:18]
    m_bias, v_bias, b_new, m_vec, v_vec, vec_new, norm_out = refs[18:25]
    near_ins, near_outs, near_through, sems = refs[25:31], refs[31:39], refs[39:41], refs[41]
    hid = bias.shape[1]
    part = hid // 2
    pieces = [(l, kind, h) for l in range(LAYERS) for kind in (0, 1) for h in (0, 1)]

    def copies(at, out):
        l, kind, h = pieces[at]
        span = pl.ds(h * part, part)
        if out:
            pairs = zip(near_outs[4 * kind : 4 * kind + 4], outs[4 * kind : 4 * kind + 4])
        else:
            pairs = zip(ins[3 * kind : 3 * kind + 3], near_ins[3 * kind : 3 * kind + 3])
        return [
            pltpu.make_async_copy(src.at[l, span], dst.at[l, span], sems.at[int(out), at, i])
            for i, (src, dst) in enumerate(pairs)
        ]

    last = len(pieces)
    through_in = [pltpu.make_async_copy(src, near_through[i], sems.at[0, last, i]) for i, src in enumerate((acts, grad))]
    through_out = [
        pltpu.make_async_copy(near_through[i], dst, sems.at[1, last, i]) for i, dst in enumerate((acts_out, grad_out))
    ]
    for at in range(len(pieces)):
        for copy in copies(at, False):
            copy.start()
    for copy in through_in:
        copy.start()
    factor = jnp.minimum(1.0, CLIP / norm[0:1, 0:1])
    norm_out[0, 0] = norm[0, 0]
    for l in range(LAYERS):
        row = jnp.concatenate([piece[2 + 2 * l : 3 + 2 * l, :], piece[3 + 2 * l : 4 + 2 * l, 0 : hid - 128]], axis=1)
        here = slice(l, l + 1)
        news = adamw(bias[here], row * factor, moment_bias[here], square_bias[here], 0.5, 0.0)
        for out, value in zip((m_bias, v_bias, b_new), news):
            out[here] = value
    news = adamw(vec[...], sum_vec[...] * factor, moment_vec[...], square_vec[...], 0.5, 0.0)
    for out, value in zip((m_vec, v_vec, vec_new), news):
        out[...] = value
    for at, (l, kind, h) in enumerate(pieces):
        for copy in copies(at, False):
            copy.wait()
        span = slice(h * part, (h + 1) * part)
        weight, moment, square = [ref[l, span] for ref in near_ins[3 * kind : 3 * kind + 3]]
        width = (D, FF)[kind]
        news = adamw(
            weight, change[l, kind, h].astype(F32) * factor, moment, square, 1.0 / math.sqrt(width), DECAY
        )
        for out, value in zip(near_outs[4 * kind : 4 * kind + 4], news + (news[2].astype(BF16),)):
            out[l, span] = value
        for copy in copies(at, True):
            copy.start()
    for copy_in, copy_out in zip(through_in, through_out):
        copy_in.wait()
        copy_out.start()
    for at in range(len(pieces)):
        for copy in copies(at, True):
            copy.wait()
    for copy in through_out:
        copy.wait()


def update(norm, bias, moment_bias, square_bias, piece, vec, moment_vec, square_vec, sum_vec, change, *far):
    near, out = pl.BlockSpec(memory_space=pltpu.VMEM), pl.BlockSpec(memory_space=pl.ANY)
    weight, acts, grad = far[0], far[6], far[7]

    def shape(value, dtype=F32):
        return jax.ShapeDtypeStruct(value.shape, dtype)

    kinds = (F32, F32, F32, BF16) * 2
    return pl.pallas_call(
        update_kernel,
        out_shape=tuple(shape(weight, kind) for kind in kinds)
        + (shape(acts, BF16), shape(grad))
        + (shape(bias),) * 3
        + (shape(vec),) * 3
        + (jax.ShapeDtypeStruct((1, 1), F32),),
        in_specs=[near] * 10 + [out] * 8,
        out_specs=[out] * 10 + [near] * 6 + [pl.BlockSpec(memory_space=pltpu.SMEM)],
        scratch_shapes=[pltpu.VMEM(weight.shape, F32)] * 6
        + [pltpu.VMEM(weight.shape, kind) for kind in kinds]
        + [pltpu.VMEM(acts.shape, BF16), pltpu.VMEM(grad.shape, F32)]
        + [pltpu.SemaphoreType.DMA((2, 9, 4))],
        compiler_params=pltpu.CompilerParams(vmem_limit_bytes=62 * 2**20),
    )(norm, bias, moment_bias, square_bias, piece, vec, moment_vec, square_vec, sum_vec, change, *far)


def on_block(
    tokens, cotangent, weight_in, bias_in, weight_out, vectors, moment_in, square_in,
    moment_bias, square_bias, moment_out, square_out, moment_vec, square_vec,
):
    rows = tokens.shape[0]
    plan = Plan(L // rows)

    def turned(value):
        return jnp.swapaxes(value, 1, 2)

    def by_kind(value):
        return jnp.swapaxes(value, 0, 1)

    win, vec = turned(weight_in), by_kind(vectors)
    acts, grad, grads, piece, sum_vec, norm = fused(
        plan, tokens.reshape(rows, D), cotangent.reshape(rows, D), win, weight_out, bias_in, vec
    )
    (
        m_in, v_in, w_in, low_in, m_out, v_out, w_out, low_out, acts, grad,
        m_bias, v_bias, b_new, m_vec, v_vec, vec_new, norm,
    ) = update(
        norm, bias_in, moment_bias, square_bias, piece, vec, by_kind(moment_vec), by_kind(square_vec), sum_vec, grads,
        win, turned(moment_in), turned(square_in), weight_out, moment_out, square_out, acts, grad,
    )
    return (
        acts.reshape(rows, 1, D),
        grad.reshape(rows, 1, D),
        norm[0, 0],
        turned(m_in),
        turned(v_in),
        turned(w_in),
        turned(low_in),
        m_out,
        v_out,
        w_out,
        low_out,
        m_bias,
        v_bias,
        b_new,
        by_kind(m_vec),
        by_kind(v_vec),
        by_kind(vec_new),
    )


def matmul(left_op, right_op):
    return jnp.dot(left_op, right_op, preferred_element_type=jnp.float32)


def inner_rows(left_op, right_op):
    return lax.dot_general(
        left_op, right_op, (((0,), (0,)), ((), ())), preferred_element_type=jnp.float32
    )


def inner_cols(left_op, right_op):
    return lax.dot_general(
        left_op, right_op, (((1,), (1,)), ((), ())), preferred_element_type=jnp.float32
    )


def layer_norm(value, gain, shift):
    centre = value - jnp.mean(value, axis=-1, keepdims=True)
    spread = jnp.mean(centre * centre, axis=-1, keepdims=True)
    return centre * lax.rsqrt(spread + EPS_NORM) * gain + shift


def adamw(weight, grad, moment, square, rate, decay):
    new_moment = BETA_ONE * moment + (1.0 - BETA_ONE) * grad
    new_square = BETA_TWO * square + (1.0 - BETA_TWO) * grad * grad
    moment_hat = new_moment / (1.0 - BETA_ONE**STEP)
    square_hat = new_square / (1.0 - BETA_TWO**STEP)
    new_weight = weight - rate * (moment_hat / (jnp.sqrt(square_hat) + EPS_ADAM) + decay * weight)
    return (new_moment, new_square, new_weight)


def on_device(
    tokens,
    cotangent,
    weight_in,
    bias_in,
    weight_out,
    vectors,
    moment_in,
    square_in,
    moment_bias,
    square_bias,
    moment_out,
    square_out,
    moment_vec,
    square_vec,
):
    row_count, seq_count, feat_count = tokens.shape
    plan = Plan(L // row_count)

    def localize(value):
        return jnp.swapaxes(value.reshape(plan.inner, plan.parts, -1), 0, 1).reshape(value.shape)

    def restore(value):
        return jnp.swapaxes(value.reshape(plan.parts, plan.inner, -1), 0, 1).reshape(value.shape)

    current = localize(tokens).astype(jnp.float32)
    saved = []
    for layer_at in range(LAYERS):
        vector_set = vectors[layer_at]
        rounded = current.astype(jnp.bfloat16)
        mixed = mix(plan, rounded.reshape(row_count, feat_count)).reshape(row_count, seq_count, feat_count)
        summed = current + mixed
        normed = layer_norm(summed, vector_set[0], vector_set[1])
        hidden_in = normed.astype(jnp.bfloat16)
        weight_one = weight_in[layer_at].astype(jnp.bfloat16)
        weight_two = weight_out[layer_at].astype(jnp.bfloat16)
        bias_one = bias_in[layer_at].astype(jnp.bfloat16)
        whole_one, whole_two, whole_bias = (
            lax.all_gather(weight_one, "mp", axis=1, tiled=True),
            lax.all_gather(weight_two, "mp", axis=0, tiled=True),
            lax.all_gather(bias_one, "mp", axis=0, tiled=True),
        )
        inputs = hidden_in.reshape(-1, feat_count)
        pre_act = matmul(inputs, whole_one) + whole_bias.astype(jnp.float32)
        acts = jax.nn.gelu(pre_act).astype(jnp.bfloat16)
        branch = matmul(acts, whole_two).reshape(row_count, seq_count, feat_count)
        held = (inputs, whole_one, whole_two)
        total = normed + branch + vector_set[2]
        current = layer_norm(total, vector_set[3], vector_set[4])
        saved.append((summed, total, pre_act, acts, held))
    activations = restore(current.astype(jnp.bfloat16))
    grad = localize(cotangent).astype(jnp.float32)
    layer_grads = [None] * LAYERS
    for layer_at in reversed(range(LAYERS)):
        vector_set = vectors[layer_at]
        summed, total, pre_act, acts, held = saved[layer_at]
        inputs, mat_one, mat_two = held
        _, pull_out = jax.vjp(layer_norm, total, vector_set[3], vector_set[4])
        grad_total, gain_two, shift_two = pull_out(grad)
        grad_branch = grad_total.astype(jnp.bfloat16)
        grad_bias_two = jnp.sum(grad_branch.astype(jnp.float32), axis=(0, 1))
        flat_grad = grad_branch.reshape(-1, feat_count)
        grad_act = inner_cols(flat_grad, mat_two)
        _, pull_gelu = jax.vjp(jax.nn.gelu, pre_act)
        grad_pre = pull_gelu(grad_act)[0].astype(jnp.bfloat16)
        full_one = inner_rows(inputs, grad_pre)
        full_two = inner_rows(acts, flat_grad)
        full_bias = jnp.sum(grad_pre.astype(jnp.float32), axis=0)
        grad_one, grad_two, grad_bias_one = (
            lax.psum_scatter(
                full_one.astype(jnp.bfloat16), "mp", scatter_dimension=1, tiled=True
            ).astype(jnp.float32),
            lax.psum_scatter(
                full_two.astype(jnp.bfloat16), "mp", scatter_dimension=0, tiled=True
            ).astype(jnp.float32),
            lax.psum_scatter(
                full_bias.astype(jnp.bfloat16), "mp", scatter_dimension=0, tiled=True
            ).astype(jnp.float32),
        )
        grad_normed = inner_cols(grad_pre, mat_one).reshape(row_count, seq_count, feat_count)
        grad_normed = grad_normed + grad_total
        _, pull_in = jax.vjp(layer_norm, summed, vector_set[0], vector_set[1])
        grad_summed, gain_one, shift_one = pull_in(grad_normed)
        mix_grad = grad_summed.astype(jnp.bfloat16).reshape(-1, feat_count)
        grad_mix = mix(plan, mix_grad).reshape(row_count, seq_count, feat_count)
        grad = grad_summed + grad_mix
        layer_grads[layer_at] = (
            grad_one,
            grad_two,
            grad_bias_one,
            jnp.stack([gain_one, shift_one, grad_bias_two, gain_two, shift_two]),
        )
    stack_in = jnp.stack([entry[0] for entry in layer_grads])
    stack_out = jnp.stack([entry[1] for entry in layer_grads])
    stack_bias = jnp.stack([entry[2] for entry in layer_grads])
    stack_vec = jnp.stack([entry[3] for entry in layer_grads])
    sum_in, sum_out, sum_bias, sum_vec = (
        lax.psum(stack_in.astype(jnp.bfloat16), "dp").astype(jnp.float32),
        lax.psum(stack_out.astype(jnp.bfloat16), "dp").astype(jnp.float32),
        lax.psum(stack_bias.astype(jnp.bfloat16), "dp").astype(jnp.float32),
        lax.psum(stack_vec.astype(jnp.bfloat16), "dp").astype(jnp.float32),
    )
    local_squares = (
        jnp.sum(sum_in * sum_in) + jnp.sum(sum_out * sum_out) + jnp.sum(sum_bias * sum_bias)
    )
    sum_vec, total_squares = lax.psum((sum_vec, local_squares), "mp")
    grad_norm = jnp.sqrt(total_squares + jnp.sum(sum_vec * sum_vec))
    factor = jnp.minimum(1.0, CLIP / grad_norm)
    m_in, v_in, w_in = adamw(
        weight_in, sum_in * factor, moment_in, square_in, 1.0 / math.sqrt(D), DECAY
    )
    m_out, v_out, w_out = adamw(
        weight_out, sum_out * factor, moment_out, square_out, 1.0 / math.sqrt(FF), DECAY
    )
    m_bias, v_bias, b_new = adamw(bias_in, sum_bias * factor, moment_bias, square_bias, 0.5, 0.0)
    m_vec, v_vec, vec_new = adamw(vectors, sum_vec * factor, moment_vec, square_vec, 0.5, 0.0)
    return (
        activations,
        restore(grad),
        grad_norm,
        m_in,
        v_in,
        w_in,
        w_in.astype(jnp.bfloat16),
        m_out,
        v_out,
        w_out,
        w_out.astype(jnp.bfloat16),
        m_bias,
        v_bias,
        b_new,
        m_vec,
        v_vec,
        vec_new,
    )


def solution(mesh):
    body = on_block if (mesh.shape["dp"], mesh.shape["mp"]) == (2, 16) else on_device
    return jax.shard_map(
        body,
        mesh=mesh,
        in_specs=(
            P("mp", "dp", None),
            P("mp", "dp", None),
            P(None, None, "mp"),
            P(None, "mp"),
            P(None, "mp", None),
            P(),
            P(None, None, "mp"),
            P(None, None, "mp"),
            P(None, "mp"),
            P(None, "mp"),
            P(None, "mp", None),
            P(None, "mp", None),
            P(),
            P(),
        ),
        out_specs=(
            P("mp", "dp", None),
            P("mp", "dp", None),
            P(),
            P(None, None, "mp"),
            P(None, None, "mp"),
            P(None, None, "mp"),
            P(None, None, "mp"),
            P(None, "mp", None),
            P(None, "mp", None),
            P(None, "mp", None),
            P(None, "mp", None),
            P(None, "mp"),
            P(None, "mp"),
            P(None, "mp"),
            P(),
            P(),
            P(),
        ),
        check_vma=False,
    )
```

```python
import functools
import math

import jax
import jax.numpy as jnp
import ml_dtypes
import numpy as np
from jax import lax
from jax.experimental import pallas as pl
from jax.experimental.pallas import tpu as pltpu
from jax.sharding import PartitionSpec as P

D = 768
FF = 3072
L = 4096
LAYERS = 2
STEP = 5


CLIP = 1.0
BETA_ONE = 0.5
BETA_TWO = 0.5
EPS_ADAM = 1e-08
EPS_NORM = 1e-05
DECAY = 0.01
MESH = pl.DeviceIdType.MESH
F32 = jnp.float32
BF16 = jnp.bfloat16


class Plan:
    def __init__(self, parts):
        self.parts = parts
        self.rows = L // parts
        self.inner = self.rows // parts
        self.pairs = D // 2 // parts
        self.feats = -(-2 * self.pairs // 16) * 16
        rows, inner = self.rows, self.inner
        lane = np.arange(rows)
        self.place = parts * (lane % inner) + lane // inner
        packed = np.zeros((parts, self.feats, D))
        rebuild = np.zeros((parts, self.feats, D))
        n = np.arange(D)
        for at in range(parts):
            for i in range(self.pairs):
                m = self.pairs * at + i
                a, b = i, self.pairs + i
                packed[at, a] = np.cos(2 * np.pi * (m * n % D) / D)
                rebuild[at, a, m] = 1.0
                if m == 0:
                    packed[at, b] = np.cos(2 * np.pi * (D // 2 * n % D) / D)
                    rebuild[at, b, D // 2] = 1.0
                else:
                    packed[at, b] = np.sin(2 * np.pi * (m * n % D) / D)
                    rebuild[at, a, D - m] = 1.0
                    rebuild[at, b, m] = -1.0
                    rebuild[at, b, D - m] = 1.0
        bf = ml_dtypes.bfloat16
        self.packed = packed.reshape(-1, D).astype(bf)
        self.rebuild = rebuild.reshape(-1, D).astype(bf)
        turn = 2 * np.pi * (np.arange(parts)[:, None] * self.place[None, :] % L) / L
        self.turn = np.stack([np.cos(turn), np.sin(turn)]).astype(np.float32)
        angle = 2 * np.pi * (self.place[:, None] * np.arange(rows)[None, :] % rows) / rows
        self.wave = np.concatenate([np.cos(angle), np.sin(angle)]).astype(bf)


def half_dft(values):
    n = len(values)
    if n == 1:
        return [(values[0], None)]
    if n == 2:
        return [(values[0] + values[1], None), (values[0] - values[1], None)]
    even, odd = half_dft(values[0::2]), half_dft(values[1::2])
    half = n // 2
    result = [None] * (half + 1)
    for k in range(half // 2 + 1):
        er, ei = even[k]
        orr, oi = odd[k]
        if k == 0:
            result[0] = (er + orr, None)
            result[half] = (er - orr, None)
        elif 2 * k == half:
            result[k] = (er, -orr)
        else:
            c, s = math.cos(2 * math.pi * k / n), math.sin(2 * math.pi * k / n)
            tr, ti = orr * c + oi * s, oi * c - orr * s
            result[k] = (er + tr, ei + ti)
            result[half - k] = (er - tr, ti - ei)
    return result


def position_dft(plan, me, recv, work, send, turn_ref, wave_ref):
    parts, feats, rows, inner, pairs = plan.parts, plan.feats, plan.rows, plan.inner, plan.pairs
    chunk = 16
    lanes = min(rows, 128)
    for lane_at in range(0, rows, lanes):

        def body(i, carry):
            at = pl.multiple_of(i * chunk, chunk)
            values = [recv[p, pl.ds(at, chunk), lane_at : lane_at + lanes].astype(F32) for p in range(parts)]
            outs = half_dft(values)
            row = at + lax.broadcasted_iota(jnp.int32, (chunk, lanes), 0)
            is_sine = (row >= pairs) & jnp.logical_not((row == pairs) & (me == 0))
            for d in range(parts):
                re, im = outs[min(d, parts - d)]
                im = jnp.zeros_like(re) if im is None else im
                if d > parts - d:
                    im = -im
                re, im = jnp.where(is_sine, -im, re), jnp.where(is_sine, re, im)
                c = turn_ref[0, d : d + 1, lane_at : lane_at + lanes]
                s = turn_ref[1, d : d + 1, lane_at : lane_at + lanes]
                work[d, pl.ds(at, chunk), lane_at : lane_at + lanes] = (re * c + im * s).astype(BF16)
                work[d, pl.ds(at, chunk), rows + lane_at : rows + lane_at + lanes] = (im * c - re * s).astype(BF16)
            return carry

        lax.fori_loop(0, feats // chunk, body, 0)

    def swap(i, carry):
        at = pl.multiple_of(i * chunk, chunk)
        spectrum = jnp.dot(
            work[:, pl.ds(at, chunk), :].reshape(parts * chunk, 2 * rows), wave_ref[...], preferred_element_type=F32
        )
        outs = [spectrum[d * chunk : (d + 1) * chunk] for d in range(parts)]
        group = lax.broadcasted_iota(jnp.int32, (chunk, rows), 1) // inner
        bit = 1
        while bit < parts:
            upper = (group // bit) % 2 == 1
            for d in range(parts):
                if d & bit:
                    continue
                low, high = outs[d], outs[d | bit]
                shift = inner * bit
                outs[d] = jnp.where(upper, pltpu.roll(high, shift, 1), low)
                outs[d | bit] = jnp.where(upper, high, pltpu.roll(low, rows - shift, 1))
            bit *= 2
        for q in range(parts):
            send[q, pl.ds(at, chunk), :] = outs[q].astype(BF16)
        return carry

    lax.fori_loop(0, feats // chunk, swap, 0)


def exchange(plan, me, send, recv, send_sem, recv_sem):
    parts = plan.parts

    def copy_to(k):
        q = lax.rem(me + k, parts)
        return pltpu.make_async_remote_copy(
            src_ref=send.at[q],
            dst_ref=recv.at[me],
            send_sem=send_sem.at[q],
            recv_sem=recv_sem.at[me],
            device_id={"mp": q},
            device_id_type=MESH,
        )

    def copy_from(k):
        p = lax.rem(me + k, parts)
        return pltpu.make_async_remote_copy(
            src_ref=send.at[p],
            dst_ref=recv.at[p],
            send_sem=send_sem.at[p],
            recv_sem=recv_sem.at[p],
            device_id={"mp": p},
            device_id_type=MESH,
        )

    def start(k, carry):
        copy_to(k).start()
        return carry

    def finish(k, carry):
        copy_from(k).wait_recv()
        return carry

    def drain(k, carry):
        copy_to(k).wait_send()
        return carry

    lax.fori_loop(1, parts, start, 0)
    recv[me] = send[me]
    lax.fori_loop(1, parts, finish, 0)
    lax.fori_loop(1, parts, drain, 0)


def mix_kernel(plan, x_ref, packed_ref, rebuild_ref, turn_ref, wave_ref, out_ref, send, recv, work, send_back, recv_back, sems):
    me = lax.axis_index("mp")
    parts, feats, rows = plan.parts, plan.feats, plan.rows
    barrier = pltpu.get_barrier_semaphore()

    def greet(k, carry):
        pl.semaphore_signal(barrier, inc=1, device_id={"mp": lax.rem(me + k, parts)}, device_id_type=MESH)
        return carry

    lax.fori_loop(1, parts, greet, 0)
    pl.semaphore_wait(barrier, parts - 1)

    columns = lax.dot_general(packed_ref[...], x_ref[...], (((1,), (1,)), ((), ())), preferred_element_type=F32)
    send[...] = columns.astype(BF16).reshape(parts, feats, rows)
    exchange(plan, me, send, recv, sems.at[0], sems.at[1])
    position_dft(plan, me, recv, work, send_back, turn_ref, wave_ref)
    exchange(plan, me, send_back, recv_back, sems.at[2], sems.at[3])
    mixed = lax.dot_general(
        recv_back[...].reshape(parts * feats, rows), rebuild_ref[...], (((0,), (0,)), ((), ())), preferred_element_type=F32
    )
    out_ref[...] = mixed * (1.0 / math.sqrt(L * D))


def mix(plan, value):
    block = (plan.parts, plan.feats, plan.rows)
    return pl.pallas_call(
        functools.partial(mix_kernel, plan),
        out_shape=jax.ShapeDtypeStruct((plan.rows, D), F32),
        in_specs=[pl.BlockSpec(memory_space=pltpu.VMEM)] * 5,
        out_specs=pl.BlockSpec(memory_space=pltpu.VMEM),
        scratch_shapes=[
            pltpu.VMEM(block, BF16),
            pltpu.VMEM(block, BF16),
            pltpu.VMEM((plan.parts, plan.feats, 2 * plan.rows), BF16),
            pltpu.VMEM(block, BF16),
            pltpu.VMEM(block, BF16),
            pltpu.SemaphoreType.DMA((4, plan.parts)),
        ],
        compiler_params=pltpu.CompilerParams(
            collective_id=0, has_side_effects=True, vmem_limit_bytes=40 * 2**20
        ),
    )(value, plan.packed, plan.rebuild, plan.turn, plan.wave)


class Spot:
    def __init__(self):
        self.y = lax.axis_index("dp")
        self.me = lax.axis_index("mp")
        self.z, self.x, self.core = self.me // 4, (self.me // 2) % 2, self.me % 2
        self.own = self.me // 2
        self.inner = (self.z == 1) | (self.z == 2)

    def at(self, y=None, z=None, x=None, core=None):
        y = self.y if y is None else y
        z = self.z if z is None else z
        x = self.x if x is None else x
        core = self.core if core is None else core
        return {"dp": y, "mp": z * 4 + x * 2 + core}

    def y_mate(self):
        return self.at(y=1 - self.y)

    def x_mate(self):
        return self.at(x=1 - self.x)

    def core_mate(self):
        return self.at(core=1 - self.core)

    def z_mate(self, k):
        return self.at(z=self.z ^ k)


class Lines:
    def __init__(self, send_sems, recv_sems):
        self.send_sems, self.recv_sems = send_sems, recv_sems
        self.next = 0
        self.sent = []

    def copy(self, sender, number, src, dst, device):
        return pltpu.make_async_remote_copy(
            src_ref=src,
            dst_ref=dst,
            send_sem=self.send_sems.at[sender],
            recv_sem=self.recv_sems.at[number],
            device_id=device,
            device_id_type=MESH,
        )

    def send(self, number, src, dst, device, sender=None, like=None, when=None, keep=True):
        if sender is None:
            sender = self.next
            self.next += 1
        self.copy(sender, number, src, dst, device).start()
        if keep:
            self.sent.append((sender, src if like is None else like, when))
        return sender

    def wait(self, number, land, device):
        self.copy(0, number, land, land, device).wait_recv()

    def wait_sent(self, sender, src, device):
        self.copy(sender, 0, src, src, device).wait_send()

    def drain(self, device):
        for sender, src, when in self.sent:
            if when is None:
                self.wait_sent(sender, src, device)
            else:
                pl.when(when)(functools.partial(self.wait_sent, sender, src, device))
        self.sent = []


class Gather:
    def __init__(self, spot, lines, base, win, wout, split):
        self.split = split
        self.spot, self.lines, self.base = spot, lines, base
        self.win, self.wout = win, wout
        self.like = win.at[0, 0, 0]
        self.senders = {}

    def along_z(self, block, hop, number):
        s, n, b = self.spot, self.lines, self.base
        zk = s.z ^ block
        for i, part in ((0, self.win), (1, self.wout)):
            ref = part.at[zk, s.x, s.y]
            when = None if block == 0 and hop == 1 else s.inner
            n.send(b + 2 * number - 2 + i, ref, ref, s.z_mate(hop), like=self.like, when=when)

    def start_z(self):
        self.along_z(0, 1, 1)
        pl.when(self.spot.inner)(lambda: self.along_z(0, 3, 3))

    def start_x(self):
        s, n, b = self.spot, self.lines, self.base
        own = self.wout.at[s.z, s.x, s.y]
        n.send(b + 9, own, own, s.x_mate())
        own = self.win.at[s.z, s.x]
        n.send(b + 13, own, own, s.x_mate())

    def arrive(self, k):
        s, n, b = self.spot, self.lines, self.base
        zk = s.z ^ k
        a, c = self.win.at[zk, s.x, s.y], self.wout.at[zk, s.x, s.y]
        n.wait(b + 2 * k - 2, a, s.z_mate(k))
        n.wait(b + 2 * k - 1, c, s.z_mate(k))
        hop, number = {1: (3, 2), 3: (1, 2), 2: (1, 3)}[k]
        return lambda: self.along_z(k, hop, number)

    def second(self, k):
        s, n, b = self.spot, self.lines, self.base
        zk = s.z ^ k
        a, c = self.win.at[zk, s.x, s.y], self.wout.at[zk, s.x, s.y]
        steps = [(b + 9 + k, c, s.x_mate())]
        if k != 1:
            steps += [(b + 5 + k, a, s.y_mate()), (b + 17 + 2 * k, c, s.y_mate())]
        if k in self.split:
            steps.append((b + 13 + k, a, s.x_mate()))
        for i, (number, ref, device) in enumerate(steps):
            known = self.senders.get((k, i))
            used = n.send(number, ref, ref, device, sender=known, like=self.like, keep=known is None)
            self.senders[(k, i)] = used

    def early(self):
        onward = self.arrive(1)
        pl.when(self.spot.inner)(onward)
        self.second(1)

        def near():
            self.arrive(3)()
            self.second(3)

        pl.when(self.spot.inner)(near)

    def late(self):
        onward = self.arrive(2)
        pl.when(self.spot.inner)(onward)
        self.second(2)

    def rest(self):
        s, n, b = self.spot, self.lines, self.base
        for i, part in ((0, self.win), (1, self.wout)):
            own = part.at[s.z, s.x, 1 - s.y]
            n.send(b + 29 + i, own, own, s.z_mate(1))

    def last(self):
        def far():
            self.arrive(3)
            self.second(3)

        pl.when(jnp.logical_not(self.spot.inner))(far)

    def third(self, k):
        s, n, b = self.spot, self.lines, self.base
        zk = s.z ^ k
        far = self.wout.at[zk, 1 - s.x, s.y]
        n.wait(b + 9 + k, far, s.x_mate())
        n.send(b + 18 + 2 * k, far, far, s.y_mate())
        if k > 1:
            n.wait(b + 5 + k, self.win.at[zk, s.x, 1 - s.y], s.y_mate())
        if k in self.split:
            far = self.win.at[zk, 1 - s.x, s.y]
            n.wait(b + 13 + k, far, s.x_mate())
            n.send(b + 25 + k, far, far, s.y_mate())
        elif k:
            n.send(b + 13 + k, self.win.at[zk, s.x], self.win.at[zk, s.x], s.x_mate())

    def finish(self, k):
        s, n, b = self.spot, self.lines, self.base
        zk = s.z ^ k
        if k in self.split:
            n.wait(b + 25 + k, self.win.at[zk, 1 - s.x, 1 - s.y], s.y_mate())
        else:
            n.wait(b + 13 + k, self.win.at[zk, 1 - s.x], s.x_mate())
        if k > 1:
            n.wait(b + 17 + 2 * k, self.wout.at[zk, s.x, 1 - s.y], s.y_mate())
        if k == 1:
            n.wait(b + 29, self.win.at[zk, s.x, 1 - s.y], s.z_mate(1))
            n.wait(b + 30, self.wout.at[zk, s.x, 1 - s.y], s.z_mate(1))
        n.wait(b + 18 + 2 * k, self.wout.at[zk, 1 - s.x, 1 - s.y], s.y_mate())


GATHER_LINES = 31


class Reduce:
    def __init__(self, spot, lines, base, parts, yins, zin, result):
        self.spot, self.lines, self.base = spot, lines, base
        self.parts, self.yins, self.zin, self.result = parts, yins, zin, result
        self.blocks = (jnp.where(spot.inner, 2, 3), jnp.where(spot.inner, 3, 2), 1, 0)
        self.like = parts[0].at[0, 0]

    def first(self, ready):
        s, n, b = self.spot, self.lines, self.base
        order = ((0, 0), (0, 1)) if ready == 0 else ((1, 0), (1, 1), (0, 2), (1, 2), (0, 3), (1, 3))
        for i, step in order:
            k = self.blocks[step]
            n.send(b + 2 * k + i, self.parts[i].at[s.z ^ k, 1 - s.y], self.yins[i].at[k], s.y_mate())

    def add(self, ref, more):
        ref[...] = (ref[...].astype(F32) + more[...].astype(F32)).astype(BF16)

    def take(self, slot, i):
        self.lines.wait(self.base + 8 + 2 * slot + i, self.zin.at[slot, i], self.spot.z_mate(1))
        return self.zin.at[slot, i]

    def second(self, first, last):
        for at in range(first, last):
            step, i = at // 2, at % 2
            self.step(step, i)

    def step(self, step, i):
        s, n, b = self.spot, self.lines, self.base
        k = self.blocks[step]
        ref, more = self.parts[i].at[s.z ^ k, s.y], self.yins[i].at[k]
        n.wait(b + 2 * k + i, more, s.y_mate())
        self.add(ref, more)
        if step == 3:
            return
        sender = n.next
        n.next += 1
        n.sent.append((sender, self.like, None))

        def onward(slot, device):
            number = b + 8 + 2 * slot + i
            n.send(number, ref, self.zin.at[slot, i], device, sender=sender, like=self.like, keep=False)

        def at_end():
            onward(step, s.z_mate(1))

        def inside():
            come, slot, hop = ((0, 4, 3), (1, 3, 3), (4, 5, 1))[step]
            self.add(ref, self.take(come, i))
            onward(slot, s.z_mate(hop))

        pl.when(s.inner)(inside)
        pl.when(jnp.logical_not(s.inner))(at_end)

    def third(self):
        s, n, b = self.spot, self.lines, self.base
        for i in (0, 1):

            def total(slots):
                value = self.parts[i][s.z, s.y].astype(F32)
                for slot in slots:
                    value = value + self.take(slot, i)[...].astype(F32)
                self.result[i, s.y] = value.astype(BF16)

            pl.when(s.inner)(lambda: total((2, 3)))
            pl.when(jnp.logical_not(s.inner))(lambda: total((5,)))

    def fourth(self):
        s, n, b = self.spot, self.lines, self.base
        for i in (0, 1):
            n.send(b + 20 + i, self.result.at[i, s.y], self.result.at[i, s.y], s.y_mate())

    def finish(self):
        s, n, b = self.spot, self.lines, self.base
        for i in (0, 1):
            n.wait(b + 20 + i, self.result.at[i, 1 - s.y], s.y_mate())


REDUCE_LINES = 22
MATE_LINES = 8
SEND_LINES = 200


def normalize(value):
    centre = value - jnp.mean(value, axis=-1, keepdims=True)
    scale = lax.rsqrt(jnp.mean(centre * centre, axis=-1, keepdims=True) + EPS_NORM)
    return centre * scale, scale


def normalize_back(grad, gain, unit, scale):
    gain_grad = jnp.sum(grad * unit, axis=0, keepdims=True)
    shift_grad = jnp.sum(grad, axis=0, keepdims=True)
    inner = grad * gain
    mean = jnp.mean(inner, axis=-1, keepdims=True)
    along = jnp.mean(inner * unit, axis=-1, keepdims=True)
    return scale * (inner - mean - unit * along), gain_grad, shift_grad


def dot(left, right):
    return jnp.dot(left, right, preferred_element_type=F32)


def dot_t(left, right):
    return lax.dot_general(left, right, (((1,), (1,)), ((), ())), preferred_element_type=F32)


def t_dot(left, right):
    return lax.dot_general(left, right, (((0,), (0,)), ((), ())), preferred_element_type=F32)


def pick(rows, columns, where):
    at = [lax.broadcasted_iota(jnp.int32, (rows, columns), axis) for axis in (0, 1)]
    return where(*at).astype(F32).astype(BF16)


def gelu_pair(v):
    root = math.sqrt(2.0 / math.pi)
    square = v * v
    tanh = jnp.tanh(root * v * (1.0 + 0.044715 * square))
    half = 0.5 + 0.5 * tanh
    slope = half + 0.5 * v * (1.0 - tanh * tanh) * (root * (1.0 + 3 * 0.044715 * square))
    return v * half, slope


def fused_kernel(
    plan,
    tokens, cotangent_far, win_far, wout_far, bias, vec, packed_far, rebuild_far, turn, wave_far,
    act_far, grad_far, weights_far, piece_out, vec_out, norm_out,
    act_out, grad_out,
    cotangent, win_own, wout_own, packed, rebuild, wave, local_sems,
    win, wout, bias_own, bias_all, hidden, acts, slopes, unit_mix, unit_out, scale_mix, scale_out, start, keep,
    branch_send, branch_recv, grad_branch, grad_pre, far_acts, far_slopes, far_pre,
    din, dout, yin, yout, zin, result,
    send, recv, work, send_back, recv_back,
    tiles, tiles_in, piece, pieces, square_send, square_recv,
    mix_sems, all_sems, send_sems, recv_sems,
):
    spot = Spot()
    lines = Lines(send_sems, recv_sems)
    parts, feats, rows = plan.parts, plan.feats, plan.rows
    me = spot.me
    hid = FF // parts
    group = 2 * hid
    barrier = pltpu.get_barrier_semaphore()

    devices = 2 * parts
    here = spot.y * parts + me

    def other(k):
        q = lax.rem(here + k, devices)
        return q, {"dp": q // parts, "mp": lax.rem(q, parts)}

    def everyone(action):
        def body(k, carry):
            action(k)
            return carry

        lax.fori_loop(1, devices, body, 0)

    everyone(lambda k: pl.semaphore_signal(barrier, inc=1, device_id=other(k)[1], device_id_type=MESH))

    loads = [
        pltpu.make_async_copy(src, dst, local_sems.at[i])
        for i, (src, dst) in enumerate(
            (
                (win_far.at[0], win_own.at[0]),
                (wout_far.at[0], wout_own.at[0]),
                (packed_far, packed),
                (wave_far, wave),
                (rebuild_far, rebuild),
                (win_far.at[1], win_own.at[1]),
                (wout_far.at[1], wout_own.at[1]),
                (cotangent_far, cotangent),
            )
        )
    ]
    for load in loads:
        load.start()

    base = 0
    gathers, reduces = [], []
    for l in range(LAYERS):
        gathers.append(Gather(spot, lines, base, win.at[l], wout.at[l], (1, 3) if l == 0 else (1, 2, 3)))
        base += GATHER_LINES
    for l in range(LAYERS):
        reduces.append(
            Reduce(
                spot, lines, base, (din.at[l], dout.at[l]), (yin.at[l], yout.at[l]), zin.at[l], result.at[l]
            )
        )
        base += REDUCE_LINES
    mates = []
    for l in range(LAYERS):
        mates.append(base)
        base += MATE_LINES
    bias_base = base

    def copy_to(k, src, dst, lane):
        q = lax.rem(me + k, parts)
        return pltpu.make_async_remote_copy(
            src_ref=src.at[q],
            dst_ref=dst.at[me],
            send_sem=mix_sems.at[lane, q],
            recv_sem=mix_sems.at[lane + 1, me],
            device_id={"mp": q},
            device_id_type=MESH,
        )

    def copy_from(k, src, dst, lane):
        p = lax.rem(me + k, parts)
        return pltpu.make_async_remote_copy(
            src_ref=src.at[p],
            dst_ref=dst.at[p],
            send_sem=mix_sems.at[lane, p],
            recv_sem=mix_sems.at[lane + 1, p],
            device_id={"mp": p},
            device_id_type=MESH,
        )

    def each(action):
        def body(k, carry):
            action(k)
            return carry

        lax.fori_loop(1, parts, body, 0)

    def mix_enter(value):
        send[...] = dot_t(packed[...], value).astype(BF16).reshape(parts, feats, rows)

    def mix_go():
        each(lambda k: copy_to(k, send, recv, 0).start())
        recv[me] = send[me]

    def mix_middle():
        each(lambda k: copy_from(k, send, recv, 0).wait_recv())
        position_dft(plan, me, recv, work, send_back, turn, wave)
        each(lambda k: copy_to(k, send_back, recv_back, 2).start())
        recv_back[me] = send_back[me]

    def mix_leave():
        each(lambda k: copy_from(k, send_back, recv_back, 2).wait_recv())
        mixed = t_dot(recv_back[...].reshape(parts * feats, rows), rebuild[...])
        each(lambda k: copy_to(k, send, recv, 0).wait_send())
        each(lambda k: copy_to(k, send_back, recv_back, 2).wait_send())
        return mixed * (1.0 / math.sqrt(L * D))

    eye = pick(hid, 256, lambda i, j: i == j)

    def bias_column(l, zk, x):
        return dot_t(eye, bias_all[zk, x])[:, l : l + 1]

    def own_weights(l):
        win[l, spot.z, spot.x] = win_own[l].astype(BF16).reshape(2, hid // 2, D)
        wout[l, spot.z, spot.x] = wout_own[l].astype(BF16).reshape(2, hid // 2, D)

    def swap_branch(number, slot):
        ref, land = branch_send.at[slot], branch_recv.at[slot]
        return lines.send(number, ref, land, spot.core_mate(), keep=False)

    def hidden_away(l):
        lines.send(mates[l] + 4, hidden.at[l, 0], hidden.at[l, 2], spot.x_mate())

    def forward(l, current, mixed, per_group):
        unit, scale = normalize(current + mixed)
        unit_mix[l] = unit
        scale_mix[l] = scale
        normed = unit * vec[0, l : l + 1] + vec[1, l : l + 1]
        keep[...] = normed
        hidden[l, 0] = normed.astype(BF16)
        lines.send(mates[l], hidden.at[l, 0], hidden.at[l, 1], spot.core_mate())
        for k in range(4):
            per_group(k)
            zk = spot.z ^ k
            weights = win[l, zk].reshape(group, D)
            column = jnp.concatenate([bias_column(l, zk, x) for x in (0, 1)], axis=0)
            for slot in (0, 1):
                if k == 0 and slot == 1:
                    lines.wait(mates[l], hidden.at[l, 1], spot.core_mate())
                value, slope = gelu_pair(dot_t(weights, hidden[l, slot]) + column)
                span = slice(slot * rows, (slot + 1) * rows)
                acts[l, zk, :, :, span] = value.astype(BF16).reshape(2, hid, rows)
                slopes[l, zk, :, :, span] = slope.astype(BF16).reshape(2, hid, rows)
        if l == LAYERS - 1:
            hidden_away(l)
        outs = wout[l].reshape(FF // 2, D)
        branch_send[0] = t_dot(acts[l, :, :, :, rows : 2 * rows].reshape(FF // 2, rows), outs).astype(BF16)
        sender = swap_branch(mates[l] + 1, 0)
        branch = t_dot(acts[l, :, :, :, 0:rows].reshape(FF // 2, rows), outs)
        lines.wait(mates[l] + 1, branch_recv.at[0], spot.core_mate())
        total = keep[...] + branch + branch_recv[0].astype(F32) + vec[2, l : l + 1]
        unit, scale = normalize(total)
        unit_out[l] = unit
        scale_out[l] = scale
        lines.wait_sent(sender, branch_send.at[0], spot.core_mate())
        return unit * vec[3, l : l + 1] + vec[4, l : l + 1]

    def vec_put(l, i, value):
        for t in range(3):
            for j in (0, 1):
                at = 256 * t + 128 * j
                tiles[3 * (5 * l + i) + t, j : j + 1, :] = value[:, at : at + 128]

    def bias_put(l):
        ones = jnp.ones((16, 2 * rows), BF16)
        for zk in range(4):
            for x in (0, 1):
                row = dot_t(ones, grad_pre[zk, x])[0:1]
                for y in (0, 1):
                    to = y * parts + zk * 4 + x * 2 + spot.core
                    tiles[to, 2 + 2 * l : 3 + 2 * l, :] = row[:, 0:128]
                    tiles[to, 3 + 2 * l : 4 + 2 * l, 0 : hid - 128] = row[:, 128:hid]

    def from_x_mate(l, parts_of):
        for i, part in parts_of:
            lines.wait(mates[l] + i, part.at[l, 2], spot.x_mate())
            lines.send(mates[l] + i + 1, part.at[l, 2], part.at[l, 3], spot.core_mate())

    half = FF // 4

    def far_hidden(l):
        ins = win[l, :, spot.x].reshape(half, D)
        column = jnp.concatenate([bias_column(l, zk, spot.x) for zk in range(4)], axis=0)
        for slot in (2, 3):
            if slot == 3:
                lines.wait(mates[l] + 5, hidden.at[l, 3], spot.core_mate())
            span = slice((slot - 2) * rows, (slot - 1) * rows)
            value, slope = gelu_pair(dot_t(ins, hidden[l, slot]) + column)
            far_acts[:, span] = value.astype(BF16)
            far_slopes[:, span] = slope.astype(BF16)

    def far_grads(l):
        outs = wout[l, :, spot.x].reshape(half, D)
        for slot in (2, 3):
            if slot == 3:
                lines.wait(mates[l] + 7, grad_branch.at[l, 3], spot.core_mate())
            span = slice((slot - 2) * rows, (slot - 1) * rows)
            grad_act = dot_t(outs, grad_branch[l, slot])
            far_pre[:, span] = (grad_act * far_slopes[:, span].astype(F32)).astype(BF16)

    def weight_grads(l):
        for i, (near, far, part, out) in enumerate(
            (
                (grad_pre[:, spot.x], far_pre, hidden, din),
                (acts[l, :, spot.x], far_acts, grad_branch, dout),
            )
        ):
            total = dot(near.reshape(half, 2 * rows), part[l, 0:2].reshape(2 * rows, D))
            total = total + dot(far[...], part[l, 2:4].reshape(2 * rows, D))
            out[l] = total.astype(BF16).reshape(4, 2, hid // 2, D)
            reduces[l].first(i)

    def backward(l, grad, middle, later):
        grad_total, gain_grad, shift_grad = normalize_back(grad, vec[3, l : l + 1], unit_out[l], scale_out[l])
        low = grad_total.astype(BF16)
        grad_branch[l, 0] = low
        lines.send(mates[l] + 2, grad_branch.at[l, 0], grad_branch.at[l, 1], spot.core_mate())
        lines.send(mates[l] + 6, grad_branch.at[l, 0], grad_branch.at[l, 2], spot.x_mate())
        keep[...] = grad_total
        vec_put(l, 2, jnp.sum(low.astype(F32), axis=0, keepdims=True))
        vec_put(l, 3, gain_grad)
        vec_put(l, 4, shift_grad)
        for slot in (0, 1):
            if slot == 1:
                lines.wait(mates[l] + 2, grad_branch.at[l, 1], spot.core_mate())
            span = slice(slot * rows, (slot + 1) * rows)
            for zk in range(4):
                grad_act = dot_t(wout[l, zk].reshape(group, D), grad_branch[l, slot]).reshape(2, hid, rows)
                grad_pre[zk, :, :, span] = (grad_act * slopes[l, zk, :, :, span].astype(F32)).astype(BF16)
        middle()
        ins = win[l].reshape(FF // 2, D)
        branch_send[1] = t_dot(grad_pre[:, :, :, rows : 2 * rows].reshape(FF // 2, rows), ins).astype(BF16)
        sender = swap_branch(mates[l] + 3, 1)
        grad_normed = t_dot(grad_pre[:, :, :, 0:rows].reshape(FF // 2, rows), ins)
        bias_put(l)
        later()
        lines.wait(mates[l] + 3, branch_recv.at[1], spot.core_mate())
        grad_normed = keep[...] + grad_normed + branch_recv[1].astype(F32)
        lines.wait_sent(sender, branch_send.at[1], spot.core_mate())
        grad_summed, gain_grad, shift_grad = normalize_back(grad_normed, vec[0, l : l + 1], unit_mix[l], scale_mix[l])
        vec_put(l, 0, gain_grad)
        vec_put(l, 1, shift_grad)
        return grad_summed

    inner = plan.inner

    def to_local(i, j):
        return j == parts * (i % inner) + i // inner

    for load in loads[:2]:
        load.wait()
    own_weights(0)
    bias_own[...] = jnp.zeros_like(bias_own)
    bias_own[0:LAYERS, 0:hid] = bias[...]
    bias_all[spot.z, spot.x] = bias_own[...].astype(BF16)
    tiles[...] = jnp.zeros_like(tiles)
    pl.semaphore_wait(barrier, devices - 1)
    gathers[0].start_z()
    gathers[0].start_x()
    local = dot(pick(rows, rows, to_local), tokens[...])
    start[...] = local
    for load in loads[2:4]:
        load.wait()
    mix_enter(local.astype(BF16))
    mix_go()
    for j in range(1, 8):
        far = spot.own ^ j
        own = bias_all.at[spot.z, spot.x]
        lines.send(bias_base + j, own, own, {"dp": spot.y, "mp": far * 2 + spot.core})
    for load in loads[4:]:
        load.wait()
    own_weights(1)
    gathers[0].early()
    gathers[0].third(0)
    gathers[0].late()
    gathers[0].third(1)
    mix_middle()
    gathers[0].last()
    gathers[0].rest()
    gathers[1].start_z()
    gathers[0].third(2)
    gathers[0].third(3)
    gathers[1].start_x()
    for j in range(1, 8):
        far = spot.own ^ j
        lines.wait(bias_base + j, bias_all.at[far // 2, far % 2], {"dp": spot.y, "mp": far * 2 + spot.core})
    mixed = mix_leave()

    def between(k):
        if k == 2:
            gathers[1].early()
        gathers[0].finish(k)

    current = forward(0, start[...], mixed, between)
    start[...] = current
    mix_enter(current.astype(BF16))
    mix_go()
    gathers[1].third(0)
    gathers[1].late()
    gathers[1].rest()
    gathers[1].third(1)
    gathers[1].last()
    gathers[1].third(2)
    mix_middle()
    gathers[1].third(3)
    mixed = mix_leave()
    current = forward(1, start[...], mixed, lambda k: gathers[1].finish(k))
    act_out[...] = t_dot(pick(rows, rows, to_local), current.astype(BF16)).astype(BF16)
    stores = [
        pltpu.make_async_copy(src, dst, local_sems.at[8 + i])
        for i, (src, dst) in enumerate(
            ((act_out, act_far), (grad_out, grad_far), (result.at[1], weights_far.at[1]), (result.at[0], weights_far.at[0]))
        )
    ]
    stores[0].start()

    by_hidden, by_grad = ((4, hidden),), ((6, grad_branch),)
    grad = backward(1, dot(pick(rows, rows, to_local), cotangent[...]), lambda: None, lambda: None)
    start[...] = grad
    mix_enter(grad.astype(BF16))
    mix_go()
    from_x_mate(1, by_hidden + by_grad)
    far_hidden(1)
    far_grads(1)
    mix_middle()
    hidden_away(0)
    weight_grads(1)
    mixed = mix_leave()

    def middle():
        from_x_mate(0, by_hidden)
        far_hidden(0)

    grad = backward(0, start[...] + mixed, middle, lambda: reduces[1].second(0, 4))

    def tile_to(k):
        q, device = other(k)
        return pltpu.make_async_remote_copy(
            src_ref=tiles.at[q], dst_ref=tiles_in.at[here], send_sem=all_sems.at[0, q], recv_sem=all_sems.at[1, here],
            device_id=device, device_id_type=MESH,
        )

    def tile_from(k):
        p, device = other(k)
        return pltpu.make_async_remote_copy(
            src_ref=tiles.at[p], dst_ref=tiles_in.at[p], send_sem=all_sems.at[0, p], recv_sem=all_sems.at[1, p],
            device_id=device, device_id_type=MESH,
        )

    everyone(lambda k: tile_to(k).start())
    tiles_in[here] = tiles[here]
    start[...] = grad
    mix_enter(grad.astype(BF16))
    mix_go()
    from_x_mate(0, by_grad)
    far_grads(0)
    reduces[1].second(4, 8)
    weight_grads(0)
    reduces[1].third()
    reduces[1].fourth()
    reduces[0].second(0, 8)
    mix_middle()
    everyone(lambda k: tile_from(k).wait_recv())
    total = tiles_in[0]
    for d in range(1, devices):
        total = total + tiles_in[d]
    piece_out[...] = total
    piece[...] = total

    def piece_to(k):
        q, device = other(k)
        return pltpu.make_async_remote_copy(
            src_ref=piece, dst_ref=pieces.at[here], send_sem=all_sems.at[2, q], recv_sem=all_sems.at[3, here],
            device_id=device, device_id_type=MESH,
        )

    def piece_from(k):
        p, device = other(k)
        return pltpu.make_async_remote_copy(
            src_ref=piece, dst_ref=pieces.at[p], send_sem=all_sems.at[2, p], recv_sem=all_sems.at[3, p],
            device_id=device, device_id_type=MESH,
        )

    everyone(lambda k: piece_to(k).start())
    pieces[here] = total
    reduces[1].finish()
    stores[2].start()
    reduces[0].third()

    def squares(ref):
        value = ref[...].astype(F32)
        return jnp.sum(value * value, axis=(0, 1), keepdims=True)

    row = lax.broadcasted_iota(jnp.int32, total.shape, 0)
    local = 0.5 * jnp.sum(jnp.where((row >= 2) & (row < 6), total * total, 0.0), axis=(0, 1), keepdims=True)
    for l in range(LAYERS):
        for i in (0, 1):
            local = local + squares(result.at[l, i, spot.y])
    square_send[...] = jnp.broadcast_to(local, square_send.shape)

    def square_to(k):
        q, device = other(k)
        return pltpu.make_async_remote_copy(
            src_ref=square_send, dst_ref=square_recv.at[here], send_sem=all_sems.at[4, q], recv_sem=all_sems.at[5, here],
            device_id=device, device_id_type=MESH,
        )

    def square_from(k):
        p, device = other(k)
        return pltpu.make_async_remote_copy(
            src_ref=square_send, dst_ref=square_recv.at[p], send_sem=all_sems.at[4, p], recv_sem=all_sems.at[5, p],
            device_id=device, device_id_type=MESH,
        )

    everyone(lambda k: square_to(k).start())
    square_recv[here] = square_send[...]
    reduces[0].fourth()
    mixed = mix_leave()
    grad = start[...] + mixed
    back = pick(rows, rows, lambda i, j: to_local(j, i))
    high = grad.astype(BF16)
    rest = grad - high.astype(F32)
    middle = rest.astype(BF16)
    low = (rest - middle.astype(F32)).astype(BF16)
    grad = dot(back, high) + (dot(back, middle) + dot(back, low))
    for t in range(D // 128):
        grad_out[pl.ds(t, rows, stride=D // 128), :] = grad[:, 128 * t : 128 * (t + 1)]
    stores[1].start()

    everyone(lambda k: piece_from(k).wait_recv())
    for l in range(LAYERS):
        for i in range(5):
            for t in range(3):
                for j in (0, 1):
                    at = 256 * t + 128 * j
                    vec_out[i, l : l + 1, at : at + 128] = pieces[3 * (5 * l + i) + t, j : j + 1, :]
    every = jnp.sum(jnp.where(row < 2, pieces[...] * pieces[...], 0.0), axis=0)
    norms = jnp.sum(every, axis=(0, 1), keepdims=True)
    everyone(lambda k: square_from(k).wait_recv())
    norms = norms + jnp.sum(square_recv[...], axis=0)[0:1, 0:1]
    norm_out[...] = jnp.broadcast_to(jnp.sqrt(norms), norm_out.shape)
    everyone(lambda k: tile_to(k).wait_send())
    everyone(lambda k: piece_to(k).wait_send())
    everyone(lambda k: square_to(k).wait_send())
    stores[0].wait()
    stores[1].wait()
    reduces[0].finish()
    stores[3].start()
    lines.drain(spot.core_mate())
    stores[2].wait()
    stores[3].wait()


def fused(plan, tokens, cotangent, weight_in, weight_out, bias_in, vec):
    parts, feats, rows = plan.parts, plan.feats, plan.rows
    block = (parts, feats, rows)
    hid = FF // parts
    half = hid // 2
    vm = pltpu.VMEM
    near, far = pl.BlockSpec(memory_space=vm), pl.BlockSpec(memory_space=pl.ANY)
    line_count = LAYERS * (GATHER_LINES + REDUCE_LINES + MATE_LINES) + 8
    return pl.pallas_call(
        functools.partial(fused_kernel, plan),
        out_shape=(
            jax.ShapeDtypeStruct((rows, D), BF16),
            jax.ShapeDtypeStruct((rows * D // 128, 128), F32),
            jax.ShapeDtypeStruct((LAYERS, 2, 2, half, D), BF16),
            jax.ShapeDtypeStruct((8, 128), F32),
            jax.ShapeDtypeStruct((5, LAYERS, D), F32),
            jax.ShapeDtypeStruct((8, 128), F32),
        ),
        in_specs=[near, far, far, far, near, near, far, far, near, far],
        out_specs=[far] * 3 + [near] * 3,
        scratch_shapes=[
            vm((rows, D), BF16),
            vm((rows * D // 128, 128), F32),
            vm((rows, D), BF16),
            vm((LAYERS, hid, D), F32),
            vm((LAYERS, hid, D), F32),
            vm((parts * feats, D), BF16),
            vm((parts * feats, D), BF16),
            vm((2 * rows, rows), BF16),
            pltpu.SemaphoreType.DMA((12,)),
            vm((LAYERS, 4, 2, 2, half, D), BF16),
            vm((LAYERS, 4, 2, 2, half, D), BF16),
            vm((16, 256), F32),
            vm((4, 2, 16, 256), BF16),
            vm((LAYERS, 4, rows, D), BF16),
            vm((LAYERS, 4, 2, hid, 2 * rows), BF16),
            vm((LAYERS, 4, 2, hid, 2 * rows), BF16),
            vm((LAYERS, rows, D), F32),
            vm((LAYERS, rows, D), F32),
            vm((LAYERS, rows, 1), F32),
            vm((LAYERS, rows, 1), F32),
            vm((rows, D), F32),
            vm((rows, D), F32),
            vm((2, rows, D), BF16),
            vm((2, rows, D), BF16),
            vm((LAYERS, 4, rows, D), BF16),
            vm((4, 2, hid, 2 * rows), BF16),
            vm((FF // 4, 2 * rows), BF16),
            vm((FF // 4, 2 * rows), BF16),
            vm((FF // 4, 2 * rows), BF16),
            vm((LAYERS, 4, 2, half, D), BF16),
            vm((LAYERS, 4, 2, half, D), BF16),
            vm((LAYERS, 4, half, D), BF16),
            vm((LAYERS, 4, half, D), BF16),
            vm((LAYERS, 6, 2, half, D), BF16),
            vm((LAYERS, 2, 2, half, D), BF16),
            vm(block, BF16),
            vm(block, BF16),
            vm((parts, feats, 2 * rows), BF16),
            vm(block, BF16),
            vm(block, BF16),
            vm((2 * parts, 8, 128), F32),
            vm((2 * parts, 8, 128), F32),
            vm((8, 128), F32),
            vm((2 * parts, 8, 128), F32),
            vm((8, 128), F32),
            vm((2 * parts, 8, 128), F32),
            pltpu.SemaphoreType.DMA((4, parts)),
            pltpu.SemaphoreType.DMA((6, 2 * parts)),
            pltpu.SemaphoreType.DMA((SEND_LINES,)),
            pltpu.SemaphoreType.DMA((line_count,)),
        ],
        compiler_params=pltpu.CompilerParams(collective_id=1, has_side_effects=True, vmem_limit_bytes=62 * 2**20),
    )(tokens, cotangent, weight_in, weight_out, bias_in, vec, plan.packed, plan.rebuild, plan.turn, plan.wave)


def update_kernel(*refs):
    far_small, (change_far,), ins, through_far = refs[0:9], refs[9:10], refs[10:16], refs[16:18]
    outs, through_out, small_outs, norm_out = refs[18:26], refs[26:28], refs[28:34], refs[34]
    small, (change,), near_ins, near_outs = refs[35:44], refs[44:45], refs[45:51], refs[51:59]
    near_through, near_small, sems, small_sems = refs[59:61], refs[61:67], refs[67], refs[68]
    norm, bias, moment_bias, square_bias, piece, vec, moment_vec, square_vec, sum_vec = small
    hid = bias.shape[1]
    part = hid // 2
    pieces = [(l, kind, h) for l in range(LAYERS) for kind in (0, 1) for h in (0, 1)]
    last = len(pieces)

    def copies(at, out):
        l, kind, h = pieces[at]
        span = pl.ds(h * part, part)
        if out:
            pairs = zip(near_outs[4 * kind : 4 * kind + 4], outs[4 * kind : 4 * kind + 4])
        else:
            pairs = zip(ins[3 * kind : 3 * kind + 3], near_ins[3 * kind : 3 * kind + 3])
        result = [(src.at[l, span], dst.at[l, span]) for src, dst in pairs]
        if not out:
            result.append((change_far.at[l, kind, h], change.at[l, kind, h]))
        return [pltpu.make_async_copy(src, dst, sems.at[int(out), at, i]) for i, (src, dst) in enumerate(result)]

    def lists(sources, targets, row, lane):
        return [
            pltpu.make_async_copy(src, dst, small_sems.at[row, lane + i])
            for i, (src, dst) in enumerate(zip(sources, targets))
        ]

    small_in = lists(far_small, small, 0, 0)
    small_out = lists(near_small, small_outs, 1, 0)
    through_in = lists(through_far, near_through, 0, 9)
    through_to = lists(near_through, through_out, 1, 9)
    for copy in small_in:
        copy.start()
    for at in range(last):
        for copy in copies(at, False):
            copy.start()
    for copy in through_in:
        copy.start()
    for copy in small_in:
        copy.wait()
    factor = jnp.minimum(1.0, CLIP / norm[0:1, 0:1])
    norm_out[0, 0] = norm[0, 0]
    m_bias, v_bias, b_new, m_vec, v_vec, vec_new = near_small
    for l in range(LAYERS):
        row = jnp.concatenate([piece[2 + 2 * l : 3 + 2 * l, :], piece[3 + 2 * l : 4 + 2 * l, 0 : hid - 128]], axis=1)
        here = slice(l, l + 1)
        news = adamw(bias[here], row * factor, moment_bias[here], square_bias[here], 0.5, 0.0)
        for out, value in zip((m_bias, v_bias, b_new), news):
            out[here] = value
    news = adamw(vec[...], sum_vec[...] * factor, moment_vec[...], square_vec[...], 0.5, 0.0)
    for out, value in zip((m_vec, v_vec, vec_new), news):
        out[...] = value
    for copy in small_out:
        copy.start()
    for at, (l, kind, h) in enumerate(pieces):
        for copy in copies(at, False):
            copy.wait()
        span = slice(h * part, (h + 1) * part)
        weight, moment, square = [ref[l, span] for ref in near_ins[3 * kind : 3 * kind + 3]]
        width = (D, FF)[kind]
        news = adamw(
            weight, change[l, kind, h].astype(F32) * factor, moment, square, 1.0 / math.sqrt(width), DECAY
        )
        for out, value in zip(near_outs[4 * kind : 4 * kind + 4], news + (news[2].astype(BF16),)):
            out[l, span] = value
        for copy in copies(at, True):
            copy.start()
    for copy_in, copy_out in zip(through_in, through_to):
        copy_in.wait()
        copy_out.start()
    for at in range(last):
        for copy in copies(at, True):
            copy.wait()
    for copy in small_out + through_to:
        copy.wait()


def update(*args):
    far = pl.BlockSpec(memory_space=pl.ANY)
    small, change, weight, through = args[0:9], args[9], args[10], args[16:18]

    def shape(value, dtype=F32):
        return jax.ShapeDtypeStruct(value.shape, dtype)

    def near(value, dtype=F32):
        return pltpu.VMEM(value.shape, dtype)

    kinds = (F32, F32, F32, BF16) * 2
    bias, vec = small[1], small[5]
    return pl.pallas_call(
        update_kernel,
        out_shape=tuple(shape(weight, kind) for kind in kinds)
        + (shape(through[0], BF16), shape(through[1]))
        + (shape(bias),) * 3
        + (shape(vec),) * 3
        + (jax.ShapeDtypeStruct((1, 1), F32),),
        in_specs=[far] * 18,
        out_specs=[far] * 16 + [pl.BlockSpec(memory_space=pltpu.SMEM)],
        scratch_shapes=[near(value) for value in small]
        + [near(change, BF16)]
        + [near(weight)] * 6
        + [near(weight, kind) for kind in kinds]
        + [near(through[0], BF16), near(through[1])]
        + [near(bias)] * 3
        + [near(vec)] * 3
        + [pltpu.SemaphoreType.DMA((2, 8, 4)), pltpu.SemaphoreType.DMA((2, 11))],
        compiler_params=pltpu.CompilerParams(vmem_limit_bytes=62 * 2**20),
    )(*args)


def on_block(
    tokens, cotangent, weight_in, bias_in, weight_out, vectors, moment_in, square_in,
    moment_bias, square_bias, moment_out, square_out, moment_vec, square_vec,
):
    rows = tokens.shape[0]
    plan = Plan(L // rows)

    def turned(value):
        return jnp.swapaxes(value, 1, 2)

    def by_kind(value):
        return jnp.swapaxes(value, 0, 1)

    win, vec = turned(weight_in), by_kind(vectors)
    acts, grad, grads, piece, sum_vec, norm = fused(
        plan, tokens.reshape(rows, D), cotangent.reshape(rows, D), win, weight_out, bias_in, vec
    )
    (
        m_in, v_in, w_in, low_in, m_out, v_out, w_out, low_out, acts, grad,
        m_bias, v_bias, b_new, m_vec, v_vec, vec_new, norm,
    ) = update(
        norm, bias_in, moment_bias, square_bias, piece, vec, by_kind(moment_vec), by_kind(square_vec), sum_vec, grads,
        win, turned(moment_in), turned(square_in), weight_out, moment_out, square_out, acts, grad,
    )
    return (
        acts.reshape(rows, 1, D),
        grad.reshape(rows, 1, D),
        norm[0, 0],
        turned(m_in),
        turned(v_in),
        turned(w_in),
        turned(low_in),
        m_out,
        v_out,
        w_out,
        low_out,
        m_bias,
        v_bias,
        b_new,
        by_kind(m_vec),
        by_kind(v_vec),
        by_kind(vec_new),
    )


def matmul(left_op, right_op):
    return jnp.dot(left_op, right_op, preferred_element_type=jnp.float32)


def inner_rows(left_op, right_op):
    return lax.dot_general(
        left_op, right_op, (((0,), (0,)), ((), ())), preferred_element_type=jnp.float32
    )


def inner_cols(left_op, right_op):
    return lax.dot_general(
        left_op, right_op, (((1,), (1,)), ((), ())), preferred_element_type=jnp.float32
    )


def layer_norm(value, gain, shift):
    centre = value - jnp.mean(value, axis=-1, keepdims=True)
    spread = jnp.mean(centre * centre, axis=-1, keepdims=True)
    return centre * lax.rsqrt(spread + EPS_NORM) * gain + shift


def adamw(weight, grad, moment, square, rate, decay):
    new_moment = BETA_ONE * moment + (1.0 - BETA_ONE) * grad
    new_square = BETA_TWO * square + (1.0 - BETA_TWO) * grad * grad
    moment_hat = new_moment / (1.0 - BETA_ONE**STEP)
    square_hat = new_square / (1.0 - BETA_TWO**STEP)
    new_weight = weight - rate * (moment_hat / (jnp.sqrt(square_hat) + EPS_ADAM) + decay * weight)
    return (new_moment, new_square, new_weight)


def on_device(
    tokens,
    cotangent,
    weight_in,
    bias_in,
    weight_out,
    vectors,
    moment_in,
    square_in,
    moment_bias,
    square_bias,
    moment_out,
    square_out,
    moment_vec,
    square_vec,
):
    row_count, seq_count, feat_count = tokens.shape
    plan = Plan(L // row_count)

    def localize(value):
        return jnp.swapaxes(value.reshape(plan.inner, plan.parts, -1), 0, 1).reshape(value.shape)

    def restore(value):
        return jnp.swapaxes(value.reshape(plan.parts, plan.inner, -1), 0, 1).reshape(value.shape)

    current = localize(tokens).astype(jnp.float32)
    saved = []
    for layer_at in range(LAYERS):
        vector_set = vectors[layer_at]
        rounded = current.astype(jnp.bfloat16)
        mixed = mix(plan, rounded.reshape(row_count, feat_count)).reshape(row_count, seq_count, feat_count)
        summed = current + mixed
        normed = layer_norm(summed, vector_set[0], vector_set[1])
        hidden_in = normed.astype(jnp.bfloat16)
        weight_one = weight_in[layer_at].astype(jnp.bfloat16)
        weight_two = weight_out[layer_at].astype(jnp.bfloat16)
        bias_one = bias_in[layer_at].astype(jnp.bfloat16)
        whole_one, whole_two, whole_bias = (
            lax.all_gather(weight_one, "mp", axis=1, tiled=True),
            lax.all_gather(weight_two, "mp", axis=0, tiled=True),
            lax.all_gather(bias_one, "mp", axis=0, tiled=True),
        )
        inputs = hidden_in.reshape(-1, feat_count)
        pre_act = matmul(inputs, whole_one) + whole_bias.astype(jnp.float32)
        acts = jax.nn.gelu(pre_act).astype(jnp.bfloat16)
        branch = matmul(acts, whole_two).reshape(row_count, seq_count, feat_count)
        held = (inputs, whole_one, whole_two)
        total = normed + branch + vector_set[2]
        current = layer_norm(total, vector_set[3], vector_set[4])
        saved.append((summed, total, pre_act, acts, held))
    activations = restore(current.astype(jnp.bfloat16))
    grad = localize(cotangent).astype(jnp.float32)
    layer_grads = [None] * LAYERS
    for layer_at in reversed(range(LAYERS)):
        vector_set = vectors[layer_at]
        summed, total, pre_act, acts, held = saved[layer_at]
        inputs, mat_one, mat_two = held
        _, pull_out = jax.vjp(layer_norm, total, vector_set[3], vector_set[4])
        grad_total, gain_two, shift_two = pull_out(grad)
        grad_branch = grad_total.astype(jnp.bfloat16)
        grad_bias_two = jnp.sum(grad_branch.astype(jnp.float32), axis=(0, 1))
        flat_grad = grad_branch.reshape(-1, feat_count)
        grad_act = inner_cols(flat_grad, mat_two)
        _, pull_gelu = jax.vjp(jax.nn.gelu, pre_act)
        grad_pre = pull_gelu(grad_act)[0].astype(jnp.bfloat16)
        full_one = inner_rows(inputs, grad_pre)
        full_two = inner_rows(acts, flat_grad)
        full_bias = jnp.sum(grad_pre.astype(jnp.float32), axis=0)
        grad_one, grad_two, grad_bias_one = (
            lax.psum_scatter(
                full_one.astype(jnp.bfloat16), "mp", scatter_dimension=1, tiled=True
            ).astype(jnp.float32),
            lax.psum_scatter(
                full_two.astype(jnp.bfloat16), "mp", scatter_dimension=0, tiled=True
            ).astype(jnp.float32),
            lax.psum_scatter(
                full_bias.astype(jnp.bfloat16), "mp", scatter_dimension=0, tiled=True
            ).astype(jnp.float32),
        )
        grad_normed = inner_cols(grad_pre, mat_one).reshape(row_count, seq_count, feat_count)
        grad_normed = grad_normed + grad_total
        _, pull_in = jax.vjp(layer_norm, summed, vector_set[0], vector_set[1])
        grad_summed, gain_one, shift_one = pull_in(grad_normed)
        mix_grad = grad_summed.astype(jnp.bfloat16).reshape(-1, feat_count)
        grad_mix = mix(plan, mix_grad).reshape(row_count, seq_count, feat_count)
        grad = grad_summed + grad_mix
        layer_grads[layer_at] = (
            grad_one,
            grad_two,
            grad_bias_one,
            jnp.stack([gain_one, shift_one, grad_bias_two, gain_two, shift_two]),
        )
    stack_in = jnp.stack([entry[0] for entry in layer_grads])
    stack_out = jnp.stack([entry[1] for entry in layer_grads])
    stack_bias = jnp.stack([entry[2] for entry in layer_grads])
    stack_vec = jnp.stack([entry[3] for entry in layer_grads])
    sum_in, sum_out, sum_bias, sum_vec = (
        lax.psum(stack_in.astype(jnp.bfloat16), "dp").astype(jnp.float32),
        lax.psum(stack_out.astype(jnp.bfloat16), "dp").astype(jnp.float32),
        lax.psum(stack_bias.astype(jnp.bfloat16), "dp").astype(jnp.float32),
        lax.psum(stack_vec.astype(jnp.bfloat16), "dp").astype(jnp.float32),
    )
    local_squares = (
        jnp.sum(sum_in * sum_in) + jnp.sum(sum_out * sum_out) + jnp.sum(sum_bias * sum_bias)
    )
    sum_vec, total_squares = lax.psum((sum_vec, local_squares), "mp")
    grad_norm = jnp.sqrt(total_squares + jnp.sum(sum_vec * sum_vec))
    factor = jnp.minimum(1.0, CLIP / grad_norm)
    m_in, v_in, w_in = adamw(
        weight_in, sum_in * factor, moment_in, square_in, 1.0 / math.sqrt(D), DECAY
    )
    m_out, v_out, w_out = adamw(
        weight_out, sum_out * factor, moment_out, square_out, 1.0 / math.sqrt(FF), DECAY
    )
    m_bias, v_bias, b_new = adamw(bias_in, sum_bias * factor, moment_bias, square_bias, 0.5, 0.0)
    m_vec, v_vec, vec_new = adamw(vectors, sum_vec * factor, moment_vec, square_vec, 0.5, 0.0)
    return (
        activations,
        restore(grad),
        grad_norm,
        m_in,
        v_in,
        w_in,
        w_in.astype(jnp.bfloat16),
        m_out,
        v_out,
        w_out,
        w_out.astype(jnp.bfloat16),
        m_bias,
        v_bias,
        b_new,
        m_vec,
        v_vec,
        vec_new,
    )


def solution(mesh):
    body = on_block if (mesh.shape["dp"], mesh.shape["mp"]) == (2, 16) else on_device
    return jax.shard_map(
        body,
        mesh=mesh,
        in_specs=(
            P("mp", "dp", None),
            P("mp", "dp", None),
            P(None, None, "mp"),
            P(None, "mp"),
            P(None, "mp", None),
            P(),
            P(None, None, "mp"),
            P(None, None, "mp"),
            P(None, "mp"),
            P(None, "mp"),
            P(None, "mp", None),
            P(None, "mp", None),
            P(),
            P(),
        ),
        out_specs=(
            P("mp", "dp", None),
            P("mp", "dp", None),
            P(),
            P(None, None, "mp"),
            P(None, None, "mp"),
            P(None, None, "mp"),
            P(None, None, "mp"),
            P(None, "mp", None),
            P(None, "mp", None),
            P(None, "mp", None),
            P(None, "mp", None),
            P(None, "mp"),
            P(None, "mp"),
            P(None, "mp"),
            P(),
            P(),
            P(),
        ),
        check_vma=False,
    )
```

```python
import functools
import math

import jax
import jax.numpy as jnp
import ml_dtypes
import numpy as np
from jax import lax
from jax.experimental import pallas as pl
from jax.experimental.pallas import tpu as pltpu
from jax.sharding import PartitionSpec as P

D = 768
FF = 3072
L = 4096
LAYERS = 2
STEP = 5


CLIP = 1.0
BETA_ONE = 0.5
BETA_TWO = 0.5
EPS_ADAM = 1e-08
EPS_NORM = 1e-05
DECAY = 0.01
MESH = pl.DeviceIdType.MESH
F32 = jnp.float32
BF16 = jnp.bfloat16


class Plan:
    def __init__(self, parts):
        self.parts = parts
        self.rows = L // parts
        self.inner = self.rows // parts
        self.pairs = D // 2 // parts
        self.feats = -(-2 * self.pairs // 16) * 16
        rows, inner = self.rows, self.inner
        lane = np.arange(rows)
        self.place = parts * (lane % inner) + lane // inner
        packed = np.zeros((parts, self.feats, D))
        rebuild = np.zeros((parts, self.feats, D))
        n = np.arange(D)
        for at in range(parts):
            for i in range(self.pairs):
                m = self.pairs * at + i
                a, b = i, self.pairs + i
                packed[at, a] = np.cos(2 * np.pi * (m * n % D) / D)
                rebuild[at, a, m] = 1.0
                if m == 0:
                    packed[at, b] = np.cos(2 * np.pi * (D // 2 * n % D) / D)
                    rebuild[at, b, D // 2] = 1.0
                else:
                    packed[at, b] = np.sin(2 * np.pi * (m * n % D) / D)
                    rebuild[at, a, D - m] = 1.0
                    rebuild[at, b, m] = -1.0
                    rebuild[at, b, D - m] = 1.0
        bf = ml_dtypes.bfloat16
        self.packed = packed.reshape(-1, D).astype(bf)
        self.rebuild = rebuild.reshape(-1, D).astype(bf)
        turn = 2 * np.pi * (np.arange(parts)[:, None] * self.place[None, :] % L) / L
        self.turn = np.stack([np.cos(turn), np.sin(turn)]).astype(np.float32)
        angle = 2 * np.pi * (self.place[:, None] * np.arange(rows)[None, :] % rows) / rows
        self.wave = np.concatenate([np.cos(angle), np.sin(angle)]).astype(bf)


def half_dft(values):
    n = len(values)
    if n == 1:
        return [(values[0], None)]
    if n == 2:
        return [(values[0] + values[1], None), (values[0] - values[1], None)]
    even, odd = half_dft(values[0::2]), half_dft(values[1::2])
    half = n // 2
    result = [None] * (half + 1)
    for k in range(half // 2 + 1):
        er, ei = even[k]
        orr, oi = odd[k]
        if k == 0:
            result[0] = (er + orr, None)
            result[half] = (er - orr, None)
        elif 2 * k == half:
            result[k] = (er, -orr)
        else:
            c, s = math.cos(2 * math.pi * k / n), math.sin(2 * math.pi * k / n)
            tr, ti = orr * c + oi * s, oi * c - orr * s
            result[k] = (er + tr, ei + ti)
            result[half - k] = (er - tr, ti - ei)
    return result


def position_dft(plan, me, recv, work, send, turn_ref, wave_ref):
    parts, feats, rows, inner, pairs = plan.parts, plan.feats, plan.rows, plan.inner, plan.pairs
    chunk = 16
    lanes = min(rows, 128)
    for lane_at in range(0, rows, lanes):

        def body(i, carry):
            at = pl.multiple_of(i * chunk, chunk)
            values = [recv[p, pl.ds(at, chunk), lane_at : lane_at + lanes].astype(F32) for p in range(parts)]
            outs = half_dft(values)
            row = at + lax.broadcasted_iota(jnp.int32, (chunk, lanes), 0)
            is_sine = (row >= pairs) & jnp.logical_not((row == pairs) & (me == 0))
            for d in range(parts):
                re, im = outs[min(d, parts - d)]
                im = jnp.zeros_like(re) if im is None else im
                if d > parts - d:
                    im = -im
                re, im = jnp.where(is_sine, -im, re), jnp.where(is_sine, re, im)
                c = turn_ref[0, d : d + 1, lane_at : lane_at + lanes]
                s = turn_ref[1, d : d + 1, lane_at : lane_at + lanes]
                work[d, pl.ds(at, chunk), lane_at : lane_at + lanes] = (re * c + im * s).astype(BF16)
                work[d, pl.ds(at, chunk), rows + lane_at : rows + lane_at + lanes] = (im * c - re * s).astype(BF16)
            return carry

        lax.fori_loop(0, feats // chunk, body, 0)

    def swap(i, carry):
        at = pl.multiple_of(i * chunk, chunk)
        spectrum = jnp.dot(
            work[:, pl.ds(at, chunk), :].reshape(parts * chunk, 2 * rows), wave_ref[...], preferred_element_type=F32
        )
        outs = [spectrum[d * chunk : (d + 1) * chunk] for d in range(parts)]
        group = lax.broadcasted_iota(jnp.int32, (chunk, rows), 1) // inner
        bit = 1
        while bit < parts:
            upper = (group // bit) % 2 == 1
            for d in range(parts):
                if d & bit:
                    continue
                low, high = outs[d], outs[d | bit]
                shift = inner * bit
                outs[d] = jnp.where(upper, pltpu.roll(high, shift, 1), low)
                outs[d | bit] = jnp.where(upper, high, pltpu.roll(low, rows - shift, 1))
            bit *= 2
        for q in range(parts):
            send[q, pl.ds(at, chunk), :] = outs[q].astype(BF16)
        return carry

    lax.fori_loop(0, feats // chunk, swap, 0)


def exchange(plan, me, send, recv, send_sem, recv_sem):
    parts = plan.parts

    def copy_to(k):
        q = lax.rem(me + k, parts)
        return pltpu.make_async_remote_copy(
            src_ref=send.at[q],
            dst_ref=recv.at[me],
            send_sem=send_sem.at[q],
            recv_sem=recv_sem.at[me],
            device_id={"mp": q},
            device_id_type=MESH,
        )

    def copy_from(k):
        p = lax.rem(me + k, parts)
        return pltpu.make_async_remote_copy(
            src_ref=send.at[p],
            dst_ref=recv.at[p],
            send_sem=send_sem.at[p],
            recv_sem=recv_sem.at[p],
            device_id={"mp": p},
            device_id_type=MESH,
        )

    def start(k, carry):
        copy_to(k).start()
        return carry

    def finish(k, carry):
        copy_from(k).wait_recv()
        return carry

    def drain(k, carry):
        copy_to(k).wait_send()
        return carry

    lax.fori_loop(1, parts, start, 0)
    recv[me] = send[me]
    lax.fori_loop(1, parts, finish, 0)
    lax.fori_loop(1, parts, drain, 0)


def mix_kernel(plan, x_ref, packed_ref, rebuild_ref, turn_ref, wave_ref, out_ref, send, recv, work, send_back, recv_back, sems):
    me = lax.axis_index("mp")
    parts, feats, rows = plan.parts, plan.feats, plan.rows
    barrier = pltpu.get_barrier_semaphore()

    def greet(k, carry):
        pl.semaphore_signal(barrier, inc=1, device_id={"mp": lax.rem(me + k, parts)}, device_id_type=MESH)
        return carry

    lax.fori_loop(1, parts, greet, 0)
    pl.semaphore_wait(barrier, parts - 1)

    columns = lax.dot_general(packed_ref[...], x_ref[...], (((1,), (1,)), ((), ())), preferred_element_type=F32)
    send[...] = columns.astype(BF16).reshape(parts, feats, rows)
    exchange(plan, me, send, recv, sems.at[0], sems.at[1])
    position_dft(plan, me, recv, work, send_back, turn_ref, wave_ref)
    exchange(plan, me, send_back, recv_back, sems.at[2], sems.at[3])
    mixed = lax.dot_general(
        recv_back[...].reshape(parts * feats, rows), rebuild_ref[...], (((0,), (0,)), ((), ())), preferred_element_type=F32
    )
    out_ref[...] = mixed * (1.0 / math.sqrt(L * D))


def mix(plan, value):
    block = (plan.parts, plan.feats, plan.rows)
    return pl.pallas_call(
        functools.partial(mix_kernel, plan),
        out_shape=jax.ShapeDtypeStruct((plan.rows, D), F32),
        in_specs=[pl.BlockSpec(memory_space=pltpu.VMEM)] * 5,
        out_specs=pl.BlockSpec(memory_space=pltpu.VMEM),
        scratch_shapes=[
            pltpu.VMEM(block, BF16),
            pltpu.VMEM(block, BF16),
            pltpu.VMEM((plan.parts, plan.feats, 2 * plan.rows), BF16),
            pltpu.VMEM(block, BF16),
            pltpu.VMEM(block, BF16),
            pltpu.SemaphoreType.DMA((4, plan.parts)),
        ],
        compiler_params=pltpu.CompilerParams(
            collective_id=0, has_side_effects=True, vmem_limit_bytes=40 * 2**20
        ),
    )(value, plan.packed, plan.rebuild, plan.turn, plan.wave)


class Spot:
    def __init__(self):
        self.y = lax.axis_index("dp")
        self.me = lax.axis_index("mp")
        self.z, self.x, self.core = self.me // 4, (self.me // 2) % 2, self.me % 2
        self.own = self.me // 2
        self.inner = (self.z == 1) | (self.z == 2)

    def at(self, y=None, z=None, x=None, core=None):
        y = self.y if y is None else y
        z = self.z if z is None else z
        x = self.x if x is None else x
        core = self.core if core is None else core
        return {"dp": y, "mp": z * 4 + x * 2 + core}

    def y_mate(self):
        return self.at(y=1 - self.y)

    def x_mate(self):
        return self.at(x=1 - self.x)

    def core_mate(self):
        return self.at(core=1 - self.core)

    def z_mate(self, k):
        return self.at(z=self.z ^ k)


class Lines:
    def __init__(self, send_sems, recv_sems):
        self.send_sems, self.recv_sems = send_sems, recv_sems
        self.next = 0
        self.sent = []

    def copy(self, sender, number, src, dst, device):
        return pltpu.make_async_remote_copy(
            src_ref=src,
            dst_ref=dst,
            send_sem=self.send_sems.at[sender],
            recv_sem=self.recv_sems.at[number],
            device_id=device,
            device_id_type=MESH,
        )

    def send(self, number, src, dst, device, sender=None, like=None, when=None, keep=True):
        if sender is None:
            sender = self.next
            self.next += 1
        self.copy(sender, number, src, dst, device).start()
        if keep:
            self.sent.append((sender, src if like is None else like, when))
        return sender

    def wait(self, number, land, device):
        self.copy(0, number, land, land, device).wait_recv()

    def wait_sent(self, sender, src, device):
        self.copy(sender, 0, src, src, device).wait_send()

    def drain(self, device):
        for sender, src, when in self.sent:
            if when is None:
                self.wait_sent(sender, src, device)
            else:
                pl.when(when)(functools.partial(self.wait_sent, sender, src, device))
        self.sent = []


class Gather:
    def __init__(self, spot, lines, base, win, wout, split):
        self.split = split
        self.spot, self.lines, self.base = spot, lines, base
        self.win, self.wout = win, wout
        self.like = win.at[0, 0, 0]
        self.senders = {}

    def along_z(self, block, hop, number):
        s, n, b = self.spot, self.lines, self.base
        zk = s.z ^ block
        for i, part in ((0, self.win), (1, self.wout)):
            ref = part.at[zk, s.x, s.y]
            when = None if block == 0 and hop == 1 else s.inner
            n.send(b + 2 * number - 2 + i, ref, ref, s.z_mate(hop), like=self.like, when=when)

    def start_z(self):
        self.along_z(0, 1, 1)
        pl.when(self.spot.inner)(lambda: self.along_z(0, 3, 3))

    def start_x(self):
        s, n, b = self.spot, self.lines, self.base
        own = self.wout.at[s.z, s.x, s.y]
        n.send(b + 9, own, own, s.x_mate())
        own = self.win.at[s.z, s.x]
        n.send(b + 13, own, own, s.x_mate())

    def arrive(self, k):
        s, n, b = self.spot, self.lines, self.base
        zk = s.z ^ k
        a, c = self.win.at[zk, s.x, s.y], self.wout.at[zk, s.x, s.y]
        n.wait(b + 2 * k - 2, a, s.z_mate(k))
        n.wait(b + 2 * k - 1, c, s.z_mate(k))
        hop, number = {1: (3, 2), 3: (1, 2), 2: (1, 3)}[k]
        return lambda: self.along_z(k, hop, number)

    def second(self, k):
        s, n, b = self.spot, self.lines, self.base
        zk = s.z ^ k
        a, c = self.win.at[zk, s.x, s.y], self.wout.at[zk, s.x, s.y]
        steps = []
        if k in self.split:
            steps.append((b + 13 + k, a, s.x_mate()))
        if k != 1:
            steps.append((b + 5 + k, a, s.y_mate()))
        steps.append((b + 9 + k, c, s.x_mate()))
        if k != 1:
            steps.append((b + 17 + 2 * k, c, s.y_mate()))
        for i, (number, ref, device) in enumerate(steps):
            known = self.senders.get((k, i))
            used = n.send(number, ref, ref, device, sender=known, like=self.like, keep=known is None)
            self.senders[(k, i)] = used

    def early(self):
        onward = self.arrive(1)
        pl.when(self.spot.inner)(onward)
        self.second(1)

        def near():
            self.arrive(3)()
            self.second(3)

        pl.when(self.spot.inner)(near)

    def late(self):
        onward = self.arrive(2)
        pl.when(self.spot.inner)(onward)
        self.second(2)

    def rest(self):
        s, n, b = self.spot, self.lines, self.base
        for i, part in ((0, self.win), (1, self.wout)):
            own = part.at[s.z, s.x, 1 - s.y]
            n.send(b + 29 + i, own, own, s.z_mate(1))

    def last(self):
        def far():
            self.arrive(3)
            self.second(3)

        pl.when(jnp.logical_not(self.spot.inner))(far)

    def third(self, k):
        s, n, b = self.spot, self.lines, self.base
        zk = s.z ^ k
        if k > 1:
            n.wait(b + 5 + k, self.win.at[zk, s.x, 1 - s.y], s.y_mate())
        if k in self.split:
            far = self.win.at[zk, 1 - s.x, s.y]
            n.wait(b + 13 + k, far, s.x_mate())
            n.send(b + 25 + k, far, far, s.y_mate())
        elif k:
            n.send(b + 13 + k, self.win.at[zk, s.x], self.win.at[zk, s.x], s.x_mate())
        far = self.wout.at[zk, 1 - s.x, s.y]
        n.wait(b + 9 + k, far, s.x_mate())
        n.send(b + 18 + 2 * k, far, far, s.y_mate())

    def finish_in(self, k):
        s, n, b = self.spot, self.lines, self.base
        zk = s.z ^ k
        if k in self.split:
            n.wait(b + 25 + k, self.win.at[zk, 1 - s.x, 1 - s.y], s.y_mate())
        else:
            n.wait(b + 13 + k, self.win.at[zk, 1 - s.x], s.x_mate())
        if k == 1:
            n.wait(b + 29, self.win.at[zk, s.x, 1 - s.y], s.z_mate(1))

    def finish_out(self):
        s, n, b = self.spot, self.lines, self.base
        for k in range(4):
            zk = s.z ^ k
            if k == 1:
                n.wait(b + 30, self.wout.at[zk, s.x, 1 - s.y], s.z_mate(1))
            elif k:
                n.wait(b + 17 + 2 * k, self.wout.at[zk, s.x, 1 - s.y], s.y_mate())
            n.wait(b + 18 + 2 * k, self.wout.at[zk, 1 - s.x, 1 - s.y], s.y_mate())


GATHER_LINES = 31


class Reduce:
    def __init__(self, spot, lines, base, parts, yins, zin, result):
        self.spot, self.lines, self.base = spot, lines, base
        self.parts, self.yins, self.zin, self.result = parts, yins, zin, result
        self.blocks = (jnp.where(spot.inner, 2, 3), jnp.where(spot.inner, 3, 2), 1, 0)
        self.like = parts[0].at[0, 0]

    def first(self, ready):
        s, n, b = self.spot, self.lines, self.base
        order = ((0, 0), (0, 1)) if ready == 0 else ((1, 0), (1, 1), (0, 2), (1, 2), (0, 3), (1, 3))
        for i, step in order:
            k = self.blocks[step]
            n.send(b + 2 * k + i, self.parts[i].at[s.z ^ k, 1 - s.y], self.yins[i].at[k], s.y_mate())

    def add(self, ref, more):
        ref[...] = (ref[...].astype(F32) + more[...].astype(F32)).astype(BF16)

    def take(self, slot, i):
        self.lines.wait(self.base + 8 + 2 * slot + i, self.zin.at[slot, i], self.spot.z_mate(1))
        return self.zin.at[slot, i]

    def second(self, first, last):
        for at in range(first, last):
            step, i = at // 2, at % 2
            self.step(step, i)

    def step(self, step, i):
        s, n, b = self.spot, self.lines, self.base
        k = self.blocks[step]
        ref, more = self.parts[i].at[s.z ^ k, s.y], self.yins[i].at[k]
        n.wait(b + 2 * k + i, more, s.y_mate())
        self.add(ref, more)
        if step == 3:
            return
        sender = n.next
        n.next += 1
        n.sent.append((sender, self.like, None))

        def onward(slot, device):
            number = b + 8 + 2 * slot + i
            n.send(number, ref, self.zin.at[slot, i], device, sender=sender, like=self.like, keep=False)

        def at_end():
            onward(step, s.z_mate(1))

        def inside():
            come, slot, hop = ((0, 4, 3), (1, 3, 3), (4, 5, 1))[step]
            self.add(ref, self.take(come, i))
            onward(slot, s.z_mate(hop))

        pl.when(s.inner)(inside)
        pl.when(jnp.logical_not(s.inner))(at_end)

    def third(self):
        s, n, b = self.spot, self.lines, self.base
        for i in (0, 1):

            def total(slots):
                value = self.parts[i][s.z, s.y].astype(F32)
                for slot in slots:
                    value = value + self.take(slot, i)[...].astype(F32)
                self.result[i, s.y] = value.astype(BF16)

            pl.when(s.inner)(lambda: total((2, 3)))
            pl.when(jnp.logical_not(s.inner))(lambda: total((5,)))

    def fourth(self):
        s, n, b = self.spot, self.lines, self.base
        for i in (0, 1):
            n.send(b + 20 + i, self.result.at[i, s.y], self.result.at[i, s.y], s.y_mate())

    def finish(self):
        s, n, b = self.spot, self.lines, self.base
        for i in (0, 1):
            n.wait(b + 20 + i, self.result.at[i, 1 - s.y], s.y_mate())


REDUCE_LINES = 22
MATE_LINES = 8
SEND_LINES = 200


def normalize(value):
    centre = value - jnp.mean(value, axis=-1, keepdims=True)
    scale = lax.rsqrt(jnp.mean(centre * centre, axis=-1, keepdims=True) + EPS_NORM)
    return centre * scale, scale


def normalize_back(grad, gain, unit, scale):
    gain_grad = jnp.sum(grad * unit, axis=0, keepdims=True)
    shift_grad = jnp.sum(grad, axis=0, keepdims=True)
    inner = grad * gain
    mean = jnp.mean(inner, axis=-1, keepdims=True)
    along = jnp.mean(inner * unit, axis=-1, keepdims=True)
    return scale * (inner - mean - unit * along), gain_grad, shift_grad


def dot(left, right):
    return jnp.dot(left, right, preferred_element_type=F32)


def dot_t(left, right):
    return lax.dot_general(left, right, (((1,), (1,)), ((), ())), preferred_element_type=F32)


def t_dot(left, right):
    return lax.dot_general(left, right, (((0,), (0,)), ((), ())), preferred_element_type=F32)


def pick(rows, columns, where):
    at = [lax.broadcasted_iota(jnp.int32, (rows, columns), axis) for axis in (0, 1)]
    return where(*at).astype(F32).astype(BF16)


def gelu_pair(v):
    root = math.sqrt(2.0 / math.pi)
    square = v * v
    tanh = jnp.tanh(root * v * (1.0 + 0.044715 * square))
    half = 0.5 + 0.5 * tanh
    slope = half + 0.5 * v * (1.0 - tanh * tanh) * (root * (1.0 + 3 * 0.044715 * square))
    return v * half, slope


def fused_kernel(
    plan,
    tokens, cotangent_far, win_far, wout_far, bias, vec, packed_far, rebuild_far, turn, wave_far,
    act_far, grad_far, weights_far, piece_out, vec_out, norm_out,
    act_out, grad_out,
    cotangent, win_own, wout_own, packed, rebuild, wave, local_sems,
    win, wout, bias_own, bias_all, hidden, acts, slopes, unit_mix, unit_out, scale_mix, scale_out, start, keep,
    branch_send, branch_recv, grad_branch, grad_pre, far_acts, far_slopes, far_pre,
    din, dout, yin, yout, zin, result,
    send, recv, work, send_back, recv_back,
    tiles, tiles_in, piece, pieces, square_send, square_recv,
    mix_sems, all_sems, send_sems, recv_sems,
):
    spot = Spot()
    lines = Lines(send_sems, recv_sems)
    parts, feats, rows = plan.parts, plan.feats, plan.rows
    me = spot.me
    hid = FF // parts
    group = 2 * hid
    barrier = pltpu.get_barrier_semaphore()

    devices = 2 * parts
    here = spot.y * parts + me

    def other(k):
        q = lax.rem(here + k, devices)
        return q, {"dp": q // parts, "mp": lax.rem(q, parts)}

    def everyone(action):
        def body(k, carry):
            action(k)
            return carry

        lax.fori_loop(1, devices, body, 0)

    everyone(lambda k: pl.semaphore_signal(barrier, inc=1, device_id=other(k)[1], device_id_type=MESH))

    loads = [
        pltpu.make_async_copy(src, dst, local_sems.at[i])
        for i, (src, dst) in enumerate(
            (
                (win_far.at[0], win_own.at[0]),
                (wout_far.at[0], wout_own.at[0]),
                (packed_far, packed),
                (wave_far, wave),
                (rebuild_far, rebuild),
                (win_far.at[1], win_own.at[1]),
                (wout_far.at[1], wout_own.at[1]),
                (cotangent_far, cotangent),
            )
        )
    ]
    for load in loads:
        load.start()

    base = 0
    gathers, reduces = [], []
    for l in range(LAYERS):
        gathers.append(Gather(spot, lines, base, win.at[l], wout.at[l], (1, 3) if l == 0 else (1, 2, 3)))
        base += GATHER_LINES
    for l in range(LAYERS):
        reduces.append(
            Reduce(
                spot, lines, base, (din.at[l], dout.at[l]), (yin.at[l], yout.at[l]), zin.at[l], result.at[l]
            )
        )
        base += REDUCE_LINES
    mates = []
    for l in range(LAYERS):
        mates.append(base)
        base += MATE_LINES
    bias_base = base

    def copy_to(k, src, dst, lane):
        q = lax.rem(me + k, parts)
        return pltpu.make_async_remote_copy(
            src_ref=src.at[q],
            dst_ref=dst.at[me],
            send_sem=mix_sems.at[lane, q],
            recv_sem=mix_sems.at[lane + 1, me],
            device_id={"mp": q},
            device_id_type=MESH,
        )

    def copy_from(k, src, dst, lane):
        p = lax.rem(me + k, parts)
        return pltpu.make_async_remote_copy(
            src_ref=src.at[p],
            dst_ref=dst.at[p],
            send_sem=mix_sems.at[lane, p],
            recv_sem=mix_sems.at[lane + 1, p],
            device_id={"mp": p},
            device_id_type=MESH,
        )

    def each(action):
        def body(k, carry):
            action(k)
            return carry

        lax.fori_loop(1, parts, body, 0)

    def mix_enter(value):
        send[...] = dot_t(packed[...], value).astype(BF16).reshape(parts, feats, rows)

    def mix_go():
        each(lambda k: copy_to(k, send, recv, 0).start())
        recv[me] = send[me]

    def mix_middle():
        each(lambda k: copy_from(k, send, recv, 0).wait_recv())
        position_dft(plan, me, recv, work, send_back, turn, wave)
        each(lambda k: copy_to(k, send_back, recv_back, 2).start())
        recv_back[me] = send_back[me]

    def mix_leave():
        each(lambda k: copy_from(k, send_back, recv_back, 2).wait_recv())
        mixed = t_dot(recv_back[...].reshape(parts * feats, rows), rebuild[...])
        each(lambda k: copy_to(k, send, recv, 0).wait_send())
        each(lambda k: copy_to(k, send_back, recv_back, 2).wait_send())
        return mixed * (1.0 / math.sqrt(L * D))

    eye = pick(hid, 256, lambda i, j: i == j)

    def bias_column(l, zk, x):
        return dot_t(eye, bias_all[zk, x])[:, l : l + 1]

    def own_weights(l):
        win[l, spot.z, spot.x] = win_own[l].astype(BF16).reshape(2, hid // 2, D)
        wout[l, spot.z, spot.x] = wout_own[l].astype(BF16).reshape(2, hid // 2, D)

    def swap_branch(number, slot):
        ref, land = branch_send.at[slot], branch_recv.at[slot]
        return lines.send(number, ref, land, spot.core_mate(), keep=False)

    def hidden_away(l):
        lines.send(mates[l] + 4, hidden.at[l, 0], hidden.at[l, 2], spot.x_mate())

    def forward(l, current, mixed, per_group):
        unit, scale = normalize(current + mixed)
        unit_mix[l] = unit
        scale_mix[l] = scale
        normed = unit * vec[0, l : l + 1] + vec[1, l : l + 1]
        keep[...] = normed
        hidden[l, 0] = normed.astype(BF16)
        lines.send(mates[l], hidden.at[l, 0], hidden.at[l, 1], spot.core_mate())
        for k in range(4):
            per_group(k)
            zk = spot.z ^ k
            weights = win[l, zk].reshape(group, D)
            column = jnp.concatenate([bias_column(l, zk, x) for x in (0, 1)], axis=0)
            for slot in (0, 1):
                if k == 0 and slot == 1:
                    lines.wait(mates[l], hidden.at[l, 1], spot.core_mate())
                value, slope = gelu_pair(dot_t(weights, hidden[l, slot]) + column)
                span = slice(slot * rows, (slot + 1) * rows)
                acts[l, zk, :, :, span] = value.astype(BF16).reshape(2, hid, rows)
                slopes[l, zk, :, :, span] = slope.astype(BF16).reshape(2, hid, rows)
        if l == LAYERS - 1:
            hidden_away(l)
        gathers[l].finish_out()
        outs = wout[l].reshape(FF // 2, D)
        branch_send[0] = t_dot(acts[l, :, :, :, rows : 2 * rows].reshape(FF // 2, rows), outs).astype(BF16)
        sender = swap_branch(mates[l] + 1, 0)
        branch = t_dot(acts[l, :, :, :, 0:rows].reshape(FF // 2, rows), outs)
        lines.wait(mates[l] + 1, branch_recv.at[0], spot.core_mate())
        total = keep[...] + branch + branch_recv[0].astype(F32) + vec[2, l : l + 1]
        unit, scale = normalize(total)
        unit_out[l] = unit
        scale_out[l] = scale
        lines.wait_sent(sender, branch_send.at[0], spot.core_mate())
        return unit * vec[3, l : l + 1] + vec[4, l : l + 1]

    def vec_put(l, i, value):
        for t in range(3):
            for j in (0, 1):
                at = 256 * t + 128 * j
                tiles[3 * (5 * l + i) + t, j : j + 1, :] = value[:, at : at + 128]

    def bias_put(l):
        ones = jnp.ones((16, 2 * rows), BF16)
        for zk in range(4):
            for x in (0, 1):
                row = dot_t(ones, grad_pre[zk, x])[0:1]
                for y in (0, 1):
                    to = y * parts + zk * 4 + x * 2 + spot.core
                    tiles[to, 2 + 2 * l : 3 + 2 * l, :] = row[:, 0:128]
                    tiles[to, 3 + 2 * l : 4 + 2 * l, 0 : hid - 128] = row[:, 128:hid]

    def from_x_mate(l, parts_of):
        for i, part in parts_of:
            lines.wait(mates[l] + i, part.at[l, 2], spot.x_mate())
            lines.send(mates[l] + i + 1, part.at[l, 2], part.at[l, 3], spot.core_mate())

    half = FF // 4

    def far_hidden(l):
        ins = win[l, :, spot.x].reshape(half, D)
        column = jnp.concatenate([bias_column(l, zk, spot.x) for zk in range(4)], axis=0)
        for slot in (2, 3):
            if slot == 3:
                lines.wait(mates[l] + 5, hidden.at[l, 3], spot.core_mate())
            span = slice((slot - 2) * rows, (slot - 1) * rows)
            value, slope = gelu_pair(dot_t(ins, hidden[l, slot]) + column)
            far_acts[:, span] = value.astype(BF16)
            far_slopes[:, span] = slope.astype(BF16)

    def far_grads(l):
        outs = wout[l, :, spot.x].reshape(half, D)
        for slot in (2, 3):
            if slot == 3:
                lines.wait(mates[l] + 7, grad_branch.at[l, 3], spot.core_mate())
            span = slice((slot - 2) * rows, (slot - 1) * rows)
            grad_act = dot_t(outs, grad_branch[l, slot])
            far_pre[:, span] = (grad_act * far_slopes[:, span].astype(F32)).astype(BF16)

    def weight_grads(l):
        for i, (near, far, part, out) in enumerate(
            (
                (grad_pre[:, spot.x], far_pre, hidden, din),
                (acts[l, :, spot.x], far_acts, grad_branch, dout),
            )
        ):
            total = dot(near.reshape(half, 2 * rows), part[l, 0:2].reshape(2 * rows, D))
            total = total + dot(far[...], part[l, 2:4].reshape(2 * rows, D))
            out[l] = total.astype(BF16).reshape(4, 2, hid // 2, D)
            reduces[l].first(i)

    def backward(l, grad, middle, later):
        grad_total, gain_grad, shift_grad = normalize_back(grad, vec[3, l : l + 1], unit_out[l], scale_out[l])
        low = grad_total.astype(BF16)
        grad_branch[l, 0] = low
        lines.send(mates[l] + 2, grad_branch.at[l, 0], grad_branch.at[l, 1], spot.core_mate())
        lines.send(mates[l] + 6, grad_branch.at[l, 0], grad_branch.at[l, 2], spot.x_mate())
        keep[...] = grad_total
        vec_put(l, 2, jnp.sum(low.astype(F32), axis=0, keepdims=True))
        vec_put(l, 3, gain_grad)
        vec_put(l, 4, shift_grad)
        for slot in (0, 1):
            if slot == 1:
                lines.wait(mates[l] + 2, grad_branch.at[l, 1], spot.core_mate())
            span = slice(slot * rows, (slot + 1) * rows)
            for zk in range(4):
                grad_act = dot_t(wout[l, zk].reshape(group, D), grad_branch[l, slot]).reshape(2, hid, rows)
                grad_pre[zk, :, :, span] = (grad_act * slopes[l, zk, :, :, span].astype(F32)).astype(BF16)
        middle()
        ins = win[l].reshape(FF // 2, D)
        branch_send[1] = t_dot(grad_pre[:, :, :, rows : 2 * rows].reshape(FF // 2, rows), ins).astype(BF16)
        sender = swap_branch(mates[l] + 3, 1)
        grad_normed = t_dot(grad_pre[:, :, :, 0:rows].reshape(FF // 2, rows), ins)
        bias_put(l)
        later()
        lines.wait(mates[l] + 3, branch_recv.at[1], spot.core_mate())
        grad_normed = keep[...] + grad_normed + branch_recv[1].astype(F32)
        lines.wait_sent(sender, branch_send.at[1], spot.core_mate())
        grad_summed, gain_grad, shift_grad = normalize_back(grad_normed, vec[0, l : l + 1], unit_mix[l], scale_mix[l])
        vec_put(l, 0, gain_grad)
        vec_put(l, 1, shift_grad)
        return grad_summed

    inner = plan.inner

    def to_local(i, j):
        return j == parts * (i % inner) + i // inner

    for load in loads[:2]:
        load.wait()
    own_weights(0)
    bias_own[...] = jnp.zeros_like(bias_own)
    bias_own[0:LAYERS, 0:hid] = bias[...]
    bias_all[spot.z, spot.x] = bias_own[...].astype(BF16)
    tiles[...] = jnp.zeros_like(tiles)
    pl.semaphore_wait(barrier, devices - 1)
    gathers[0].start_z()
    local = dot(pick(rows, rows, to_local), tokens[...])
    start[...] = local
    for load in loads[2:4]:
        load.wait()
    mix_enter(local.astype(BF16))
    mix_go()
    gathers[0].start_x()
    for j in range(1, 8):
        far = spot.own ^ j
        own = bias_all.at[spot.z, spot.x]
        lines.send(bias_base + j, own, own, {"dp": spot.y, "mp": far * 2 + spot.core})
    for load in loads[4:]:
        load.wait()
    own_weights(1)
    gathers[0].early()
    gathers[0].third(0)
    gathers[0].late()
    gathers[0].third(1)
    mix_middle()
    gathers[0].last()
    gathers[0].rest()
    gathers[1].start_z()
    gathers[0].third(2)
    gathers[0].third(3)
    gathers[1].start_x()
    for j in range(1, 8):
        far = spot.own ^ j
        lines.wait(bias_base + j, bias_all.at[far // 2, far % 2], {"dp": spot.y, "mp": far * 2 + spot.core})
    mixed = mix_leave()

    def between(k):
        if k == 2:
            gathers[1].early()
        gathers[0].finish_in(k)

    current = forward(0, start[...], mixed, between)
    start[...] = current
    mix_enter(current.astype(BF16))
    mix_go()
    gathers[1].third(0)
    gathers[1].late()
    gathers[1].rest()
    gathers[1].third(1)
    gathers[1].last()
    gathers[1].third(2)
    mix_middle()
    gathers[1].third(3)
    mixed = mix_leave()
    current = forward(1, start[...], mixed, gathers[1].finish_in)
    act_out[...] = t_dot(pick(rows, rows, to_local), current.astype(BF16)).astype(BF16)
    stores = [
        pltpu.make_async_copy(src, dst, local_sems.at[8 + i])
        for i, (src, dst) in enumerate(
            ((act_out, act_far), (grad_out, grad_far), (result.at[1], weights_far.at[1]), (result.at[0], weights_far.at[0]))
        )
    ]
    stores[0].start()

    by_hidden, by_grad = ((4, hidden),), ((6, grad_branch),)
    grad = backward(1, dot(pick(rows, rows, to_local), cotangent[...]), lambda: None, lambda: None)
    start[...] = grad
    mix_enter(grad.astype(BF16))
    mix_go()
    from_x_mate(1, by_hidden + by_grad)
    far_hidden(1)
    far_grads(1)
    mix_middle()
    hidden_away(0)
    weight_grads(1)
    mixed = mix_leave()

    def middle():
        from_x_mate(0, by_hidden)
        far_hidden(0)

    grad = backward(0, start[...] + mixed, middle, lambda: reduces[1].second(0, 4))

    def tile_to(k):
        q, device = other(k)
        return pltpu.make_async_remote_copy(
            src_ref=tiles.at[q], dst_ref=tiles_in.at[here], send_sem=all_sems.at[0, q], recv_sem=all_sems.at[1, here],
            device_id=device, device_id_type=MESH,
        )

    def tile_from(k):
        p, device = other(k)
        return pltpu.make_async_remote_copy(
            src_ref=tiles.at[p], dst_ref=tiles_in.at[p], send_sem=all_sems.at[0, p], recv_sem=all_sems.at[1, p],
            device_id=device, device_id_type=MESH,
        )

    everyone(lambda k: tile_to(k).start())
    tiles_in[here] = tiles[here]
    start[...] = grad
    mix_enter(grad.astype(BF16))
    mix_go()
    from_x_mate(0, by_grad)
    far_grads(0)
    reduces[1].second(4, 6)
    weight_grads(0)
    reduces[1].second(6, 8)
    reduces[1].third()
    reduces[1].fourth()
    reduces[0].second(0, 6)
    mix_middle()
    reduces[0].second(6, 8)
    everyone(lambda k: tile_from(k).wait_recv())
    total = tiles_in[0]
    for d in range(1, devices):
        total = total + tiles_in[d]
    piece_out[...] = total
    piece[...] = total

    def piece_to(k):
        q, device = other(k)
        return pltpu.make_async_remote_copy(
            src_ref=piece, dst_ref=pieces.at[here], send_sem=all_sems.at[2, q], recv_sem=all_sems.at[3, here],
            device_id=device, device_id_type=MESH,
        )

    def piece_from(k):
        p, device = other(k)
        return pltpu.make_async_remote_copy(
            src_ref=piece, dst_ref=pieces.at[p], send_sem=all_sems.at[2, p], recv_sem=all_sems.at[3, p],
            device_id=device, device_id_type=MESH,
        )

    everyone(lambda k: piece_to(k).start())
    pieces[here] = total
    reduces[1].finish()
    stores[2].start()
    reduces[0].third()

    def squares(ref):
        value = ref[...].astype(F32)
        return jnp.sum(value * value, axis=(0, 1), keepdims=True)

    row = lax.broadcasted_iota(jnp.int32, total.shape, 0)
    local = 0.5 * jnp.sum(jnp.where((row >= 2) & (row < 6), total * total, 0.0), axis=(0, 1), keepdims=True)
    for l in range(LAYERS):
        for i in (0, 1):
            local = local + squares(result.at[l, i, spot.y])
    square_send[...] = jnp.broadcast_to(local, square_send.shape)

    def square_to(k):
        q, device = other(k)
        return pltpu.make_async_remote_copy(
            src_ref=square_send, dst_ref=square_recv.at[here], send_sem=all_sems.at[4, q], recv_sem=all_sems.at[5, here],
            device_id=device, device_id_type=MESH,
        )

    def square_from(k):
        p, device = other(k)
        return pltpu.make_async_remote_copy(
            src_ref=square_send, dst_ref=square_recv.at[p], send_sem=all_sems.at[4, p], recv_sem=all_sems.at[5, p],
            device_id=device, device_id_type=MESH,
        )

    everyone(lambda k: square_to(k).start())
    square_recv[here] = square_send[...]
    reduces[0].fourth()
    mixed = mix_leave()
    grad = start[...] + mixed
    back = pick(rows, rows, lambda i, j: to_local(j, i))
    high = grad.astype(BF16)
    rest = grad - high.astype(F32)
    middle = rest.astype(BF16)
    low = (rest - middle.astype(F32)).astype(BF16)
    grad = dot(back, high) + (dot(back, middle) + dot(back, low))
    for t in range(D // 128):
        grad_out[pl.ds(t, rows, stride=D // 128), :] = grad[:, 128 * t : 128 * (t + 1)]
    stores[1].start()

    everyone(lambda k: piece_from(k).wait_recv())
    for l in range(LAYERS):
        for i in range(5):
            for t in range(3):
                for j in (0, 1):
                    at = 256 * t + 128 * j
                    vec_out[i, l : l + 1, at : at + 128] = pieces[3 * (5 * l + i) + t, j : j + 1, :]
    every = jnp.sum(jnp.where(row < 2, pieces[...] * pieces[...], 0.0), axis=0)
    norms = jnp.sum(every, axis=(0, 1), keepdims=True)
    everyone(lambda k: square_from(k).wait_recv())
    norms = norms + jnp.sum(square_recv[...], axis=0)[0:1, 0:1]
    norm_out[...] = jnp.broadcast_to(jnp.sqrt(norms), norm_out.shape)
    everyone(lambda k: tile_to(k).wait_send())
    everyone(lambda k: piece_to(k).wait_send())
    everyone(lambda k: square_to(k).wait_send())
    stores[0].wait()
    stores[1].wait()
    reduces[0].finish()
    stores[3].start()
    lines.drain(spot.core_mate())
    stores[2].wait()
    stores[3].wait()


def fused(plan, tokens, cotangent, weight_in, weight_out, bias_in, vec):
    parts, feats, rows = plan.parts, plan.feats, plan.rows
    block = (parts, feats, rows)
    hid = FF // parts
    half = hid // 2
    vm = pltpu.VMEM
    near, far = pl.BlockSpec(memory_space=vm), pl.BlockSpec(memory_space=pl.ANY)
    line_count = LAYERS * (GATHER_LINES + REDUCE_LINES + MATE_LINES) + 8
    return pl.pallas_call(
        functools.partial(fused_kernel, plan),
        out_shape=(
            jax.ShapeDtypeStruct((rows, D), BF16),
            jax.ShapeDtypeStruct((rows * D // 128, 128), F32),
            jax.ShapeDtypeStruct((LAYERS, 2, 2, half, D), BF16),
            jax.ShapeDtypeStruct((8, 128), F32),
            jax.ShapeDtypeStruct((5, LAYERS, D), F32),
            jax.ShapeDtypeStruct((8, 128), F32),
        ),
        in_specs=[near, far, far, far, near, near, far, far, near, far],
        out_specs=[far] * 3 + [near] * 3,
        scratch_shapes=[
            vm((rows, D), BF16),
            vm((rows * D // 128, 128), F32),
            vm((rows, D), BF16),
            vm((LAYERS, hid, D), F32),
            vm((LAYERS, hid, D), F32),
            vm((parts * feats, D), BF16),
            vm((parts * feats, D), BF16),
            vm((2 * rows, rows), BF16),
            pltpu.SemaphoreType.DMA((12,)),
            vm((LAYERS, 4, 2, 2, half, D), BF16),
            vm((LAYERS, 4, 2, 2, half, D), BF16),
            vm((16, 256), F32),
            vm((4, 2, 16, 256), BF16),
            vm((LAYERS, 4, rows, D), BF16),
            vm((LAYERS, 4, 2, hid, 2 * rows), BF16),
            vm((LAYERS, 4, 2, hid, 2 * rows), BF16),
            vm((LAYERS, rows, D), F32),
            vm((LAYERS, rows, D), F32),
            vm((LAYERS, rows, 1), F32),
            vm((LAYERS, rows, 1), F32),
            vm((rows, D), F32),
            vm((rows, D), F32),
            vm((2, rows, D), BF16),
            vm((2, rows, D), BF16),
            vm((LAYERS, 4, rows, D), BF16),
            vm((4, 2, hid, 2 * rows), BF16),
            vm((FF // 4, 2 * rows), BF16),
            vm((FF // 4, 2 * rows), BF16),
            vm((FF // 4, 2 * rows), BF16),
            vm((LAYERS, 4, 2, half, D), BF16),
            vm((LAYERS, 4, 2, half, D), BF16),
            vm((LAYERS, 4, half, D), BF16),
            vm((LAYERS, 4, half, D), BF16),
            vm((LAYERS, 6, 2, half, D), BF16),
            vm((LAYERS, 2, 2, half, D), BF16),
            vm(block, BF16),
            vm(block, BF16),
            vm((parts, feats, 2 * rows), BF16),
            vm(block, BF16),
            vm(block, BF16),
            vm((2 * parts, 8, 128), F32),
            vm((2 * parts, 8, 128), F32),
            vm((8, 128), F32),
            vm((2 * parts, 8, 128), F32),
            vm((8, 128), F32),
            vm((2 * parts, 8, 128), F32),
            pltpu.SemaphoreType.DMA((4, parts)),
            pltpu.SemaphoreType.DMA((6, 2 * parts)),
            pltpu.SemaphoreType.DMA((SEND_LINES,)),
            pltpu.SemaphoreType.DMA((line_count,)),
        ],
        compiler_params=pltpu.CompilerParams(collective_id=1, has_side_effects=True, vmem_limit_bytes=62 * 2**20),
    )(tokens, cotangent, weight_in, weight_out, bias_in, vec, plan.packed, plan.rebuild, plan.turn, plan.wave)


def update_kernel(*refs):
    far_small, (change_far,), ins, through_far = refs[0:9], refs[9:10], refs[10:16], refs[16:18]
    outs, through_out, small_outs, norm_out = refs[18:26], refs[26:28], refs[28:34], refs[34]
    small, (change,), near_ins, near_outs = refs[35:44], refs[44:45], refs[45:51], refs[51:59]
    near_through, near_small, sems, small_sems = refs[59:61], refs[61:67], refs[67], refs[68]
    norm, bias, moment_bias, square_bias, piece, vec, moment_vec, square_vec, sum_vec = small
    hid = bias.shape[1]
    part = hid // 2
    pieces = [(l, kind, h) for l in range(LAYERS) for kind in (0, 1) for h in (0, 1)]
    last = len(pieces)

    def copies(at, out):
        l, kind, h = pieces[at]
        span = pl.ds(h * part, part)
        if out:
            pairs = zip(near_outs[4 * kind : 4 * kind + 4], outs[4 * kind : 4 * kind + 4])
        else:
            pairs = zip(ins[3 * kind : 3 * kind + 3], near_ins[3 * kind : 3 * kind + 3])
        result = [(src.at[l, span], dst.at[l, span]) for src, dst in pairs]
        if not out:
            result.append((change_far.at[l, kind, h], change.at[l, kind, h]))
        return [pltpu.make_async_copy(src, dst, sems.at[int(out), at, i]) for i, (src, dst) in enumerate(result)]

    def lists(sources, targets, row, lane):
        return [
            pltpu.make_async_copy(src, dst, small_sems.at[row, lane + i])
            for i, (src, dst) in enumerate(zip(sources, targets))
        ]

    small_in = lists(far_small, small, 0, 0)
    small_out = lists(near_small, small_outs, 1, 0)
    through_in = lists(through_far, near_through, 0, 9)
    through_to = lists(near_through, through_out, 1, 9)
    for copy in small_in:
        copy.start()
    for at in range(last):
        for copy in copies(at, False):
            copy.start()
    for copy in through_in:
        copy.start()
    for copy in small_in:
        copy.wait()
    factor = jnp.minimum(1.0, CLIP / norm[0:1, 0:1])
    norm_out[0, 0] = norm[0, 0]
    m_bias, v_bias, b_new, m_vec, v_vec, vec_new = near_small
    for l in range(LAYERS):
        row = jnp.concatenate([piece[2 + 2 * l : 3 + 2 * l, :], piece[3 + 2 * l : 4 + 2 * l, 0 : hid - 128]], axis=1)
        here = slice(l, l + 1)
        news = adamw(bias[here], row * factor, moment_bias[here], square_bias[here], 0.5, 0.0)
        for out, value in zip((m_bias, v_bias, b_new), news):
            out[here] = value
    news = adamw(vec[...], sum_vec[...] * factor, moment_vec[...], square_vec[...], 0.5, 0.0)
    for out, value in zip((m_vec, v_vec, vec_new), news):
        out[...] = value
    for copy in small_out:
        copy.start()
    for at, (l, kind, h) in enumerate(pieces):
        for copy in copies(at, False):
            copy.wait()
        span = slice(h * part, (h + 1) * part)
        weight, moment, square = [ref[l, span] for ref in near_ins[3 * kind : 3 * kind + 3]]
        width = (D, FF)[kind]
        news = adamw(
            weight, change[l, kind, h].astype(F32) * factor, moment, square, 1.0 / math.sqrt(width), DECAY
        )
        for out, value in zip(near_outs[4 * kind : 4 * kind + 4], news + (news[2].astype(BF16),)):
            out[l, span] = value
        for copy in copies(at, True):
            copy.start()
    for copy_in, copy_out in zip(through_in, through_to):
        copy_in.wait()
        copy_out.start()
    for at in range(last):
        for copy in copies(at, True):
            copy.wait()
    for copy in small_out + through_to:
        copy.wait()


def update(*args):
    far = pl.BlockSpec(memory_space=pl.ANY)
    small, change, weight, through = args[0:9], args[9], args[10], args[16:18]

    def shape(value, dtype=F32):
        return jax.ShapeDtypeStruct(value.shape, dtype)

    def near(value, dtype=F32):
        return pltpu.VMEM(value.shape, dtype)

    kinds = (F32, F32, F32, BF16) * 2
    bias, vec = small[1], small[5]
    return pl.pallas_call(
        update_kernel,
        out_shape=tuple(shape(weight, kind) for kind in kinds)
        + (shape(through[0], BF16), shape(through[1]))
        + (shape(bias),) * 3
        + (shape(vec),) * 3
        + (jax.ShapeDtypeStruct((1, 1), F32),),
        in_specs=[far] * 18,
        out_specs=[far] * 16 + [pl.BlockSpec(memory_space=pltpu.SMEM)],
        scratch_shapes=[near(value) for value in small]
        + [near(change, BF16)]
        + [near(weight)] * 6
        + [near(weight, kind) for kind in kinds]
        + [near(through[0], BF16), near(through[1])]
        + [near(bias)] * 3
        + [near(vec)] * 3
        + [pltpu.SemaphoreType.DMA((2, 8, 4)), pltpu.SemaphoreType.DMA((2, 11))],
        compiler_params=pltpu.CompilerParams(vmem_limit_bytes=62 * 2**20),
    )(*args)


def on_block(
    tokens, cotangent, weight_in, bias_in, weight_out, vectors, moment_in, square_in,
    moment_bias, square_bias, moment_out, square_out, moment_vec, square_vec,
):
    rows = tokens.shape[0]
    plan = Plan(L // rows)

    def turned(value):
        return jnp.swapaxes(value, 1, 2)

    def by_kind(value):
        return jnp.swapaxes(value, 0, 1)

    win, vec = turned(weight_in), by_kind(vectors)
    acts, grad, grads, piece, sum_vec, norm = fused(
        plan, tokens.reshape(rows, D), cotangent.reshape(rows, D), win, weight_out, bias_in, vec
    )
    (
        m_in, v_in, w_in, low_in, m_out, v_out, w_out, low_out, acts, grad,
        m_bias, v_bias, b_new, m_vec, v_vec, vec_new, norm,
    ) = update(
        norm, bias_in, moment_bias, square_bias, piece, vec, by_kind(moment_vec), by_kind(square_vec), sum_vec, grads,
        win, turned(moment_in), turned(square_in), weight_out, moment_out, square_out, acts, grad,
    )
    return (
        acts.reshape(rows, 1, D),
        grad.reshape(rows, 1, D),
        norm[0, 0],
        turned(m_in),
        turned(v_in),
        turned(w_in),
        turned(low_in),
        m_out,
        v_out,
        w_out,
        low_out,
        m_bias,
        v_bias,
        b_new,
        by_kind(m_vec),
        by_kind(v_vec),
        by_kind(vec_new),
    )


def matmul(left_op, right_op):
    return jnp.dot(left_op, right_op, preferred_element_type=jnp.float32)


def inner_rows(left_op, right_op):
    return lax.dot_general(
        left_op, right_op, (((0,), (0,)), ((), ())), preferred_element_type=jnp.float32
    )


def inner_cols(left_op, right_op):
    return lax.dot_general(
        left_op, right_op, (((1,), (1,)), ((), ())), preferred_element_type=jnp.float32
    )


def layer_norm(value, gain, shift):
    centre = value - jnp.mean(value, axis=-1, keepdims=True)
    spread = jnp.mean(centre * centre, axis=-1, keepdims=True)
    return centre * lax.rsqrt(spread + EPS_NORM) * gain + shift


def adamw(weight, grad, moment, square, rate, decay):
    new_moment = BETA_ONE * moment + (1.0 - BETA_ONE) * grad
    new_square = BETA_TWO * square + (1.0 - BETA_TWO) * grad * grad
    moment_hat = new_moment / (1.0 - BETA_ONE**STEP)
    square_hat = new_square / (1.0 - BETA_TWO**STEP)
    new_weight = weight - rate * (moment_hat / (jnp.sqrt(square_hat) + EPS_ADAM) + decay * weight)
    return (new_moment, new_square, new_weight)


def on_device(
    tokens,
    cotangent,
    weight_in,
    bias_in,
    weight_out,
    vectors,
    moment_in,
    square_in,
    moment_bias,
    square_bias,
    moment_out,
    square_out,
    moment_vec,
    square_vec,
):
    row_count, seq_count, feat_count = tokens.shape
    plan = Plan(L // row_count)

    def localize(value):
        return jnp.swapaxes(value.reshape(plan.inner, plan.parts, -1), 0, 1).reshape(value.shape)

    def restore(value):
        return jnp.swapaxes(value.reshape(plan.parts, plan.inner, -1), 0, 1).reshape(value.shape)

    current = localize(tokens).astype(jnp.float32)
    saved = []
    for layer_at in range(LAYERS):
        vector_set = vectors[layer_at]
        rounded = current.astype(jnp.bfloat16)
        mixed = mix(plan, rounded.reshape(row_count, feat_count)).reshape(row_count, seq_count, feat_count)
        summed = current + mixed
        normed = layer_norm(summed, vector_set[0], vector_set[1])
        hidden_in = normed.astype(jnp.bfloat16)
        weight_one = weight_in[layer_at].astype(jnp.bfloat16)
        weight_two = weight_out[layer_at].astype(jnp.bfloat16)
        bias_one = bias_in[layer_at].astype(jnp.bfloat16)
        whole_one, whole_two, whole_bias = (
            lax.all_gather(weight_one, "mp", axis=1, tiled=True),
            lax.all_gather(weight_two, "mp", axis=0, tiled=True),
            lax.all_gather(bias_one, "mp", axis=0, tiled=True),
        )
        inputs = hidden_in.reshape(-1, feat_count)
        pre_act = matmul(inputs, whole_one) + whole_bias.astype(jnp.float32)
        acts = jax.nn.gelu(pre_act).astype(jnp.bfloat16)
        branch = matmul(acts, whole_two).reshape(row_count, seq_count, feat_count)
        held = (inputs, whole_one, whole_two)
        total = normed + branch + vector_set[2]
        current = layer_norm(total, vector_set[3], vector_set[4])
        saved.append((summed, total, pre_act, acts, held))
    activations = restore(current.astype(jnp.bfloat16))
    grad = localize(cotangent).astype(jnp.float32)
    layer_grads = [None] * LAYERS
    for layer_at in reversed(range(LAYERS)):
        vector_set = vectors[layer_at]
        summed, total, pre_act, acts, held = saved[layer_at]
        inputs, mat_one, mat_two = held
        _, pull_out = jax.vjp(layer_norm, total, vector_set[3], vector_set[4])
        grad_total, gain_two, shift_two = pull_out(grad)
        grad_branch = grad_total.astype(jnp.bfloat16)
        grad_bias_two = jnp.sum(grad_branch.astype(jnp.float32), axis=(0, 1))
        flat_grad = grad_branch.reshape(-1, feat_count)
        grad_act = inner_cols(flat_grad, mat_two)
        _, pull_gelu = jax.vjp(jax.nn.gelu, pre_act)
        grad_pre = pull_gelu(grad_act)[0].astype(jnp.bfloat16)
        full_one = inner_rows(inputs, grad_pre)
        full_two = inner_rows(acts, flat_grad)
        full_bias = jnp.sum(grad_pre.astype(jnp.float32), axis=0)
        grad_one, grad_two, grad_bias_one = (
            lax.psum_scatter(
                full_one.astype(jnp.bfloat16), "mp", scatter_dimension=1, tiled=True
            ).astype(jnp.float32),
            lax.psum_scatter(
                full_two.astype(jnp.bfloat16), "mp", scatter_dimension=0, tiled=True
            ).astype(jnp.float32),
            lax.psum_scatter(
                full_bias.astype(jnp.bfloat16), "mp", scatter_dimension=0, tiled=True
            ).astype(jnp.float32),
        )
        grad_normed = inner_cols(grad_pre, mat_one).reshape(row_count, seq_count, feat_count)
        grad_normed = grad_normed + grad_total
        _, pull_in = jax.vjp(layer_norm, summed, vector_set[0], vector_set[1])
        grad_summed, gain_one, shift_one = pull_in(grad_normed)
        mix_grad = grad_summed.astype(jnp.bfloat16).reshape(-1, feat_count)
        grad_mix = mix(plan, mix_grad).reshape(row_count, seq_count, feat_count)
        grad = grad_summed + grad_mix
        layer_grads[layer_at] = (
            grad_one,
            grad_two,
            grad_bias_one,
            jnp.stack([gain_one, shift_one, grad_bias_two, gain_two, shift_two]),
        )
    stack_in = jnp.stack([entry[0] for entry in layer_grads])
    stack_out = jnp.stack([entry[1] for entry in layer_grads])
    stack_bias = jnp.stack([entry[2] for entry in layer_grads])
    stack_vec = jnp.stack([entry[3] for entry in layer_grads])
    sum_in, sum_out, sum_bias, sum_vec = (
        lax.psum(stack_in.astype(jnp.bfloat16), "dp").astype(jnp.float32),
        lax.psum(stack_out.astype(jnp.bfloat16), "dp").astype(jnp.float32),
        lax.psum(stack_bias.astype(jnp.bfloat16), "dp").astype(jnp.float32),
        lax.psum(stack_vec.astype(jnp.bfloat16), "dp").astype(jnp.float32),
    )
    local_squares = (
        jnp.sum(sum_in * sum_in) + jnp.sum(sum_out * sum_out) + jnp.sum(sum_bias * sum_bias)
    )
    sum_vec, total_squares = lax.psum((sum_vec, local_squares), "mp")
    grad_norm = jnp.sqrt(total_squares + jnp.sum(sum_vec * sum_vec))
    factor = jnp.minimum(1.0, CLIP / grad_norm)
    m_in, v_in, w_in = adamw(
        weight_in, sum_in * factor, moment_in, square_in, 1.0 / math.sqrt(D), DECAY
    )
    m_out, v_out, w_out = adamw(
        weight_out, sum_out * factor, moment_out, square_out, 1.0 / math.sqrt(FF), DECAY
    )
    m_bias, v_bias, b_new = adamw(bias_in, sum_bias * factor, moment_bias, square_bias, 0.5, 0.0)
    m_vec, v_vec, vec_new = adamw(vectors, sum_vec * factor, moment_vec, square_vec, 0.5, 0.0)
    return (
        activations,
        restore(grad),
        grad_norm,
        m_in,
        v_in,
        w_in,
        w_in.astype(jnp.bfloat16),
        m_out,
        v_out,
        w_out,
        w_out.astype(jnp.bfloat16),
        m_bias,
        v_bias,
        b_new,
        m_vec,
        v_vec,
        vec_new,
    )


def solution(mesh):
    body = on_block if (mesh.shape["dp"], mesh.shape["mp"]) == (2, 16) else on_device
    return jax.shard_map(
        body,
        mesh=mesh,
        in_specs=(
            P("mp", "dp", None),
            P("mp", "dp", None),
            P(None, None, "mp"),
            P(None, "mp"),
            P(None, "mp", None),
            P(),
            P(None, None, "mp"),
            P(None, None, "mp"),
            P(None, "mp"),
            P(None, "mp"),
            P(None, "mp", None),
            P(None, "mp", None),
            P(),
            P(),
        ),
        out_specs=(
            P("mp", "dp", None),
            P("mp", "dp", None),
            P(),
            P(None, None, "mp"),
            P(None, None, "mp"),
            P(None, None, "mp"),
            P(None, None, "mp"),
            P(None, "mp", None),
            P(None, "mp", None),
            P(None, "mp", None),
            P(None, "mp", None),
            P(None, "mp"),
            P(None, "mp"),
            P(None, "mp"),
            P(),
            P(),
            P(),
        ),
        check_vma=False,
    )
```
